128 devices in a mesh: dp: 2 (over y_hi), seq: 8 (over x, y_lo), expert: 8 (over z, core).
Axes of the slice: x: 4, y: 4 (y_hi: 2, y_lo: 2; y = y_hi * 2 + y_lo), z: 4, core: 2. Of those that a mesh axis runs over, the one named last changes fastest.
Arguments:
- queries: bfloat16 [4, 4096, 4096], P('dp', 'seq', 'expert'), may hold values from -10 to 10
- keys: bfloat16 [4, 4096, 4096], P('dp', 'seq', 'expert'), may hold values from -10 to 10
- values: bfloat16 [4, 4096, 4096], P('dp', 'seq', 'expert'), may hold values from -6 to 6
- residual: bfloat16 [4, 4096, 4096], P('dp', ('seq', 'expert')), may hold values from -4 to 4
- out_weight: bfloat16 [4096, 4096], P('expert'), may hold values from -0.09375 to 0.09375
- norm_gain: float32 [4096], replicated, may hold values from 0.5 to 1.5
- routes: int32 [4, 4096, 2], P('dp', ('seq', 'expert')), may hold values from 0 to 63, all different within a row; in each aligned block of 64 rows (0 to 63, 64 to 127, ..., all dimensions but the last counted through in order) at most 3 rows name the same one
- route_weights: float32 [4, 4096, 2], P('dp', ('seq', 'expert')), may hold values from 0.2 to 1
- sample_flags: int32 [4], P('dp'), may hold values from 0 to 1, as said below
- cond_gate: float32 [2, 4096], replicated, may hold values from 0.5 to 1.5
- up_weight: bfloat16 [64, 4096, 512], P(('seq', 'expert')), may hold values from -0.09375 to 0.09375
- down_weight: bfloat16 [64, 512, 4096], P(('seq', 'expert')), may hold values from -0.25 to 0.25
- cotangent: bfloat16 [4, 4096, 4096], P('dp', ('seq', 'expert')), may hold values from -2 to 2
Outputs:
- block_out: bfloat16 [4, 4096, 4096], P('dp', ('seq', 'expert'))
- up_grad: bfloat16 [64, 4096, 512], P(('seq', 'expert'), None, 'dp')
- down_grad: bfloat16 [64, 512, 4096], P(('seq', 'expert'), 'dp')
The draws below stay inside these ranges and needn't reach their ends.
Inputs may be any that keep to these rules, and one draw needn't show every extreme that they name: `routes`: in each aligned block of 64 tokens of a sample no expert is named by more than 3 route entries, and in some blocks one is named by exactly 3; the two experts of a token differ. `sample_flags`: half of the 4 samples carry each flag.
All inputs are finite; a program needn't handle non-finite values.
Results may differ from the reference program's by a relative error of at most 0.025.
Values may be sent and summed in bfloat16 or wider, within the bound.
No kernel may reach another device: no remote copies, remote signals or barrier semaphores. Data moves between devices by JAX's collectives and lax.ppermute only.
A program may use at most 192 MiB of HBM per device.

```python
import math
import jax
import jax.numpy as jnp
import numpy as np
from jax import lax

D = 4096
HEADS = 32
FF = 512
LENGTH = 4096
GROUPS = 8
BATCH = 4
EXPERTS = 64
TOK_MOE = 64
MOST = 3
N_SEQ = 8
N_EXPERT = 8


def draw_queries(key, part):
    key = jax.random.fold_in(key, 5)
    return jnp.clip(2.0 * jax.random.normal(key, (BATCH, LENGTH, D), jnp.float32), -9.5, 9.5).astype(jnp.bfloat16)


def draw_keys(key, part):
    key = jax.random.fold_in(key, 6)
    return jnp.clip(2.0 * jax.random.normal(key, (BATCH, LENGTH, D), jnp.float32), -9.5, 9.5).astype(jnp.bfloat16)


def draw_sample_flags(key, part):
    key = jax.random.fold_in(key, 9)
    shuffled = jax.random.permutation(key, jnp.arange(BATCH, dtype=jnp.int32))
    return (shuffled % 2).astype(jnp.int32)


def levels(key, shape, shards, smallest, largest):
    def one(dim, shards_of):
        draws = jax.random.uniform(jax.random.fold_in(jax.random.fold_in(key, 6), dim), (shards_of,), jnp.float32, smallest / len(shards), largest / len(shards))
        return jnp.repeat(jnp.exp(draws), shape[dim] // shards_of).reshape((-1,) + (1,) * (len(shape) - dim - 1))

    factor_of = one(*shards[0])
    for cut in shards[1:]:
        factor_of = factor_of * one(*cut)
    return factor_of


def assign_block(rng, own, number, rows, amount, top, reach, skew):
    ranking = jax.random.permutation(rng, amount)
    packed, ordinary = portions_of(amount, rows * top, reach, skew, True), portions_of(amount, rows * top, reach, skew, False)
    places = jnp.arange(amount)

    def named(tallies, rotation):
        used = int((tallies > 0).sum())
        fixed = max(1, used // 4)
        moved = fixed + (places - fixed + rotation * (used - fixed)) % max(1, amount - fixed)
        return jnp.zeros((amount,), jnp.int32).at[ranking[jnp.where(places < fixed, places, moved)]].set(jnp.asarray(tallies, jnp.int32))

    tallies = jnp.where(number % 4 == 0, named(packed, number // 4), named(ordinary, number - number // 4 - 1))
    mixed = jax.random.permutation(jax.random.fold_in(own, 3), amount)
    donor, sink = mixed[0:amount // 2 * 2:2], mixed[1:amount // 2 * 2:2]
    slack = jnp.minimum(tallies[donor] - 1, reach - tallies[sink]) // 2
    slack = jnp.where((donor == ranking[0]) | (sink == ranking[0]) | (tallies[sink] == 0), 0, jnp.maximum(slack, 0))
    moved = jax.random.randint(jax.random.fold_in(own, 4), (amount // 2,), 0, 1 << 20) % (slack + 1)
    tallies = tallies.at[donor].add(-moved).at[sink].add(moved)
    items = jnp.searchsorted(jnp.cumsum(tallies), jnp.arange(rows * top), side="right").astype(jnp.int32)
    table = items.reshape(top, rows).T
    table = table[jax.random.permutation(jax.random.fold_in(own, 1), rows)]
    rotation = jax.random.randint(jax.random.fold_in(own, 2), (rows, 1), 0, top)
    return jnp.take_along_axis(table, (jnp.arange(top)[None, :] + rotation) % top, axis=1)


def portions_of(amount, total, reach, lean, full):
    weights = [(1 << 20) // math.isqrt(standing ** lean) + 1 for standing in range(1, amount + 1)]
    largest = reach if full else min(reach, max(-(-total // amount), total * weights[0] // sum(weights)))
    least = 1 if total - largest >= amount - 1 else 0
    counts, surplus = [largest] + [least] * (amount - 1), total - largest - least * (amount - 1)
    while surplus > 0:
        candidates = [i for i in range(1, amount) if counts[i] < largest] or [i for i in range(1, amount) if counts[i] < reach]
        whole, left = sum([weights[i] for i in candidates]), surplus
        for i in candidates:
            extra = min(reach - counts[i], max(1, left * weights[i] // whole), surplus)
            counts[i] = counts[i] + extra
            surplus = surplus - extra
    return np.array(counts)


def normal_values(rng, dims, width, limit, cuts=(), kind=jnp.bfloat16):
    result = width * jax.random.normal(rng, dims, jnp.float32)
    if cuts:
        result = result * levels(rng, dims, cuts, -0.22, 0.18)
    return jnp.clip(result, -limit, limit).astype(kind)


def setup_inputs(seed: int = 0) -> dict:
    splits = jax.random.split(jax.random.key(seed), 14)
    queries = draw_queries(jax.random.fold_in(splits[13], 71), 0)
    keys = draw_keys(jax.random.fold_in(splits[13], 71), 0)
    values = normal_values(splits[2], (BATCH, LENGTH, D), 1.0, 6.0, ((0, 2), (1, 8), (2, 8)))
    residual = normal_values(splits[3], (BATCH, LENGTH, D), 0.5, 4.0, ((0, 2), (1, 64)))
    out_weight = normal_values(splits[4], (D, D), D ** -0.5, 0.09375, ((0, 8),))
    norm_gain = jnp.clip(1.0 + 0.1 * jax.random.normal(splits[5], (D,), jnp.float32), 0.5, 1.5)
    routes_keys = jax.random.split(jax.random.fold_in(splits[6], 1), BATCH * LENGTH // TOK_MOE)
    routes_turns = jax.random.permutation(jax.random.fold_in(splits[6], 3), BATCH * LENGTH // TOK_MOE)
    routes = jax.vmap(lambda own, number: assign_block(jax.random.fold_in(splits[6], 2), own, number, TOK_MOE, EXPERTS, 2, MOST, 2))(routes_keys, routes_turns).reshape((BATCH, LENGTH, 2))
    route_weights = jnp.clip(0.2 + 0.8 * jax.random.uniform(splits[7], (BATCH, LENGTH, 2), jnp.float32) ** levels(splits[7], (BATCH, LENGTH, 2), ((0, 2), (1, 64)), -0.2, 0.2), 0.2, 1.0)
    sample_flags = draw_sample_flags(jax.random.fold_in(splits[13], 71), 0)
    cond_gate = jnp.clip(jax.random.uniform(splits[9], (2, D), jnp.float32, 0.5, 1.5), 0.5, 1.5)
    up_weight = normal_values(splits[10], (EXPERTS, D, FF), D ** -0.5, 0.09375, ((0, 64),))
    down_weight = normal_values(splits[11], (EXPERTS, FF, D), FF ** -0.5, 0.25, ((0, 64),))
    cotangent = normal_values(splits[12], (BATCH, LENGTH, D), 0.25, 2.0, ((0, 2), (1, 64)))
    return dict(queries=queries, keys=keys, values=values, residual=residual, out_weight=out_weight, norm_gain=norm_gain, routes=routes, route_weights=route_weights, sample_flags=sample_flags, cond_gate=cond_gate, up_weight=up_weight, down_weight=down_weight, cotangent=cotangent)


def rounded(value):
    return lax.optimization_barrier(value.astype(jnp.bfloat16))

def gelu_pair(pre):
    cdf_part = 0.5 * (1.0 + lax.erf(pre * 0.7071067811865476))
    density = jnp.exp(-0.5 * pre * pre) * 0.3989422804014327
    return (pre * cdf_part, cdf_part + pre * density)

def reference(queries, keys, values, residual, out_weight, norm_gain, routes, route_weights, sample_flags, cond_gate, up_weight, down_weight, cotangent):
    head_dim = D // HEADS
    scale = head_dim ** (-0.5)

    def one_head(index):
        batch_index = index // HEADS
        head_index = index % HEADS
        start = (batch_index, jnp.int32(0), head_index * head_dim)
        query_block = lax.dynamic_slice(queries, start, (1, LENGTH, head_dim))[0]
        key_block = lax.dynamic_slice(keys, start, (1, LENGTH, head_dim))[0]
        value_block = lax.dynamic_slice(values, start, (1, LENGTH, head_dim))[0]
        scores = jnp.dot(query_block, key_block.T, preferred_element_type=jnp.float32) * scale
        top = lax.optimization_barrier(jnp.max(scores, axis=1, keepdims=True))
        expo = jnp.exp(scores - top)
        total = lax.optimization_barrier(jnp.sum(expo, axis=1, keepdims=True))
        weighted = jnp.dot(rounded(expo), value_block, preferred_element_type=jnp.float32)
        return rounded(weighted / total)
    per_head = lax.map(one_head, jnp.arange(BATCH * HEADS, dtype=jnp.int32))
    attended = per_head.reshape(BATCH, HEADS, LENGTH, head_dim).transpose(0, 2, 1, 3).reshape(BATCH * LENGTH, D)
    group_width = D // GROUPS
    projected = jnp.zeros((BATCH * LENGTH, D), jnp.float32)
    for group in range(GROUPS):
        columns = attended[:, group * group_width:(group + 1) * group_width]
        rows = out_weight[group * group_width:(group + 1) * group_width]
        partial_g = rounded(jnp.dot(columns, rows, preferred_element_type=jnp.float32))
        projected = projected + partial_g.astype(jnp.float32)
    stream = residual.astype(jnp.float32) + projected.reshape(BATCH, LENGTH, D)
    normed = rounded(stream * lax.rsqrt(lax.optimization_barrier(jnp.mean(stream * stream, axis=-1, keepdims=True)) + 1e-06) * norm_gain)
    gate_vec = cond_gate[sample_flags]
    out_grad = rounded(route_weights[:, :, :, None] * gate_vec[:, None, None, :] * cotangent.astype(jnp.float32)[:, :, None, :])
    blocks = N_SEQ * N_EXPERT
    tok_moe = LENGTH // blocks
    expert_ids = routes.reshape(BATCH, blocks, tok_moe * 2)
    onehot = (expert_ids[:, :, :, None] == jnp.arange(EXPERTS, dtype=jnp.int32)).astype(jnp.int32)
    slot_index = lax.optimization_barrier(jnp.sum((jnp.cumsum(onehot, axis=2) - onehot) * onehot, axis=-1))
    batch_ids = jnp.arange(BATCH, dtype=jnp.int32)[:, None, None]
    block_ids = jnp.arange(blocks, dtype=jnp.int32)[None, :, None]
    flat_index = (((batch_ids * EXPERTS + expert_ids) * blocks + block_ids) * MOST + slot_index).reshape(-1)
    total_rows = BATCH * EXPERTS * blocks * MOST
    entries_in = jnp.broadcast_to(normed[:, :, None, :], (BATCH, LENGTH, 2, D)).reshape(-1, D)
    buffer_in = jnp.zeros((total_rows, D), jnp.bfloat16).at[flat_index].set(entries_in)
    buffer_grad = jnp.zeros((total_rows, D), jnp.bfloat16).at[flat_index].set(out_grad.reshape(-1, D))
    buffer_in = buffer_in.reshape(BATCH, EXPERTS, blocks * MOST, D)
    buffer_grad = buffer_grad.reshape(BATCH, EXPERTS, blocks * MOST, D)

    def one_expert(expert):
        rows_in = lax.dynamic_index_in_dim(buffer_in, expert, 1, keepdims=False).astype(jnp.float32)
        rows_grad = lax.dynamic_index_in_dim(buffer_grad, expert, 1, keepdims=False).astype(jnp.float32)
        up_mat = lax.dynamic_index_in_dim(up_weight, expert, 0, keepdims=False).astype(jnp.float32)
        down_mat = lax.dynamic_index_in_dim(down_weight, expert, 0, keepdims=False).astype(jnp.float32)
        pre = jnp.einsum('brd,df->brf', rows_in, up_mat)
        act, slope = gelu_pair(pre)
        hidden = rounded(act).astype(jnp.float32)
        produced = rounded(jnp.einsum('brf,fd->brd', hidden, down_mat))
        back_grad = jnp.einsum('brd,fd->brf', rows_grad, down_mat)
        pre_grad = rounded(back_grad * slope).astype(jnp.float32)
        down_part = rounded(jnp.einsum('brf,brd->bfd', hidden, rows_grad)).astype(jnp.float32)
        up_part = rounded(jnp.einsum('brd,brf->bdf', rows_in, pre_grad)).astype(jnp.float32)
        return (produced, lax.optimization_barrier(jnp.sum(up_part, axis=0)).astype(jnp.bfloat16), lax.optimization_barrier(jnp.sum(down_part, axis=0)).astype(jnp.bfloat16))
    produced, up_grad, down_grad = lax.map(one_expert, jnp.arange(EXPERTS, dtype=jnp.int32))
    produced = produced.transpose(1, 0, 2, 3).reshape(total_rows, D)
    returned = produced[flat_index].reshape(BATCH, LENGTH, 2, D).astype(jnp.float32)
    mixture = lax.optimization_barrier(jnp.sum(route_weights[:, :, :, None] * returned, axis=2))
    block_out = (stream + gate_vec[:, None, :] * mixture).astype(jnp.bfloat16)
    return (block_out, up_grad, down_grad)
```

```python
import functools

import jax
import jax.numpy as jnp
from jax import lax
from jax.experimental import pallas as pl
from jax.experimental.pallas import tpu as pltpu
from jax.sharding import Mesh
from jax.sharding import PartitionSpec as P

BF = jnp.bfloat16
F32 = jnp.float32
D = 4096
FF = 512
HEAD = 128
LENGTH = 4096
HALF = FF // 2
EXPERTS = 64
ROWS = 6
TOK = 128
SLOTS = EXPERTS * ROWS
CB = 4
CW = D // CB
GROUP = 8
GR = GROUP * ROWS
EXP_SCALE = HEAD**-0.5 * 1.4426950408889634
QB = 256
KB = 512
SEQ = ("x", "yl")
BACK = ("x", "yl", "core")
ALL = ("x", "yl", "z", "core")
VMEM_LIMIT = 56 * 1024 * 1024


def params(limit=VMEM_LIMIT):
    return pltpu.CompilerParams(vmem_limit_bytes=limit)


def whole(*shape):
    return pl.BlockSpec(shape, lambda *_: (0,) * len(shape))


def dot_nt(a, b):
    return lax.dot_general(a, b, (((1,), (1,)), ((), ())), preferred_element_type=F32)


def dot_tn(a, b):
    return lax.dot_general(a, b, (((0,), (0,)), ((), ())), preferred_element_type=F32)


def dot_nn(a, b):
    return jnp.dot(a, b, preferred_element_type=F32)


def pack(queries, keys, values):
    def kernel(q_ref, k_ref, v_ref, o_ref):
        o_ref[0, 0] = q_ref[0]
        o_ref[0, 1] = k_ref[0]
        o_ref[0, 2] = v_ref[0]

    spec = pl.BlockSpec((1, 512, HEAD), lambda b, h: (b, 0, h))
    return pl.pallas_call(
        kernel,
        grid=(2, 4),
        in_specs=[spec] * 3,
        out_specs=pl.BlockSpec((1, 3, 512, HEAD), lambda b, h: (b * 4 + h, 0, 0, 0)),
        out_shape=jax.ShapeDtypeStruct((8, 3, 512, HEAD), BF),
        compiler_params=params(),
        name="pack_heads",
    )(queries, keys, values)


def lane_tiles(value):
    return [value[:, j : j + 128] for j in range(0, value.shape[1], 128)]


def attend(rows):
    pieces = [slice(i, i + KB) for i in range(0, LENGTH, KB)]

    def scores_of(q, k, s_ref):
        top = None
        for cut in pieces:
            s = dot_nt(q, k[cut])
            s_ref[:, cut] = s
            high = functools.reduce(jnp.maximum, lane_tiles(s))
            top = high if top is None else jnp.maximum(top, high)
        return jnp.max(top, axis=-1, keepdims=True)

    def step(q_next, k, s_next, s_now, top_now, v):
        top = None
        out = None
        for cut in pieces:
            s = dot_nt(q_next, k[cut])
            p = jnp.exp2((s_now[:, cut] - top_now) * EXP_SCALE).astype(BF)
            s_next[:, cut] = s
            high = functools.reduce(jnp.maximum, lane_tiles(s))
            top = high if top is None else jnp.maximum(top, high)
            wide = jnp.concatenate([v[cut], jnp.ones((KB, HEAD), BF)], axis=1)
            part = dot_nn(p, wide)
            out = part if out is None else out + part
        return jnp.max(top, axis=-1, keepdims=True), out[:, :HEAD] / out[:, HEAD:]

    def kernel(q_ref, qn_ref, k_ref, v_ref, o_ref, sa_ref, sb_ref, top_ref):
        k = k_ref[:, 0].reshape(LENGTH, HEAD)
        v = v_ref[:, 0].reshape(LENGTH, HEAD)

        @pl.when(pl.program_id(0) == 0)
        def _():
            top_ref[...] = jnp.broadcast_to(scores_of(q_ref[0, 0, :QB], k, sa_ref), (QB, 128))

        top_a = top_ref[:, :1]
        top_b, out_a = step(q_ref[0, 0, QB:], k, sb_ref, sa_ref, top_a, v)
        top_n, out_b = step(qn_ref[0, 0], k, sa_ref, sb_ref, top_b, v)
        top_ref[...] = jnp.broadcast_to(top_n, (QB, 128))
        for base, out in ((0, out_a), (4, out_b)):
            for t in range(QB // 64):
                j = base + t
                o_ref[0, j % 2, j // 2] = out[64 * t : 64 * t + 64].astype(BF)

    def following(i):
        j = jnp.minimum(2 * i + 2, LENGTH // QB - 1)
        return (j // 2, 0, j % 2, 0)

    return pl.pallas_call(
        kernel,
        grid=(8,),
        in_specs=[
            pl.BlockSpec((1, 1, 512, HEAD), lambda i: (i, 0, 0, 0)),
            pl.BlockSpec((1, 1, QB, HEAD), following),
            pl.BlockSpec((8, 1, 512, HEAD), lambda i: (0, 1, 0, 0)),
            pl.BlockSpec((8, 1, 512, HEAD), lambda i: (0, 2, 0, 0)),
        ],
        out_specs=pl.BlockSpec((1, 2, 4, 64, HEAD), lambda i: (i, 0, 0, 0, 0)),
        out_shape=jax.ShapeDtypeStruct((8, 2, 4, 64, HEAD), BF),
        scratch_shapes=[
            pltpu.VMEM((QB, LENGTH), F32),
            pltpu.VMEM((QB, LENGTH), F32),
            pltpu.VMEM((QB, 128), F32),
        ],
        compiler_params=params(),
        cost_estimate=pl.CostEstimate(
            flops=4 * LENGTH * LENGTH * 256, bytes_accessed=4 << 20, transcendentals=LENGTH * LENGTH
        ),
        name="attend",
    )(rows, rows, rows, rows)


def project(place, heads, weight_own, weight_other):
    def kernel(place_ref, a_ref, wo_ref, ws_ref, fa, fb, ua, ub, da, db, own):
        core = place_ref[1]

        def side(c):
            return jnp.concatenate(
                [
                    jnp.concatenate([a_ref[b, h, c, 0] for h in range(4)], axis=1)
                    for b in range(2)
                ],
                axis=0,
            )

        lhs_own = side(core)
        lhs_other = side(1 - core)
        total = dot_nn(lhs_own, wo_ref[...]) + dot_nn(lhs_other, ws_ref[...])
        for number, refs in enumerate(((fa, fb), (ua, ub), (da, db))):

            @pl.when(pl.program_id(0) == number)
            def _(refs=refs):
                refs[0][...] = total[:, : D // 2].astype(BF)
                refs[1][...] = total[:, D // 2 :].astype(BF)

        @pl.when(pl.program_id(0) == 3)
        def _():
            own[...] = total.astype(BF)

    def chunk_index(r, place_ref):
        offset = jnp.where(r == 0, 2, jnp.where(r == 1, 1, jnp.where(r == 2, 3, 0)))
        return (0, 0, 0, lax.rem(place_ref[0] + offset, 4), 0, 0)

    half = jax.ShapeDtypeStruct((TOK, D // 2), BF)
    return pl.pallas_call(
        kernel,
        grid_spec=pltpu.PrefetchScalarGridSpec(
            num_scalar_prefetch=1,
            grid=(4,),
            in_specs=[
                pl.BlockSpec((2, 4, 2, 1, 64, HEAD), chunk_index),
                whole(FF, D),
                whole(FF, D),
            ],
            out_specs=[whole(TOK, D // 2)] * 6 + [whole(TOK, D)],
        ),
        out_shape=[half] * 6 + [jax.ShapeDtypeStruct((TOK, D), BF)],
        compiler_params=params(),
        cost_estimate=pl.CostEstimate(
            flops=2 * 512 * 1024 * D, bytes_accessed=13 << 20, transcendentals=0
        ),
        name="project",
    )(place, heads, weight_own, weight_other)


def source_of(d):
    return lax.rem(d, CB * ROWS) // ROWS * GR + d // (CB * ROWS) * ROWS + lax.rem(d, ROWS)


def mixer():
    n = CB * GR
    d = lax.broadcasted_iota(jnp.int32, (n, n), 0)
    s = lax.broadcasted_iota(jnp.int32, (n, n), 1)
    return (s == source_of(d)).astype(BF)


def unmixer():
    n = CB * GR
    s = lax.broadcasted_iota(jnp.int32, (n, n), 0)
    d = lax.broadcasted_iota(jnp.int32, (n, n), 1)
    return (s == source_of(d)).astype(BF)


def mix_out(sc_ref, o_ref):
    mat = mixer()
    for g in range(EXPERTS // GROUP):
        stack = jnp.concatenate([sc_ref[c, g * GR : (g + 1) * GR, :] for c in range(CB)], axis=0)
        o_ref[g * CB * GR : (g + 1) * CB * GR, :] = dot_nn(mat, stack).astype(BF)


def mix_in(i_ref, sc_ref):
    mat = unmixer()
    for g in range(EXPERTS // GROUP):
        stack = dot_nn(mat, i_ref[g * CB * GR : (g + 1) * CB * GR, :]).astype(BF)
        for c in range(CB):
            sc_ref[c, g * GR : (g + 1) * GR, :] = stack[c * GR : (c + 1) * GR]


def placing(tgt_ref, k):
    slot = lax.broadcasted_iota(jnp.int32, (SLOTS, TOK), 0)
    return slot == tgt_ref[k : k + 1, :]


def send_grads(cotangent, gate, target, weight):
    def kernel(cot_ref, gate_ref, tgt_ref, w_ref, o_ref, sc_ref):
        first, second = placing(tgt_ref, 0), placing(tgt_ref, 1)
        both = (first | second).astype(BF)
        w = jnp.sum(
            jnp.where(first, w_ref[0:1, :], 0.0) + jnp.where(second, w_ref[1:2, :], 0.0),
            axis=1,
            keepdims=True,
        )
        odd = lax.rem(lax.broadcasted_iota(jnp.int32, (SLOTS, 1), 0), 2) == 1
        for c in range(CB):
            cut = slice(c * CW, (c + 1) * CW)
            rows = dot_nn(both, cot_ref[:, cut])
            gates = jnp.where(odd, gate_ref[1:2, cut], gate_ref[0:1, cut])
            sc_ref[c] = (w * gates * rows).astype(BF)
        mix_out(sc_ref, o_ref)

    return pl.pallas_call(
        kernel,
        grid=(1,),
        in_specs=[whole(TOK, D), whole(2, D), whole(2, TOK), whole(2, TOK)],
        out_specs=whole(CB * SLOTS, CW),
        out_shape=jax.ShapeDtypeStruct((CB * SLOTS, CW), BF),
        scratch_shapes=[pltpu.VMEM((CB, SLOTS, CW), BF)],
        compiler_params=params(),
        name="send_grads",
    )(cotangent, gate, target, weight)


def norm_send(own, up_a, up_b, down_a, down_b, residual, gain, target):
    def kernel(own_ref, ua, ub, da, db, res_ref, gain_ref, tgt_ref, s_ref, o_ref, sc_ref):
        square = jnp.zeros((TOK, 1), F32)
        for half, first, second in ((0, ua, da), (1, ub, db)):
            cut = slice(half * D // 2, (half + 1) * D // 2)
            s = own_ref[:, cut].astype(F32) + first[...].astype(F32) + second[...].astype(F32)
            s = res_ref[:, cut].astype(F32) + s
            s_ref[:, cut] = s
            square += jnp.sum(s * s, axis=1, keepdims=True)
        factor = lax.rsqrt(square * (1.0 / D) + 1e-06)
        both = (placing(tgt_ref, 0) | placing(tgt_ref, 1)).astype(BF)
        for c in range(CB):
            cut = slice(c * CW, (c + 1) * CW)
            normed = (s_ref[:, cut] * factor * gain_ref[:, cut]).astype(BF)
            sc_ref[c] = dot_nn(both, normed).astype(BF)
        mix_out(sc_ref, o_ref)

    return pl.pallas_call(
        kernel,
        grid=(1,),
        in_specs=[whole(TOK, D)]
        + [whole(TOK, D // 2)] * 4
        + [whole(TOK, D), whole(1, D), whole(2, TOK)],
        out_specs=[whole(TOK, D), whole(CB * SLOTS, CW)],
        out_shape=[
            jax.ShapeDtypeStruct((TOK, D), F32),
            jax.ShapeDtypeStruct((CB * SLOTS, CW), BF),
        ],
        scratch_shapes=[pltpu.VMEM((CB, SLOTS, CW), BF)],
        compiler_params=params(),
        name="norm_send",
    )(own, up_a, up_b, down_a, down_b, residual, gain, target)


def grads_in(chunks, down):
    def kernel(i_ref, d_ref, g_ref, b_ref):
        mix_in(i_ref, g_ref)
        back = None
        for c in range(CB):
            part = dot_nt(g_ref[c], d_ref[:, c * CW : (c + 1) * CW])
            back = part if back is None else back + part
        b_ref[...] = back

    return pl.pallas_call(
        kernel,
        grid=(1,),
        in_specs=[whole(CB * SLOTS, CW), whole(FF, D)],
        out_specs=[whole(CB, SLOTS, CW), whole(SLOTS, FF)],
        out_shape=[
            jax.ShapeDtypeStruct((CB, SLOTS, CW), BF),
            jax.ShapeDtypeStruct((SLOTS, FF), F32),
        ],
        compiler_params=params(),
        name="grads_in",
    )(chunks, down)


def gelu_pair(pre):
    cdf_part = 0.5 * (1.0 + lax.erf(pre * 0.7071067811865476))
    density = jnp.exp(-0.5 * pre * pre) * 0.3989422804014327
    return (pre * cdf_part, cdf_part + pre * density)


def experts(place, chunks, up, down, back):
    def kernel(place_ref, i_ref, up_ref, down_ref, b_ref, x_ref, ho_ref, hs_ref, pg_ref, o_ref, pre, hid, prod):
        i = pl.program_id(0)

        @pl.when(i == 0)
        def _():
            mix_in(i_ref, x_ref)
            pre[...] = dot_nn(x_ref[0], up_ref[...])

        @pl.when((i > 0) & (i < CB))
        def _():
            pre[...] += dot_nn(x_ref[i], up_ref[...])

        @pl.when(i == CB - 1)
        def _():
            act, slope = gelu_pair(pre[...])
            hid[...] = act.astype(BF)
            pg_ref[...] = (b_ref[...] * slope).astype(BF)
            low, high = act[:, :HALF].astype(BF), act[:, HALF:].astype(BF)
            mine = place_ref[2] == 0
            hs_ref[...] = jnp.where(mine, low, high)
            ho_ref[...] = jnp.where(mine, high, low)

        @pl.when(i >= CB)
        def _():
            prod[i - CB] = dot_nn(hid[...], down_ref[...]).astype(BF)

        @pl.when(i == 2 * CB - 1)
        def _():
            mix_out(prod, o_ref)

    return pl.pallas_call(
        kernel,
        grid_spec=pltpu.PrefetchScalarGridSpec(
            num_scalar_prefetch=1,
            grid=(2 * CB,),
            in_specs=[
                whole(CB * SLOTS, CW),
                pl.BlockSpec((CW, FF), lambda i, _: (jnp.minimum(i, CB - 1), 0)),
                pl.BlockSpec((FF, CW), lambda i, _: (0, jnp.maximum(i - CB, 0))),
                whole(SLOTS, FF),
            ],
            out_specs=[
                whole(CB, SLOTS, CW),
                whole(SLOTS, HALF),
                whole(SLOTS, HALF),
                whole(SLOTS, FF),
                whole(CB * SLOTS, CW),
            ],
            scratch_shapes=[
                pltpu.VMEM((SLOTS, FF), F32),
                pltpu.VMEM((SLOTS, FF), BF),
                pltpu.VMEM((CB, SLOTS, CW), BF),
            ],
        ),
        out_shape=[
            jax.ShapeDtypeStruct((CB, SLOTS, CW), BF),
            jax.ShapeDtypeStruct((SLOTS, HALF), BF),
            jax.ShapeDtypeStruct((SLOTS, HALF), BF),
            jax.ShapeDtypeStruct((SLOTS, FF), BF),
            jax.ShapeDtypeStruct((CB * SLOTS, CW), BF),
        ],
        compiler_params=params(),
        name="experts",
    )(place, chunks, up, down, back)


def up_half(half, rows, pre_grad):
    def kernel(half_ref, x_ref, p_ref, o_ref):
        o_ref[...] = dot_tn(x_ref[0], p_ref[...]).astype(BF)

    return pl.pallas_call(
        kernel,
        grid_spec=pltpu.PrefetchScalarGridSpec(
            num_scalar_prefetch=1,
            grid=(CB,),
            in_specs=[
                pl.BlockSpec((1, SLOTS, CW), lambda c, _: (c, 0, 0)),
                pl.BlockSpec((SLOTS, HALF), lambda c, half_ref: (0, half_ref[0])),
            ],
            out_specs=pl.BlockSpec((CW, HALF), lambda c, _: (c, 0)),
        ),
        out_shape=jax.ShapeDtypeStruct((D, HALF), BF),
        compiler_params=params(),
        cost_estimate=pl.CostEstimate(
            flops=2 * SLOTS * D * HALF, bytes_accessed=6 << 20, transcendentals=0
        ),
        name="up_half",
    )(half, rows, pre_grad)


def down_sum(hidden, grads, hidden_far, grads_far):
    def kernel(h_ref, g_ref, hf_ref, gf_ref, o_ref):
        total = dot_tn(h_ref[...], g_ref[0]) + dot_tn(hf_ref[...], gf_ref[0])
        o_ref[...] = total.astype(BF)

    rows = pl.BlockSpec((1, SLOTS, CW), lambda c: (c, 0, 0))
    return pl.pallas_call(
        kernel,
        grid=(CB,),
        in_specs=[whole(SLOTS, HALF), rows, whole(SLOTS, HALF), rows],
        out_specs=pl.BlockSpec((HALF, CW), lambda c: (0, c)),
        out_shape=jax.ShapeDtypeStruct((HALF, D), BF),
        compiler_params=params(),
        cost_estimate=pl.CostEstimate(
            flops=4 * SLOTS * D * HALF, bytes_accessed=9 << 20, transcendentals=0
        ),
        name="down_sum",
    )(hidden, grads, hidden_far, grads_far)


def combine(chunks, stream, gate, target, weight):
    def kernel(i_ref, s_ref, gate_ref, tgt_ref, w_ref, o_ref, sc_ref):
        mix_in(i_ref, sc_ref)
        first, second = placing(tgt_ref, 0).astype(BF), placing(tgt_ref, 1).astype(BF)
        late = lax.broadcasted_iota(jnp.int32, (TOK, 1), 0) >= TOK // 2
        for c in range(CB):
            cut = slice(c * CW, (c + 1) * CW)
            mix = w_ref[:, 0:1] * dot_tn(first, sc_ref[c]) + w_ref[:, 1:2] * dot_tn(second, sc_ref[c])
            gates = jnp.where(late, gate_ref[1:2, cut], gate_ref[0:1, cut])
            o_ref[:, cut] = (s_ref[:, cut] + gates * mix).astype(BF)

    return pl.pallas_call(
        kernel,
        grid=(1,),
        in_specs=[whole(CB * SLOTS, CW), whole(TOK, D), whole(2, D), whole(2, TOK), whole(TOK, 2)],
        out_specs=whole(TOK, D),
        out_shape=jax.ShapeDtypeStruct((TOK, D), BF),
        scratch_shapes=[pltpu.VMEM((CB, SLOTS, CW), BF)],
        compiler_params=params(),
        name="combine",
    )(chunks, stream, gate, target, weight)


def plus(a, b):
    return (a.astype(F32) + b.astype(F32)).astype(BF)


def body(
    queries,
    keys,
    values,
    residual,
    out_weight,
    norm_gain,
    routes,
    route_weights,
    sample_flags,
    cond_gate,
    up_weight,
    down_weight,
    cotangent,
):
    z, core, dp = lax.axis_index("z"), lax.axis_index("core"), lax.axis_index("dp")
    place = jnp.stack([z, core, dp]).astype(jnp.int32)
    swap = [(0, 1), (1, 0)]
    above = [(i, (i + 1) % 4) for i in range(4)]
    below = [(i, (i + 3) % 4) for i in range(4)]
    exchange = functools.partial(lax.all_to_all, split_axis=0, concat_axis=0, tiled=True)

    ids = routes.reshape(2, TOK)
    earlier = jnp.arange(TOK)[:, None] > jnp.arange(TOK)[None, :]
    same = (ids[:, :, None] == ids[:, None, :]) & earlier[None]
    slot = jnp.sum(same.astype(jnp.int32), axis=2)
    row = ids * ROWS + slot * 2 + jnp.arange(2, dtype=jnp.int32)[:, None]
    target = row.reshape(TOK, 2).T
    weight_col = route_weights.reshape(TOK, 2)
    gate = jnp.where((sample_flags == 1)[:, None], cond_gate[1][None, :], cond_gate[0][None, :])

    rows = exchange(pack(queries, keys, values), SEQ)
    weight_other = lax.ppermute(out_weight, "core", swap)

    grad_chunks = send_grads(cotangent.reshape(TOK, D), gate, target, weight_col.T)
    rows, grad_chunks = lax.optimization_barrier((rows, grad_chunks))
    grad_arrived = exchange(grad_chunks, ALL)

    heads = attend(rows).reshape(16, 256, HEAD)
    heads = exchange(heads, BACK).reshape(2, 4, 2, 4, 64, HEAD)
    fa, fb, ua, ub, da, db, own = project(place, heads, out_weight, weight_other)
    fa = lax.ppermute(fa, "z", above)
    fb = lax.ppermute(fb, "z", below)
    ub = lax.ppermute(ub, "z", above)
    da = lax.ppermute(da, "z", below)
    ua = lax.ppermute(plus(ua, fa), "z", above)
    db = lax.ppermute(plus(db, fb), "z", below)
    stream, chunks = norm_send(
        own, ua, ub, da, db, residual.reshape(TOK, D), norm_gain[None], target
    )
    arrived = exchange(chunks, ALL)

    grads, back = grads_in(grad_arrived, down_weight[0])
    grads_far = lax.ppermute(grads, "dp", swap)

    own_rows, hid_other, hid_own, pre_grad, products = experts(
        place, arrived, up_weight[0], down_weight[0], back
    )
    returned = exchange(products, ALL)
    hid_far = lax.ppermute(hid_other, "dp", swap)
    up_other = up_half((1 - dp)[None].astype(jnp.int32), own_rows, pre_grad)
    up_far = lax.ppermute(up_other, "dp", swap)
    up_own = up_half(dp[None].astype(jnp.int32), own_rows, pre_grad)
    down_total = down_sum(hid_own, grads, hid_far, grads_far)
    block_out = combine(returned, stream, gate, target, weight_col)
    up_total = plus(up_own, up_far)
    return (block_out.reshape(2, TOK // 2, D), up_total[None], down_total[None])


def solution(mesh):
    fine = Mesh(mesh.devices.reshape(2, 4, 2, 4, 2), ("dp", "x", "yl", "z", "core"))
    expert = ("z", "core")
    tokens = P("dp", ALL, None)
    placed = (
        P("dp", SEQ, expert),
        P("dp", SEQ, expert),
        P("dp", SEQ, expert),
        tokens,
        P(expert, None),
        P(),
        tokens,
        tokens,
        P("dp"),
        P(),
        P(ALL, None, None),
        P(ALL, None, None),
        tokens,
    )
    return jax.shard_map(
        body,
        mesh=fine,
        in_specs=placed,
        out_specs=(tokens, P(ALL, None, "dp"), P(ALL, "dp", None)),
        check_vma=False,
    )
```

```python
import functools

import jax
import jax.numpy as jnp
from jax import lax
from jax.experimental import pallas as pl
from jax.experimental.pallas import tpu as pltpu
from jax.sharding import Mesh
from jax.sharding import PartitionSpec as P

BF = jnp.bfloat16
F32 = jnp.float32
D = 4096
FF = 512
HEAD = 128
LENGTH = 4096
HALF = FF // 2
EXPERTS = 64
ROWS = 6
TOK = 128
SLOTS = EXPERTS * ROWS
CB = 4
CW = D // CB
GROUP = 8
GR = GROUP * ROWS
EXP_SCALE = HEAD**-0.5 * 1.4426950408889634
QB = 256
KB = 512
SEQ = ("x", "yl")
BACK = ("x", "yl", "core")
ALL = ("x", "yl", "z", "core")
VMEM_LIMIT = 56 * 1024 * 1024


def params(limit=VMEM_LIMIT):
    return pltpu.CompilerParams(vmem_limit_bytes=limit)


def whole(*shape):
    return pl.BlockSpec(shape, lambda *_: (0,) * len(shape))


def dot_nt(a, b):
    return lax.dot_general(a, b, (((1,), (1,)), ((), ())), preferred_element_type=F32)


def dot_tn(a, b):
    return lax.dot_general(a, b, (((0,), (0,)), ((), ())), preferred_element_type=F32)


def dot_nn(a, b):
    return jnp.dot(a, b, preferred_element_type=F32)


def pack(queries, keys, values):
    def kernel(q_ref, k_ref, v_ref, o_ref):
        o_ref[0, 0] = q_ref[0]
        o_ref[0, 1] = k_ref[0]
        o_ref[0, 2] = v_ref[0]

    spec = pl.BlockSpec((1, 512, HEAD), lambda b, h: (b, 0, h))
    return pl.pallas_call(
        kernel,
        grid=(2, 4),
        in_specs=[spec] * 3,
        out_specs=pl.BlockSpec((1, 3, 512, HEAD), lambda b, h: (b * 4 + h, 0, 0, 0)),
        out_shape=jax.ShapeDtypeStruct((8, 3, 512, HEAD), BF),
        compiler_params=params(),
        name="pack_heads",
    )(queries, keys, values)


def lane_tiles(value):
    return [value[:, j : j + 128] for j in range(0, value.shape[1], 128)]


def attend(rows):
    pieces = [slice(i, i + KB) for i in range(0, LENGTH, KB)]

    def scores_of(q, k, s_ref):
        top = None
        for cut in pieces:
            s = dot_nt(q, k[cut])
            s_ref[:, cut] = s
            high = functools.reduce(jnp.maximum, lane_tiles(s))
            top = high if top is None else jnp.maximum(top, high)
        return jnp.max(top, axis=-1, keepdims=True)

    def step(q_next, k, s_next, s_now, top_now, v):
        top = None
        out = None
        for cut in pieces:
            s = dot_nt(q_next, k[cut])
            p = jnp.exp2((s_now[:, cut] - top_now) * EXP_SCALE).astype(BF)
            s_next[:, cut] = s
            high = functools.reduce(jnp.maximum, lane_tiles(s))
            top = high if top is None else jnp.maximum(top, high)
            wide = jnp.concatenate([v[cut], jnp.ones((KB, HEAD), BF)], axis=1)
            part = dot_nn(p, wide)
            out = part if out is None else out + part
        return jnp.max(top, axis=-1, keepdims=True), out[:, :HEAD] / out[:, HEAD:]

    def kernel(q_ref, qn_ref, k_ref, v_ref, o_ref, sa_ref, sb_ref, top_ref):
        k = k_ref[:, 0].reshape(LENGTH, HEAD)
        v = v_ref[:, 0].reshape(LENGTH, HEAD)

        @pl.when(pl.program_id(0) == 0)
        def _():
            top_ref[...] = jnp.broadcast_to(scores_of(q_ref[0, 0, :QB], k, sa_ref), (QB, 128))

        top_a = top_ref[:, :1]
        top_b, out_a = step(q_ref[0, 0, QB:], k, sb_ref, sa_ref, top_a, v)
        top_n, out_b = step(qn_ref[0, 0], k, sa_ref, sb_ref, top_b, v)
        top_ref[...] = jnp.broadcast_to(top_n, (QB, 128))
        for base, out in ((0, out_a), (4, out_b)):
            for t in range(QB // 64):
                j = base + t
                o_ref[0, j % 2, j // 2] = out[64 * t : 64 * t + 64].astype(BF)

    def following(i):
        j = jnp.minimum(2 * i + 2, LENGTH // QB - 1)
        return (j // 2, 0, j % 2, 0)

    return pl.pallas_call(
        kernel,
        grid=(8,),
        in_specs=[
            pl.BlockSpec((1, 1, 512, HEAD), lambda i: (i, 0, 0, 0)),
            pl.BlockSpec((1, 1, QB, HEAD), following),
            pl.BlockSpec((8, 1, 512, HEAD), lambda i: (0, 1, 0, 0)),
            pl.BlockSpec((8, 1, 512, HEAD), lambda i: (0, 2, 0, 0)),
        ],
        out_specs=pl.BlockSpec((1, 2, 4, 64, HEAD), lambda i: (i, 0, 0, 0, 0)),
        out_shape=jax.ShapeDtypeStruct((8, 2, 4, 64, HEAD), BF),
        scratch_shapes=[
            pltpu.VMEM((QB, LENGTH), F32),
            pltpu.VMEM((QB, LENGTH), F32),
            pltpu.VMEM((QB, 128), F32),
        ],
        compiler_params=params(),
        cost_estimate=pl.CostEstimate(
            flops=4 * LENGTH * LENGTH * 256, bytes_accessed=4 << 20, transcendentals=LENGTH * LENGTH
        ),
        name="attend",
    )(rows, rows, rows, rows)


def project(place, half, heads, weight_own, weight_other):
    width = 512
    blocks = D // 2 // width

    def kernel(place_ref, a_ref, wo_ref, ws_ref, *refs):
        lhs = refs[-1]
        core = place_ref[1]

        @pl.when(pl.program_id(0) == 0)
        def _():
            for side, c in enumerate((core, 1 - core)):
                for number, offset in enumerate((2, 1, 3, 0)):
                    z = lax.rem(place_ref[0] + offset, 4)
                    for b in range(2):
                        for h in range(4):
                            lhs[
                                number * TOK + b * 64 : number * TOK + (b + 1) * 64,
                                side * FF + h * HEAD : side * FF + (h + 1) * HEAD,
                            ] = a_ref[b, h, c, z]

        total = dot_nn(lhs[:, :FF], wo_ref[...]) + dot_nn(lhs[:, FF:], ws_ref[...])
        for number in range(4):
            refs[number][...] = total[number * TOK : (number + 1) * TOK].astype(BF)

    weights = pl.BlockSpec((FF, width), lambda n, _: (0, half * blocks + n))
    return pl.pallas_call(
        kernel,
        grid_spec=pltpu.PrefetchScalarGridSpec(
            num_scalar_prefetch=1,
            grid=(blocks,),
            in_specs=[whole(2, 4, 2, 4, 64, HEAD), weights, weights],
            out_specs=[pl.BlockSpec((TOK, width), lambda n, _: (0, n))] * 4,
            scratch_shapes=[pltpu.VMEM((4 * TOK, 2 * FF), BF)],
        ),
        out_shape=[jax.ShapeDtypeStruct((TOK, D // 2), BF)] * 4,
        compiler_params=params(),
        cost_estimate=pl.CostEstimate(
            flops=512 * 1024 * D, bytes_accessed=7 << 20, transcendentals=0
        ),
        name="project",
    )(place, heads, weight_own, weight_other)


def source_of(d):
    return lax.rem(d, CB * ROWS) // ROWS * GR + d // (CB * ROWS) * ROWS + lax.rem(d, ROWS)


def mixer():
    n = CB * GR
    d = lax.broadcasted_iota(jnp.int32, (n, n), 0)
    s = lax.broadcasted_iota(jnp.int32, (n, n), 1)
    return (s == source_of(d)).astype(BF)


def unmixer():
    n = CB * GR
    s = lax.broadcasted_iota(jnp.int32, (n, n), 0)
    d = lax.broadcasted_iota(jnp.int32, (n, n), 1)
    return (s == source_of(d)).astype(BF)


def mix_out(sc_ref, o_ref):
    mat = mixer()
    for g in range(EXPERTS // GROUP):
        stack = jnp.concatenate([sc_ref[c, g * GR : (g + 1) * GR, :] for c in range(CB)], axis=0)
        o_ref[g * CB * GR : (g + 1) * CB * GR, :] = dot_nn(mat, stack).astype(BF)


def mix_in(i_ref, sc_ref):
    mat = unmixer()
    for g in range(EXPERTS // GROUP):
        stack = dot_nn(mat, i_ref[g * CB * GR : (g + 1) * CB * GR, :]).astype(BF)
        for c in range(CB):
            sc_ref[c, g * GR : (g + 1) * GR, :] = stack[c * GR : (c + 1) * GR]


def placing(tgt_ref, k):
    slot = lax.broadcasted_iota(jnp.int32, (SLOTS, TOK), 0)
    return slot == tgt_ref[k : k + 1, :]


def send_grads(cotangent, gate, target, weight):
    def kernel(cot_ref, gate_ref, tgt_ref, w_ref, o_ref, sc_ref):
        first, second = placing(tgt_ref, 0), placing(tgt_ref, 1)
        both = (first | second).astype(BF)
        w = jnp.sum(
            jnp.where(first, w_ref[0:1, :], 0.0) + jnp.where(second, w_ref[1:2, :], 0.0),
            axis=1,
            keepdims=True,
        )
        odd = lax.rem(lax.broadcasted_iota(jnp.int32, (SLOTS, 1), 0), 2) == 1
        for c in range(CB):
            cut = slice(c * CW, (c + 1) * CW)
            rows = dot_nn(both, cot_ref[:, cut])
            gates = jnp.where(odd, gate_ref[1:2, cut], gate_ref[0:1, cut])
            sc_ref[c] = (w * gates * rows).astype(BF)
        mix_out(sc_ref, o_ref)

    return pl.pallas_call(
        kernel,
        grid=(1,),
        in_specs=[whole(TOK, D), whole(2, D), whole(2, TOK), whole(2, TOK)],
        out_specs=whole(CB * SLOTS, CW),
        out_shape=jax.ShapeDtypeStruct((CB * SLOTS, CW), BF),
        scratch_shapes=[pltpu.VMEM((CB, SLOTS, CW), BF)],
        compiler_params=params(),
        name="send_grads",
    )(cotangent, gate, target, weight)


def norm_send(own_a, own_b, up_a, up_b, down_a, down_b, residual, gain, target):
    def kernel(oa, ob, ua, ub, da, db, res_ref, gain_ref, tgt_ref, s_ref, o_ref, sc_ref):
        square = jnp.zeros((TOK, 1), F32)
        for half, own, first, second in ((0, oa, ua, da), (1, ob, ub, db)):
            cut = slice(half * D // 2, (half + 1) * D // 2)
            s = own[...].astype(F32) + first[...].astype(F32) + second[...].astype(F32)
            s = res_ref[:, cut].astype(F32) + s
            s_ref[:, cut] = s
            square += jnp.sum(s * s, axis=1, keepdims=True)
        factor = lax.rsqrt(square * (1.0 / D) + 1e-06)
        both = (placing(tgt_ref, 0) | placing(tgt_ref, 1)).astype(BF)
        for c in range(CB):
            cut = slice(c * CW, (c + 1) * CW)
            normed = (s_ref[:, cut] * factor * gain_ref[:, cut]).astype(BF)
            sc_ref[c] = dot_nn(both, normed).astype(BF)
        mix_out(sc_ref, o_ref)

    return pl.pallas_call(
        kernel,
        grid=(1,),
        in_specs=[whole(TOK, D // 2)] * 6
        + [whole(TOK, D), whole(1, D), whole(2, TOK)],
        out_specs=[whole(TOK, D), whole(CB * SLOTS, CW)],
        out_shape=[
            jax.ShapeDtypeStruct((TOK, D), F32),
            jax.ShapeDtypeStruct((CB * SLOTS, CW), BF),
        ],
        scratch_shapes=[pltpu.VMEM((CB, SLOTS, CW), BF)],
        compiler_params=params(),
        name="norm_send",
    )(own_a, own_b, up_a, up_b, down_a, down_b, residual, gain, target)


def grads_in(chunks, down):
    def kernel(i_ref, d_ref, g_ref, b_ref):
        mix_in(i_ref, g_ref)
        back = None
        for c in range(CB):
            part = dot_nt(g_ref[c], d_ref[:, c * CW : (c + 1) * CW])
            back = part if back is None else back + part
        b_ref[...] = back

    return pl.pallas_call(
        kernel,
        grid=(1,),
        in_specs=[whole(CB * SLOTS, CW), whole(FF, D)],
        out_specs=[whole(CB, SLOTS, CW), whole(SLOTS, FF)],
        out_shape=[
            jax.ShapeDtypeStruct((CB, SLOTS, CW), BF),
            jax.ShapeDtypeStruct((SLOTS, FF), F32),
        ],
        compiler_params=params(),
        name="grads_in",
    )(chunks, down)


def gelu_pair(pre):
    cdf_part = 0.5 * (1.0 + lax.erf(pre * 0.7071067811865476))
    density = jnp.exp(-0.5 * pre * pre) * 0.3989422804014327
    return (pre * cdf_part, cdf_part + pre * density)


def experts(place, chunks, up, down, back):
    def kernel(place_ref, i_ref, up_ref, down_ref, b_ref, x_ref, ho_ref, hs_ref, pg_ref, o_ref, pre, hid, prod):
        i = pl.program_id(0)

        @pl.when(i == 0)
        def _():
            mix_in(i_ref, x_ref)
            pre[...] = dot_nn(x_ref[0], up_ref[...])

        @pl.when((i > 0) & (i < CB))
        def _():
            pre[...] += dot_nn(x_ref[i], up_ref[...])

        @pl.when(i == CB - 1)
        def _():
            act, slope = gelu_pair(pre[...])
            hid[...] = act.astype(BF)
            pg_ref[...] = (b_ref[...] * slope).astype(BF)
            low, high = act[:, :HALF].astype(BF), act[:, HALF:].astype(BF)
            mine = place_ref[2] == 0
            hs_ref[...] = jnp.where(mine, low, high)
            ho_ref[...] = jnp.where(mine, high, low)

        @pl.when(i >= CB)
        def _():
            prod[i - CB] = dot_nn(hid[...], down_ref[...]).astype(BF)

        @pl.when(i == 2 * CB - 1)
        def _():
            mix_out(prod, o_ref)

    return pl.pallas_call(
        kernel,
        grid_spec=pltpu.PrefetchScalarGridSpec(
            num_scalar_prefetch=1,
            grid=(2 * CB,),
            in_specs=[
                whole(CB * SLOTS, CW),
                pl.BlockSpec((CW, FF), lambda i, _: (jnp.minimum(i, CB - 1), 0)),
                pl.BlockSpec((FF, CW), lambda i, _: (0, jnp.maximum(i - CB, 0))),
                whole(SLOTS, FF),
            ],
            out_specs=[
                whole(CB, SLOTS, CW),
                whole(SLOTS, HALF),
                whole(SLOTS, HALF),
                whole(SLOTS, FF),
                whole(CB * SLOTS, CW),
            ],
            scratch_shapes=[
                pltpu.VMEM((SLOTS, FF), F32),
                pltpu.VMEM((SLOTS, FF), BF),
                pltpu.VMEM((CB, SLOTS, CW), BF),
            ],
        ),
        out_shape=[
            jax.ShapeDtypeStruct((CB, SLOTS, CW), BF),
            jax.ShapeDtypeStruct((SLOTS, HALF), BF),
            jax.ShapeDtypeStruct((SLOTS, HALF), BF),
            jax.ShapeDtypeStruct((SLOTS, FF), BF),
            jax.ShapeDtypeStruct((CB * SLOTS, CW), BF),
        ],
        compiler_params=params(),
        name="experts",
    )(place, chunks, up, down, back)


def up_half(half, rows, pre_grad):
    def kernel(half_ref, x_ref, p_ref, o_ref):
        o_ref[...] = dot_tn(x_ref[0], p_ref[...]).astype(BF)

    return pl.pallas_call(
        kernel,
        grid_spec=pltpu.PrefetchScalarGridSpec(
            num_scalar_prefetch=1,
            grid=(CB,),
            in_specs=[
                pl.BlockSpec((1, SLOTS, CW), lambda c, _: (c, 0, 0)),
                pl.BlockSpec((SLOTS, HALF), lambda c, half_ref: (0, half_ref[0])),
            ],
            out_specs=pl.BlockSpec((CW, HALF), lambda c, _: (c, 0)),
        ),
        out_shape=jax.ShapeDtypeStruct((D, HALF), BF),
        compiler_params=params(),
        cost_estimate=pl.CostEstimate(
            flops=2 * SLOTS * D * HALF, bytes_accessed=6 << 20, transcendentals=0
        ),
        name="up_half",
    )(half, rows, pre_grad)


def down_sum(hidden, grads, hidden_far, grads_far):
    def kernel(h_ref, g_ref, hf_ref, gf_ref, o_ref):
        total = dot_tn(h_ref[...], g_ref[0]) + dot_tn(hf_ref[...], gf_ref[0])
        o_ref[...] = total.astype(BF)

    rows = pl.BlockSpec((1, SLOTS, CW), lambda c: (c, 0, 0))
    return pl.pallas_call(
        kernel,
        grid=(CB,),
        in_specs=[whole(SLOTS, HALF), rows, whole(SLOTS, HALF), rows],
        out_specs=pl.BlockSpec((HALF, CW), lambda c: (0, c)),
        out_shape=jax.ShapeDtypeStruct((HALF, D), BF),
        compiler_params=params(),
        cost_estimate=pl.CostEstimate(
            flops=4 * SLOTS * D * HALF, bytes_accessed=9 << 20, transcendentals=0
        ),
        name="down_sum",
    )(hidden, grads, hidden_far, grads_far)


def combine(chunks, stream, gate, target, weight):
    def kernel(i_ref, s_ref, gate_ref, tgt_ref, w_ref, o_ref, sc_ref):
        mix_in(i_ref, sc_ref)
        first, second = placing(tgt_ref, 0).astype(BF), placing(tgt_ref, 1).astype(BF)
        late = lax.broadcasted_iota(jnp.int32, (TOK, 1), 0) >= TOK // 2
        for c in range(CB):
            cut = slice(c * CW, (c + 1) * CW)
            mix = w_ref[:, 0:1] * dot_tn(first, sc_ref[c]) + w_ref[:, 1:2] * dot_tn(second, sc_ref[c])
            gates = jnp.where(late, gate_ref[1:2, cut], gate_ref[0:1, cut])
            o_ref[:, cut] = (s_ref[:, cut] + gates * mix).astype(BF)

    return pl.pallas_call(
        kernel,
        grid=(1,),
        in_specs=[whole(CB * SLOTS, CW), whole(TOK, D), whole(2, D), whole(2, TOK), whole(TOK, 2)],
        out_specs=whole(TOK, D),
        out_shape=jax.ShapeDtypeStruct((TOK, D), BF),
        scratch_shapes=[pltpu.VMEM((CB, SLOTS, CW), BF)],
        compiler_params=params(),
        name="combine",
    )(chunks, stream, gate, target, weight)


def plus(a, b):
    return (a.astype(F32) + b.astype(F32)).astype(BF)


def body(
    queries,
    keys,
    values,
    residual,
    out_weight,
    norm_gain,
    routes,
    route_weights,
    sample_flags,
    cond_gate,
    up_weight,
    down_weight,
    cotangent,
):
    z, core, dp = lax.axis_index("z"), lax.axis_index("core"), lax.axis_index("dp")
    place = jnp.stack([z, core, dp]).astype(jnp.int32)
    swap = [(0, 1), (1, 0)]
    above = [(i, (i + 1) % 4) for i in range(4)]
    below = [(i, (i + 3) % 4) for i in range(4)]
    exchange = functools.partial(lax.all_to_all, split_axis=0, concat_axis=0, tiled=True)

    ids = routes.reshape(2, TOK)
    earlier = jnp.arange(TOK)[:, None] > jnp.arange(TOK)[None, :]
    same = (ids[:, :, None] == ids[:, None, :]) & earlier[None]
    slot = jnp.sum(same.astype(jnp.int32), axis=2)
    row = ids * ROWS + slot * 2 + jnp.arange(2, dtype=jnp.int32)[:, None]
    target = row.reshape(TOK, 2).T
    weight_col = route_weights.reshape(TOK, 2)
    gate = jnp.where((sample_flags == 1)[:, None], cond_gate[1][None, :], cond_gate[0][None, :])

    rows = exchange(pack(queries, keys, values), SEQ)
    weight_other = lax.ppermute(out_weight, "core", swap)

    grad_chunks = send_grads(cotangent.reshape(TOK, D), gate, target, weight_col.T)
    rows, grad_chunks = lax.optimization_barrier((rows, grad_chunks))
    grad_arrived = exchange(grad_chunks, ALL)

    heads = attend(rows).reshape(16, 256, HEAD)
    heads, grad_arrived = lax.optimization_barrier((heads, grad_arrived))
    heads = exchange(heads, BACK).reshape(2, 4, 2, 4, 64, HEAD)
    grads, back = grads_in(grad_arrived, down_weight[0])
    grads_far = lax.ppermute(grads, "dp", swap)
    heads, grads, back = lax.optimization_barrier((heads, grads, back))
    fa, ua, da, own_a = project(place, 0, heads, out_weight, weight_other)
    fa = lax.ppermute(fa, "z", above)
    fb, ub, db, own_b = project(place, 1, heads, out_weight, weight_other)
    fb = lax.ppermute(fb, "z", below)
    ub = lax.ppermute(ub, "z", above)
    da = lax.ppermute(da, "z", below)
    ua = lax.ppermute(plus(ua, fa), "z", above)
    db = lax.ppermute(plus(db, fb), "z", below)
    stream, chunks = norm_send(
        own_a, own_b, ua, ub, da, db, residual.reshape(TOK, D), norm_gain[None], target
    )
    arrived = exchange(chunks, ALL)

    own_rows, hid_other, hid_own, pre_grad, products = experts(
        place, arrived, up_weight[0], down_weight[0], back
    )
    hid_far = lax.ppermute(hid_other, "dp", swap)
    returned = exchange(products, ALL)
    up_other = up_half((1 - dp)[None].astype(jnp.int32), own_rows, pre_grad)
    up_far = lax.ppermute(up_other, "dp", swap)
    up_own = up_half(dp[None].astype(jnp.int32), own_rows, pre_grad)
    down_total = down_sum(hid_own, grads, hid_far, grads_far)
    block_out = combine(returned, stream, gate, target, weight_col)
    up_total = plus(up_own, up_far)
    return (block_out.reshape(2, TOK // 2, D), up_total[None], down_total[None])


def solution(mesh):
    fine = Mesh(mesh.devices.reshape(2, 4, 2, 4, 2), ("dp", "x", "yl", "z", "core"))
    expert = ("z", "core")
    tokens = P("dp", ALL, None)
    placed = (
        P("dp", SEQ, expert),
        P("dp", SEQ, expert),
        P("dp", SEQ, expert),
        tokens,
        P(expert, None),
        P(),
        tokens,
        tokens,
        P("dp"),
        P(),
        P(ALL, None, None),
        P(ALL, None, None),
        tokens,
    )
    return jax.shard_map(
        body,
        mesh=fine,
        in_specs=placed,
        out_specs=(tokens, P(ALL, None, "dp"), P(ALL, "dp", None)),
        check_vma=False,
    )
```

```python
import functools

import jax
import jax.numpy as jnp
from jax import lax
from jax.experimental import pallas as pl
from jax.experimental.pallas import tpu as pltpu
from jax.sharding import Mesh
from jax.sharding import PartitionSpec as P

BF = jnp.bfloat16
F32 = jnp.float32
D = 4096
FF = 512
HEAD = 128
LENGTH = 4096
HALF = FF // 2
EXPERTS = 64
ROWS = 6
TOK = 128
SLOTS = EXPERTS * ROWS
CB = 4
CW = D // CB
GROUP = 8
GR = GROUP * ROWS
GRAD_WIDTHS = (CW, 2 * CW, CW)
GRAD_CUTS = ((0, slice(0, CW)), (1, slice(0, CW)), (1, slice(CW, 2 * CW)), (2, slice(0, CW)))
EXP_SCALE = HEAD**-0.5 * 1.4426950408889634
QB = 256
KB = 512
SEQ = ("x", "yl")
BACK = ("x", "yl", "core")
ALL = ("x", "yl", "z", "core")
VMEM_LIMIT = 56 * 1024 * 1024


def params(limit=VMEM_LIMIT):
    return pltpu.CompilerParams(vmem_limit_bytes=limit)


def whole(*shape):
    return pl.BlockSpec(shape, lambda *_: (0,) * len(shape))


def dot_nt(a, b):
    return lax.dot_general(a, b, (((1,), (1,)), ((), ())), preferred_element_type=F32)


def dot_tn(a, b):
    return lax.dot_general(a, b, (((0,), (0,)), ((), ())), preferred_element_type=F32)


def dot_nn(a, b):
    return jnp.dot(a, b, preferred_element_type=F32)


def pack(queries, keys, values):
    def kernel(q_ref, k_ref, v_ref, o_ref):
        for part, ref in enumerate((q_ref, k_ref, v_ref)):
            for h in range(4):
                o_ref[h, part] = ref[0, :, h * HEAD : (h + 1) * HEAD]

    spec = pl.BlockSpec((1, 256, 4 * HEAD), lambda b, t: (b, t, 0))
    return pl.pallas_call(
        kernel,
        grid=(2, 2),
        in_specs=[spec] * 3,
        out_specs=pl.BlockSpec((4, 3, 256, HEAD), lambda b, t: (b, 0, t, 0)),
        out_shape=jax.ShapeDtypeStruct((8, 3, 512, HEAD), BF),
        compiler_params=params(),
        name="pack_heads",
    )(queries, keys, values)


def lane_tiles(value):
    return [value[:, j : j + 128] for j in range(0, value.shape[1], 128)]


def attend(rows):
    pieces = [slice(i, i + KB) for i in range(0, LENGTH, KB)]

    def scores_of(q, k, s_ref):
        top = None
        for cut in pieces:
            s = dot_nt(q, k[cut])
            s_ref[:, cut] = s
            high = functools.reduce(jnp.maximum, lane_tiles(s))
            top = high if top is None else jnp.maximum(top, high)
        return jnp.max(top, axis=-1, keepdims=True)

    def step(q_next, k, s_next, s_now, top_now, v):
        top = None
        out = None
        for cut in pieces:
            s = dot_nt(q_next, k[cut])
            p = jnp.exp2((s_now[:, cut] - top_now) * EXP_SCALE).astype(BF)
            s_next[:, cut] = s
            high = functools.reduce(jnp.maximum, lane_tiles(s))
            top = high if top is None else jnp.maximum(top, high)
            wide = jnp.concatenate([v[cut], jnp.ones((KB, HEAD), BF)], axis=1)
            part = dot_nn(p, wide)
            out = part if out is None else out + part
        return jnp.max(top, axis=-1, keepdims=True), out[:, :HEAD] / out[:, HEAD:]

    def kernel(q_ref, qn_ref, k_ref, v_ref, o_ref, sa_ref, sb_ref, top_ref):
        k = k_ref[:, 0].reshape(LENGTH, HEAD)
        v = v_ref[:, 0].reshape(LENGTH, HEAD)

        @pl.when(pl.program_id(0) == 0)
        def _():
            top_ref[...] = jnp.broadcast_to(scores_of(q_ref[0, 0, :QB], k, sa_ref), (QB, 128))

        top_a = top_ref[:, :1]
        top_b, out_a = step(q_ref[0, 0, QB:], k, sb_ref, sa_ref, top_a, v)
        top_n, out_b = step(qn_ref[0, 0], k, sa_ref, sb_ref, top_b, v)
        top_ref[...] = jnp.broadcast_to(top_n, (QB, 128))
        for base, out in ((0, out_a), (4, out_b)):
            for t in range(QB // 64):
                j = base + t
                o_ref[0, j % 2, j // 2] = out[64 * t : 64 * t + 64].astype(BF)

    def following(i):
        j = jnp.minimum(2 * i + 2, LENGTH // QB - 1)
        return (j // 2, 0, j % 2, 0)

    return pl.pallas_call(
        kernel,
        grid=(8,),
        in_specs=[
            pl.BlockSpec((1, 1, 512, HEAD), lambda i: (i, 0, 0, 0)),
            pl.BlockSpec((1, 1, QB, HEAD), following),
            pl.BlockSpec((8, 1, 512, HEAD), lambda i: (0, 1, 0, 0)),
            pl.BlockSpec((8, 1, 512, HEAD), lambda i: (0, 2, 0, 0)),
        ],
        out_specs=pl.BlockSpec((1, 2, 4, 64, HEAD), lambda i: (i, 0, 0, 0, 0)),
        out_shape=jax.ShapeDtypeStruct((8, 2, 4, 64, HEAD), BF),
        scratch_shapes=[
            pltpu.VMEM((QB, LENGTH), F32),
            pltpu.VMEM((QB, LENGTH), F32),
            pltpu.VMEM((QB, 128), F32),
        ],
        compiler_params=params(),
        cost_estimate=pl.CostEstimate(
            flops=4 * LENGTH * LENGTH * 256, bytes_accessed=4 << 20, transcendentals=LENGTH * LENGTH
        ),
        name="attend",
    )(rows, rows, rows, rows)


def project(place, half, heads, weight_own, weight_other):
    width = 512
    blocks = D // 2 // width

    def kernel(place_ref, a_ref, wo_ref, ws_ref, *refs):
        lhs = refs[-1]
        core = place_ref[1]

        @pl.when(pl.program_id(0) == 0)
        def _():
            for side, c in enumerate((core, 1 - core)):
                for number, offset in enumerate((2, 1, 3, 0)):
                    z = lax.rem(place_ref[0] + offset, 4)
                    for b in range(2):
                        for h in range(4):
                            lhs[
                                number * TOK + b * 64 : number * TOK + (b + 1) * 64,
                                side * FF + h * HEAD : side * FF + (h + 1) * HEAD,
                            ] = a_ref[b, h, c, z]

        total = dot_nn(lhs[:, :FF], wo_ref[...]) + dot_nn(lhs[:, FF:], ws_ref[...])
        for number in range(4):
            refs[number][...] = total[number * TOK : (number + 1) * TOK].astype(BF)

    weights = pl.BlockSpec((FF, width), lambda n, _: (0, half * blocks + n))
    return pl.pallas_call(
        kernel,
        grid_spec=pltpu.PrefetchScalarGridSpec(
            num_scalar_prefetch=1,
            grid=(blocks,),
            in_specs=[whole(2, 4, 2, 4, 64, HEAD), weights, weights],
            out_specs=[pl.BlockSpec((TOK, width), lambda n, _: (0, n))] * 4,
            scratch_shapes=[pltpu.VMEM((4 * TOK, 2 * FF), BF)],
        ),
        out_shape=[jax.ShapeDtypeStruct((TOK, D // 2), BF)] * 4,
        compiler_params=params(),
        cost_estimate=pl.CostEstimate(
            flops=512 * 1024 * D, bytes_accessed=7 << 20, transcendentals=0
        ),
        name="project",
    )(place, heads, weight_own, weight_other)


def source_of(d):
    return lax.rem(d, CB * ROWS) // ROWS * GR + d // (CB * ROWS) * ROWS + lax.rem(d, ROWS)


def mixer():
    n = CB * GR
    d = lax.broadcasted_iota(jnp.int32, (n, n), 0)
    s = lax.broadcasted_iota(jnp.int32, (n, n), 1)
    return (s == source_of(d)).astype(BF)


def unmixer():
    n = CB * GR
    s = lax.broadcasted_iota(jnp.int32, (n, n), 0)
    d = lax.broadcasted_iota(jnp.int32, (n, n), 1)
    return (s == source_of(d)).astype(BF)


def mix_out(sc_ref, o_ref):
    mat = mixer()
    for g in range(EXPERTS // GROUP):
        stack = jnp.concatenate([sc_ref[c, g * GR : (g + 1) * GR, :] for c in range(CB)], axis=0)
        o_ref[g * CB * GR : (g + 1) * CB * GR, :] = dot_nn(mat, stack).astype(BF)


def mix_in(i_ref, sc_ref):
    mat = unmixer()
    for g in range(EXPERTS // GROUP):
        stack = dot_nn(mat, i_ref[g * CB * GR : (g + 1) * CB * GR, :]).astype(BF)
        for c in range(CB):
            sc_ref[c, g * GR : (g + 1) * GR, :] = stack[c * GR : (c + 1) * GR]


def placing(tgt_ref, k):
    slot = lax.broadcasted_iota(jnp.int32, (SLOTS, TOK), 0)
    return slot == tgt_ref[k : k + 1, :]


def send_grads(cotangent, gate, target, weight):
    def kernel(cot_ref, gate_ref, tgt_ref, w_ref, o_ref, sc_ref):
        first, second = placing(tgt_ref, 0), placing(tgt_ref, 1)
        both = (first | second).astype(BF)
        w = jnp.sum(
            jnp.where(first, w_ref[0:1, :], 0.0) + jnp.where(second, w_ref[1:2, :], 0.0),
            axis=1,
            keepdims=True,
        )
        odd = lax.rem(lax.broadcasted_iota(jnp.int32, (SLOTS, 1), 0), 2) == 1
        for c in range(CB):
            cut = slice(c * CW, (c + 1) * CW)
            rows = dot_nn(both, cot_ref[:, cut])
            gates = jnp.where(odd, gate_ref[1:2, cut], gate_ref[0:1, cut])
            sc_ref[c] = (w * gates * rows).astype(BF)
        mix_out(sc_ref, o_ref)

    return pl.pallas_call(
        kernel,
        grid=(1,),
        in_specs=[whole(TOK, D), whole(2, D), whole(2, TOK), whole(2, TOK)],
        out_specs=whole(CB * SLOTS, CW),
        out_shape=jax.ShapeDtypeStruct((CB * SLOTS, CW), BF),
        scratch_shapes=[pltpu.VMEM((CB, SLOTS, CW), BF)],
        compiler_params=params(),
        name="send_grads",
    )(cotangent, gate, target, weight)


def norm_send(own_a, own_b, up_a, up_b, down_a, down_b, residual, gain, target):
    def kernel(oa, ob, ua, ub, da, db, res_ref, gain_ref, tgt_ref, s_ref, o_ref, sc_ref):
        square = jnp.zeros((TOK, 1), F32)
        for half, own, first, second in ((0, oa, ua, da), (1, ob, ub, db)):
            cut = slice(half * D // 2, (half + 1) * D // 2)
            s = own[...].astype(F32) + first[...].astype(F32) + second[...].astype(F32)
            s = res_ref[:, cut].astype(F32) + s
            s_ref[:, cut] = s
            square += jnp.sum(s * s, axis=1, keepdims=True)
        factor = lax.rsqrt(square * (1.0 / D) + 1e-06)
        both = (placing(tgt_ref, 0) | placing(tgt_ref, 1)).astype(BF)
        for c in range(CB):
            cut = slice(c * CW, (c + 1) * CW)
            normed = (s_ref[:, cut] * factor * gain_ref[:, cut]).astype(BF)
            sc_ref[c] = dot_nn(both, normed).astype(BF)
        mix_out(sc_ref, o_ref)

    return pl.pallas_call(
        kernel,
        grid=(1,),
        in_specs=[whole(TOK, D // 2)] * 6
        + [whole(TOK, D), whole(1, D), whole(2, TOK)],
        out_specs=[whole(TOK, D), whole(CB * SLOTS, CW)],
        out_shape=[
            jax.ShapeDtypeStruct((TOK, D), F32),
            jax.ShapeDtypeStruct((CB * SLOTS, CW), BF),
        ],
        scratch_shapes=[pltpu.VMEM((CB, SLOTS, CW), BF)],
        compiler_params=params(),
        name="norm_send",
    )(own_a, own_b, up_a, up_b, down_a, down_b, residual, gain, target)


def grads_in(chunks, down):
    def kernel(i_ref, d_ref, *refs):
        b_ref, sc_ref = refs[-2:]
        mix_in(i_ref, sc_ref)
        back = None
        for c in range(CB):
            number, cut = GRAD_CUTS[c]
            refs[number][:, cut] = sc_ref[c]
            part = dot_nt(sc_ref[c], d_ref[:, c * CW : (c + 1) * CW])
            back = part if back is None else back + part
        b_ref[...] = back

    return pl.pallas_call(
        kernel,
        grid=(1,),
        in_specs=[whole(CB * SLOTS, CW), whole(FF, D)],
        out_specs=[whole(SLOTS, w) for w in GRAD_WIDTHS] + [whole(SLOTS, FF)],
        out_shape=[jax.ShapeDtypeStruct((SLOTS, w), BF) for w in GRAD_WIDTHS]
        + [jax.ShapeDtypeStruct((SLOTS, FF), F32)],
        scratch_shapes=[pltpu.VMEM((CB, SLOTS, CW), BF)],
        compiler_params=params(),
        name="grads_in",
    )(chunks, down)


def gelu_pair(pre):
    cdf_part = 0.5 * (1.0 + lax.erf(pre * 0.7071067811865476))
    density = jnp.exp(-0.5 * pre * pre) * 0.3989422804014327
    return (pre * cdf_part, cdf_part + pre * density)


def hidden_units(place, chunks, up, back):
    def kernel(place_ref, i_ref, up_ref, b_ref, x_ref, hid_ref, ho_ref, hs_ref, pg_ref, pre):
        i = pl.program_id(0)

        @pl.when(i == 0)
        def _():
            mix_in(i_ref, x_ref)
            pre[...] = dot_nn(x_ref[0], up_ref[...])

        @pl.when(i > 0)
        def _():
            pre[...] += dot_nn(x_ref[i], up_ref[...])

        @pl.when(i == CB - 1)
        def _():
            act, slope = gelu_pair(pre[...])
            hid_ref[...] = act.astype(BF)
            pg_ref[...] = (b_ref[...] * slope).astype(BF)
            low, high = act[:, :HALF].astype(BF), act[:, HALF:].astype(BF)
            mine = place_ref[2] == 0
            hs_ref[...] = jnp.where(mine, low, high)
            ho_ref[...] = jnp.where(mine, high, low)

    return pl.pallas_call(
        kernel,
        grid_spec=pltpu.PrefetchScalarGridSpec(
            num_scalar_prefetch=1,
            grid=(CB,),
            in_specs=[
                whole(CB * SLOTS, CW),
                pl.BlockSpec((CW, FF), lambda i, _: (i, 0)),
                whole(SLOTS, FF),
            ],
            out_specs=[
                whole(CB, SLOTS, CW),
                whole(SLOTS, FF),
                whole(SLOTS, HALF),
                whole(SLOTS, HALF),
                whole(SLOTS, FF),
            ],
            scratch_shapes=[pltpu.VMEM((SLOTS, FF), F32)],
        ),
        out_shape=[
            jax.ShapeDtypeStruct((CB, SLOTS, CW), BF),
            jax.ShapeDtypeStruct((SLOTS, FF), BF),
            jax.ShapeDtypeStruct((SLOTS, HALF), BF),
            jax.ShapeDtypeStruct((SLOTS, HALF), BF),
            jax.ShapeDtypeStruct((SLOTS, FF), BF),
        ],
        compiler_params=params(),
        name="hidden_units",
    )(place, chunks, up, back)


def expert_out(hidden, down):
    def kernel(h_ref, down_ref, o_ref, prod):
        i = pl.program_id(0)
        prod[i] = dot_nn(h_ref[...], down_ref[...]).astype(BF)

        @pl.when(i == CB - 1)
        def _():
            mix_out(prod, o_ref)

    return pl.pallas_call(
        kernel,
        grid=(CB,),
        in_specs=[whole(SLOTS, FF), pl.BlockSpec((FF, CW), lambda i: (0, i))],
        out_specs=whole(CB * SLOTS, CW),
        out_shape=jax.ShapeDtypeStruct((CB * SLOTS, CW), BF),
        scratch_shapes=[pltpu.VMEM((CB, SLOTS, CW), BF)],
        compiler_params=params(),
        name="expert_out",
    )(hidden, down)


def up_half(half, rows, pre_grad):
    def kernel(half_ref, x_ref, p_ref, o_ref):
        o_ref[...] = dot_tn(x_ref[0], p_ref[...]).astype(BF)

    return pl.pallas_call(
        kernel,
        grid_spec=pltpu.PrefetchScalarGridSpec(
            num_scalar_prefetch=1,
            grid=(CB,),
            in_specs=[
                pl.BlockSpec((1, SLOTS, CW), lambda c, _: (c, 0, 0)),
                pl.BlockSpec((SLOTS, HALF), lambda c, half_ref: (0, half_ref[0])),
            ],
            out_specs=pl.BlockSpec((CW, HALF), lambda c, _: (c, 0)),
        ),
        out_shape=jax.ShapeDtypeStruct((D, HALF), BF),
        compiler_params=params(),
        cost_estimate=pl.CostEstimate(
            flops=2 * SLOTS * D * HALF, bytes_accessed=6 << 20, transcendentals=0
        ),
        name="up_half",
    )(half, rows, pre_grad)


def down_sum(hidden, grads, hidden_far, grads_far):
    def kernel(h_ref, hf_ref, *refs):
        o_ref = refs[-1]
        for c in range(CB):
            number, cut = GRAD_CUTS[c]
            near, far = refs[number], refs[3 + number]
            total = dot_tn(h_ref[...], near[:, cut]) + dot_tn(hf_ref[...], far[:, cut])
            o_ref[:, c * CW : (c + 1) * CW] = total.astype(BF)

    return pl.pallas_call(
        kernel,
        grid=(1,),
        in_specs=[whole(SLOTS, HALF)] * 2 + [whole(SLOTS, w) for w in GRAD_WIDTHS] * 2,
        out_specs=whole(HALF, D),
        out_shape=jax.ShapeDtypeStruct((HALF, D), BF),
        compiler_params=params(),
        cost_estimate=pl.CostEstimate(
            flops=4 * SLOTS * D * HALF, bytes_accessed=9 << 20, transcendentals=0
        ),
        name="down_sum",
    )(hidden, hidden_far, *grads, *grads_far)


def combine(chunks, stream, gate, target, weight):
    def kernel(i_ref, s_ref, gate_ref, tgt_ref, w_ref, o_ref, sc_ref):
        mix_in(i_ref, sc_ref)
        first, second = placing(tgt_ref, 0).astype(BF), placing(tgt_ref, 1).astype(BF)
        late = lax.broadcasted_iota(jnp.int32, (TOK, 1), 0) >= TOK // 2
        for c in range(CB):
            cut = slice(c * CW, (c + 1) * CW)
            mix = w_ref[:, 0:1] * dot_tn(first, sc_ref[c]) + w_ref[:, 1:2] * dot_tn(second, sc_ref[c])
            gates = jnp.where(late, gate_ref[1:2, cut], gate_ref[0:1, cut])
            o_ref[:, cut] = (s_ref[:, cut] + gates * mix).astype(BF)

    return pl.pallas_call(
        kernel,
        grid=(1,),
        in_specs=[whole(CB * SLOTS, CW), whole(TOK, D), whole(2, D), whole(2, TOK), whole(TOK, 2)],
        out_specs=whole(TOK, D),
        out_shape=jax.ShapeDtypeStruct((TOK, D), BF),
        scratch_shapes=[pltpu.VMEM((CB, SLOTS, CW), BF)],
        compiler_params=params(),
        name="combine",
    )(chunks, stream, gate, target, weight)


def plus(a, b):
    return (a.astype(F32) + b.astype(F32)).astype(BF)


def body(
    queries,
    keys,
    values,
    residual,
    out_weight,
    norm_gain,
    routes,
    route_weights,
    sample_flags,
    cond_gate,
    up_weight,
    down_weight,
    cotangent,
):
    z, core, dp = lax.axis_index("z"), lax.axis_index("core"), lax.axis_index("dp")
    place = jnp.stack([z, core, dp]).astype(jnp.int32)
    swap = [(0, 1), (1, 0)]
    above = [(i, (i + 1) % 4) for i in range(4)]
    below = [(i, (i + 3) % 4) for i in range(4)]
    exchange = functools.partial(lax.all_to_all, split_axis=0, concat_axis=0, tiled=True)

    ids = routes.reshape(2, TOK)
    earlier = jnp.arange(TOK)[:, None] > jnp.arange(TOK)[None, :]
    same = (ids[:, :, None] == ids[:, None, :]) & earlier[None]
    slot = jnp.sum(same.astype(jnp.int32), axis=2)
    row = ids * ROWS + slot * 2 + jnp.arange(2, dtype=jnp.int32)[:, None]
    target = row.reshape(TOK, 2).T
    weight_col = route_weights.reshape(TOK, 2)
    gate = jnp.where((sample_flags == 1)[:, None], cond_gate[1][None, :], cond_gate[0][None, :])

    rows = exchange(pack(queries, keys, values), SEQ)
    weight_other = lax.ppermute(out_weight, "core", swap)

    grad_chunks = send_grads(cotangent.reshape(TOK, D), gate, target, weight_col.T)
    rows, grad_chunks = lax.optimization_barrier((rows, grad_chunks))
    grad_arrived = exchange(grad_chunks, ALL)

    heads = attend(rows).reshape(16, 256, HEAD)
    heads, grad_arrived = lax.optimization_barrier((heads, grad_arrived))
    heads = exchange(heads, BACK).reshape(2, 4, 2, 4, 64, HEAD)
    *grads, back = grads_in(grad_arrived, down_weight[0])
    heads, grads, back = lax.optimization_barrier((heads, grads, back))
    far_0, far_1, far_2 = [lax.ppermute(g, "dp", swap) for g in grads]
    fa, ua, da, own_a = project(place, 0, heads, out_weight, weight_other)
    fa = lax.ppermute(fa, "z", above)
    heads, far_0 = lax.optimization_barrier((heads, far_0))
    fb, ub, db, own_b = project(place, 1, heads, out_weight, weight_other)
    fb = lax.ppermute(fb, "z", below)
    ub = lax.ppermute(ub, "z", above)
    da = lax.ppermute(da, "z", below)
    ua = lax.ppermute(plus(ua, fa), "z", above)
    db = lax.ppermute(plus(db, fb), "z", below)
    own_a, ua, far_1 = lax.optimization_barrier((own_a, ua, far_1))
    stream, chunks = norm_send(
        own_a, own_b, ua, ub, da, db, residual.reshape(TOK, D), norm_gain[None], target
    )
    arrived = exchange(chunks, ALL)

    own_rows, hidden, hid_other, hid_own, pre_grad = hidden_units(place, arrived, up_weight[0], back)
    hid_far = lax.ppermute(hid_other, "dp", swap)
    returned = exchange(expert_out(hidden, down_weight[0]), ALL)
    own_rows, pre_grad, far_2 = lax.optimization_barrier((own_rows, pre_grad, far_2))
    up_other = up_half((1 - dp)[None].astype(jnp.int32), own_rows, pre_grad)
    up_other, hid_far = lax.optimization_barrier((up_other, hid_far))
    up_far = lax.ppermute(up_other, "dp", swap)
    up_own = up_half(dp[None].astype(jnp.int32), own_rows, pre_grad)
    down_total = down_sum(hid_own, grads, hid_far, (far_0, far_1, far_2))
    block_out = combine(returned, stream, gate, target, weight_col)
    up_total = plus(up_own, up_far)
    return (block_out.reshape(2, TOK // 2, D), up_total[None], down_total[None])


def solution(mesh):
    fine = Mesh(mesh.devices.reshape(2, 4, 2, 4, 2), ("dp", "x", "yl", "z", "core"))
    expert = ("z", "core")
    tokens = P("dp", ALL, None)
    placed = (
        P("dp", SEQ, expert),
        P("dp", SEQ, expert),
        P("dp", SEQ, expert),
        tokens,
        P(expert, None),
        P(),
        tokens,
        tokens,
        P("dp"),
        P(),
        P(ALL, None, None),
        P(ALL, None, None),
        tokens,
    )
    return jax.shard_map(
        body,
        mesh=fine,
        in_specs=placed,
        out_specs=(tokens, P(ALL, None, "dp"), P(ALL, "dp", None)),
        check_vma=False,
    )
```

```python
import functools

import jax
import jax.numpy as jnp
from jax import lax
from jax.experimental import pallas as pl
from jax.experimental.pallas import tpu as pltpu
from jax.sharding import Mesh
from jax.sharding import PartitionSpec as P

BF = jnp.bfloat16
F32 = jnp.float32
D = 4096
FF = 512
HEAD = 128
LENGTH = 4096
HALF = FF // 2
EXPERTS = 64
ROWS = 6
TOK = 128
SLOTS = EXPERTS * ROWS
CB = 4
CW = D // CB
GROUP = 8
GR = GROUP * ROWS
GRAD_WIDTHS = (CW, 2 * CW, CW)
GRAD_CUTS = ((0, slice(0, CW)), (1, slice(0, CW)), (1, slice(CW, 2 * CW)), (2, slice(0, CW)))
EXP_SCALE = HEAD**-0.5 * 1.4426950408889634
QB = 256
KB = 512
SEQ = ("x", "yl")
BACK = ("x", "yl", "core")
ALL = ("x", "yl", "z", "core")
VMEM_LIMIT = 24 * 1024 * 1024


def params(limit=VMEM_LIMIT):
    return pltpu.CompilerParams(vmem_limit_bytes=limit)


def cost(multiply_adds, transcendentals=0):
    return pl.CostEstimate(
        flops=2 * multiply_adds, bytes_accessed=1 << 20, transcendentals=transcendentals
    )


def resident(count):
    return [pl.BlockSpec(memory_space=pltpu.VMEM)] * count


def scalars():
    return pl.BlockSpec(memory_space=pltpu.SMEM)


def array(*shape, dtype=BF):
    return jax.ShapeDtypeStruct(shape, dtype)


def dot_nt(a, b):
    return lax.dot_general(a, b, (((1,), (1,)), ((), ())), preferred_element_type=F32)


def dot_tn(a, b):
    return lax.dot_general(a, b, (((0,), (0,)), ((), ())), preferred_element_type=F32)


def dot_nn(a, b):
    return jnp.dot(a, b, preferred_element_type=F32)


def pack(queries, keys, values):
    def kernel(q_ref, k_ref, v_ref, o_ref):
        for part, ref in enumerate((q_ref, k_ref, v_ref)):
            for h in range(4):
                o_ref[h, part] = ref[0, :, h * HEAD : (h + 1) * HEAD]

    spec = pl.BlockSpec((1, 256, 4 * HEAD), lambda b, t: (b, t, 0))
    return pl.pallas_call(
        kernel,
        grid=(2, 2),
        in_specs=[spec] * 3,
        out_specs=pl.BlockSpec((4, 3, 256, HEAD), lambda b, t: (b, 0, t, 0)),
        out_shape=jax.ShapeDtypeStruct((8, 3, 512, HEAD), BF),
        compiler_params=params(),
        name="pack_heads",
    )(queries, keys, values)


def lane_tiles(value):
    return [value[:, j : j + 128] for j in range(0, value.shape[1], 128)]


def attend(rows):
    pieces = [slice(i, i + KB) for i in range(0, LENGTH, KB)]

    def scores_of(q, k, s_ref):
        top = None
        for cut in pieces:
            s = dot_nt(q, k[cut])
            s_ref[:, cut] = s
            high = functools.reduce(jnp.maximum, lane_tiles(s))
            top = high if top is None else jnp.maximum(top, high)
        return jnp.max(top, axis=-1, keepdims=True)

    def step(q_next, k, s_next, s_now, top_now, v):
        top = None
        out = None
        for cut in pieces:
            s = dot_nt(q_next, k[cut])
            p = jnp.exp2((s_now[:, cut] - top_now) * EXP_SCALE).astype(BF)
            s_next[:, cut] = s
            high = functools.reduce(jnp.maximum, lane_tiles(s))
            top = high if top is None else jnp.maximum(top, high)
            wide = jnp.concatenate([v[cut], jnp.ones((KB, HEAD), BF)], axis=1)
            part = dot_nn(p, wide)
            out = part if out is None else out + part
        return jnp.max(top, axis=-1, keepdims=True), out[:, :HEAD] / out[:, HEAD:]

    def kernel(q_ref, qn_ref, k_ref, v_ref, o_ref, sa_ref, sb_ref, top_ref):
        k = k_ref[:, 0].reshape(LENGTH, HEAD)
        v = v_ref[:, 0].reshape(LENGTH, HEAD)

        @pl.when(pl.program_id(0) == 0)
        def _():
            top_ref[...] = jnp.broadcast_to(scores_of(q_ref[0, 0, :QB], k, sa_ref), (QB, 128))

        top_a = top_ref[:, :1]
        top_b, out_a = step(q_ref[0, 0, QB:], k, sb_ref, sa_ref, top_a, v)
        top_n, out_b = step(qn_ref[0, 0], k, sa_ref, sb_ref, top_b, v)
        top_ref[...] = jnp.broadcast_to(top_n, (QB, 128))
        for base, out in ((0, out_a), (4, out_b)):
            for t in range(QB // 64):
                j = base + t
                o_ref[0, j % 2, j // 2] = out[64 * t : 64 * t + 64].astype(BF)

    def following(i):
        j = jnp.minimum(2 * i + 2, LENGTH // QB - 1)
        return (j // 2, 0, j % 2, 0)

    return pl.pallas_call(
        kernel,
        grid=(8,),
        in_specs=[
            pl.BlockSpec((1, 1, 512, HEAD), lambda i: (i, 0, 0, 0)),
            pl.BlockSpec((1, 1, QB, HEAD), following),
            pl.BlockSpec((8, 1, 512, HEAD), lambda i: (0, 1, 0, 0)),
            pl.BlockSpec((8, 1, 512, HEAD), lambda i: (0, 2, 0, 0)),
        ],
        out_specs=pl.BlockSpec((1, 2, 4, 64, HEAD), lambda i: (i, 0, 0, 0, 0)),
        out_shape=jax.ShapeDtypeStruct((8, 2, 4, 64, HEAD), BF),
        scratch_shapes=[
            pltpu.VMEM((QB, LENGTH), F32),
            pltpu.VMEM((QB, LENGTH), F32),
            pltpu.VMEM((QB, 128), F32),
        ],
        compiler_params=params(),
        cost_estimate=pl.CostEstimate(
            flops=4 * LENGTH * LENGTH * 256, bytes_accessed=4 << 20, transcendentals=LENGTH * LENGTH
        ),
        name="attend",
    )(rows, rows, rows, rows)


def project(place, half, heads, weight_own, weight_other):
    width = 512

    def kernel(place_ref, a_ref, wo_ref, ws_ref, *refs):
        lhs = refs[-1]
        core = place_ref[1]
        for side, c in enumerate((core, 1 - core)):
            for number, offset in enumerate((2, 1, 3, 0)):
                z = lax.rem(place_ref[0] + offset, 4)
                for b in range(2):
                    for h in range(4):
                        lhs[
                            number * TOK + b * 64 : number * TOK + (b + 1) * 64,
                            side * FF + h * HEAD : side * FF + (h + 1) * HEAD,
                        ] = a_ref[b, h, c, z]

        @pl.loop(0, D // 2 // width)
        def _(n):
            near = pl.ds(pl.multiple_of(n * width, width), width)
            cut = pl.ds(pl.multiple_of(half * (D // 2) + n * width, width), width)
            total = dot_nn(lhs[:, :FF], wo_ref[:, cut]) + dot_nn(lhs[:, FF:], ws_ref[:, cut])
            for number in range(4):
                refs[number][:, near] = total[number * TOK : (number + 1) * TOK].astype(BF)

    return pl.pallas_call(
        kernel,
        in_specs=[scalars()] + resident(3),
        out_specs=resident(4),
        scratch_shapes=[pltpu.VMEM((4 * TOK, 2 * FF), BF)],
        out_shape=[array(TOK, D // 2)] * 4,
        compiler_params=params(),
        cost_estimate=cost(512 * 1024 * D // 2),
        name="project",
    )(place, heads, weight_own, weight_other)


def source_of(d):
    return lax.rem(d, CB * ROWS) // ROWS * GR + d // (CB * ROWS) * ROWS + lax.rem(d, ROWS)


def mixer():
    n = CB * GR
    d = lax.broadcasted_iota(jnp.int32, (n, n), 0)
    s = lax.broadcasted_iota(jnp.int32, (n, n), 1)
    return (s == source_of(d)).astype(BF)


def unmixer():
    n = CB * GR
    s = lax.broadcasted_iota(jnp.int32, (n, n), 0)
    d = lax.broadcasted_iota(jnp.int32, (n, n), 1)
    return (s == source_of(d)).astype(BF)


def mix_out(sc_ref, o_ref):
    mat = mixer()
    for g in range(EXPERTS // GROUP):
        stack = jnp.concatenate([sc_ref[c, g * GR : (g + 1) * GR, :] for c in range(CB)], axis=0)
        o_ref[g * CB * GR : (g + 1) * CB * GR, :] = dot_nn(mat, stack).astype(BF)


def mix_in(i_ref, sc_ref):
    mat = unmixer()
    for g in range(EXPERTS // GROUP):
        stack = dot_nn(mat, i_ref[g * CB * GR : (g + 1) * CB * GR, :]).astype(BF)
        for c in range(CB):
            sc_ref[c, g * GR : (g + 1) * GR, :] = stack[c * GR : (c + 1) * GR]


def placing(tgt_ref, k):
    slot = lax.broadcasted_iota(jnp.int32, (SLOTS, TOK), 0)
    return slot == tgt_ref[k : k + 1, :]


def send_grads(cotangent, gate, target, weight):
    def kernel(cot_ref, gate_ref, tgt_ref, w_ref, o_ref, sc_ref):
        first, second = placing(tgt_ref, 0), placing(tgt_ref, 1)
        both = (first | second).astype(BF)
        w = jnp.sum(
            jnp.where(first, w_ref[0:1, :], 0.0) + jnp.where(second, w_ref[1:2, :], 0.0),
            axis=1,
            keepdims=True,
        )
        odd = lax.rem(lax.broadcasted_iota(jnp.int32, (SLOTS, 1), 0), 2) == 1
        for c in range(CB):
            cut = slice(c * CW, (c + 1) * CW)
            rows = dot_nn(both, cot_ref[:, cut])
            gates = jnp.where(odd, gate_ref[1:2, cut], gate_ref[0:1, cut])
            sc_ref[c] = (w * gates * rows).astype(BF)
        mix_out(sc_ref, o_ref)

    return pl.pallas_call(
        kernel,
        in_specs=resident(4),
        out_specs=resident(1)[0],
        out_shape=jax.ShapeDtypeStruct((CB * SLOTS, CW), BF),
        scratch_shapes=[pltpu.VMEM((CB, SLOTS, CW), BF)],
        compiler_params=params(),
        name="send_grads",
    )(cotangent, gate, target, weight)


def norm_send(own_a, own_b, up_a, up_b, down_a, down_b, residual, gain, target):
    def kernel(oa, ob, ua, ub, da, db, res_ref, gain_ref, tgt_ref, s_ref, o_ref, sc_ref):
        square = jnp.zeros((TOK, 1), F32)
        for half, own, first, second in ((0, oa, ua, da), (1, ob, ub, db)):
            cut = slice(half * D // 2, (half + 1) * D // 2)
            s = own[...].astype(F32) + first[...].astype(F32) + second[...].astype(F32)
            s = res_ref[:, cut].astype(F32) + s
            s_ref[:, cut] = s
            square += jnp.sum(s * s, axis=1, keepdims=True)
        factor = lax.rsqrt(square * (1.0 / D) + 1e-06)
        both = (placing(tgt_ref, 0) | placing(tgt_ref, 1)).astype(BF)
        for c in range(CB):
            cut = slice(c * CW, (c + 1) * CW)
            normed = (s_ref[:, cut] * factor * gain_ref[:, cut]).astype(BF)
            sc_ref[c] = dot_nn(both, normed).astype(BF)
        mix_out(sc_ref, o_ref)

    return pl.pallas_call(
        kernel,
        in_specs=resident(9),
        out_specs=resident(2),
        out_shape=[
            jax.ShapeDtypeStruct((TOK, D), F32),
            jax.ShapeDtypeStruct((CB * SLOTS, CW), BF),
        ],
        scratch_shapes=[pltpu.VMEM((CB, SLOTS, CW), BF)],
        compiler_params=params(),
        name="norm_send",
    )(own_a, own_b, up_a, up_b, down_a, down_b, residual, gain, target)


def grads_in(chunks, down):
    def kernel(i_ref, d_ref, *refs):
        b_ref, sc_ref = refs[-2:]
        mix_in(i_ref, sc_ref)
        back = None
        for c in range(CB):
            number, cut = GRAD_CUTS[c]
            refs[number][:, cut] = sc_ref[c]
            part = dot_nt(sc_ref[c], d_ref[:, c * CW : (c + 1) * CW])
            back = part if back is None else back + part
        b_ref[...] = back

    return pl.pallas_call(
        kernel,
        in_specs=resident(2),
        out_specs=resident(4),
        out_shape=[jax.ShapeDtypeStruct((SLOTS, w), BF) for w in GRAD_WIDTHS]
        + [jax.ShapeDtypeStruct((SLOTS, FF), F32)],
        scratch_shapes=[pltpu.VMEM((CB, SLOTS, CW), BF)],
        compiler_params=params(),
        name="grads_in",
    )(chunks, down)


def gelu_pair(pre):
    cdf_part = 0.5 * (1.0 + lax.erf(pre * 0.7071067811865476))
    density = jnp.exp(-0.5 * pre * pre) * 0.3989422804014327
    return (pre * cdf_part, cdf_part + pre * density)


def hidden_units(place, chunks, up, back):
    def kernel(place_ref, i_ref, up_ref, b_ref, x_ref, hid_ref, ho_ref, hs_ref, po_ref, ps_ref):
        mix_in(i_ref, x_ref)
        pre = None
        for c in range(CB):
            part = dot_nn(x_ref[c], up_ref[c * CW : (c + 1) * CW, :])
            pre = part if pre is None else pre + part
        act, slope = gelu_pair(pre)
        hidden, grad = act.astype(BF), (b_ref[...] * slope).astype(BF)
        hid_ref[...] = hidden
        mine = place_ref[2] == 0
        for value, other, own in ((hidden, ho_ref, hs_ref), (grad, po_ref, ps_ref)):
            low, high = value[:, :HALF], value[:, HALF:]
            own[...] = jnp.where(mine, low, high)
            other[...] = jnp.where(mine, high, low)

    return pl.pallas_call(
        kernel,
        in_specs=[scalars()] + resident(3),
        out_specs=resident(6),
        out_shape=[array(CB, SLOTS, CW), array(SLOTS, FF)] + [array(SLOTS, HALF)] * 4,
        compiler_params=params(),
        cost_estimate=cost(SLOTS * D * FF, SLOTS * FF),
        name="hidden_units",
    )(place, chunks, up, back)


def expert_out(hidden, down):
    def kernel(h_ref, down_ref, o_ref, prod):
        for c in range(CB):
            prod[c] = dot_nn(h_ref[...], down_ref[:, c * CW : (c + 1) * CW]).astype(BF)
        mix_out(prod, o_ref)

    return pl.pallas_call(
        kernel,
        in_specs=resident(2),
        out_specs=resident(1)[0],
        out_shape=array(CB * SLOTS, CW),
        scratch_shapes=[pltpu.VMEM((CB, SLOTS, CW), BF)],
        compiler_params=params(),
        cost_estimate=cost(SLOTS * D * FF),
        name="expert_out",
    )(hidden, down)


def up_half(rows, pre_grad):
    def kernel(x_ref, p_ref, o_ref):
        for c in range(CB):
            o_ref[c * CW : (c + 1) * CW, :] = dot_tn(x_ref[c], p_ref[...]).astype(BF)

    return pl.pallas_call(
        kernel,
        in_specs=resident(2),
        out_specs=resident(1)[0],
        out_shape=array(D, HALF),
        compiler_params=params(),
        cost_estimate=cost(SLOTS * D * HALF),
        name="up_half",
    )(rows, pre_grad)


def down_sum(hidden, grads, hidden_far, grads_far):
    def kernel(h_ref, hf_ref, *refs):
        o_ref = refs[-1]
        for c in range(CB):
            number, cut = GRAD_CUTS[c]
            near, far = refs[number], refs[3 + number]
            total = dot_tn(h_ref[...], near[:, cut]) + dot_tn(hf_ref[...], far[:, cut])
            o_ref[:, c * CW : (c + 1) * CW] = total.astype(BF)

    return pl.pallas_call(
        kernel,
        in_specs=resident(8),
        out_specs=resident(1)[0],
        out_shape=array(HALF, D),
        compiler_params=params(),
        cost_estimate=cost(2 * SLOTS * D * HALF),
        name="down_sum",
    )(hidden, hidden_far, *grads, *grads_far)


def combine(chunks, stream, gate, target, weight):
    def kernel(i_ref, s_ref, gate_ref, tgt_ref, w_ref, o_ref, sc_ref):
        mix_in(i_ref, sc_ref)
        first, second = placing(tgt_ref, 0).astype(BF), placing(tgt_ref, 1).astype(BF)
        late = lax.broadcasted_iota(jnp.int32, (TOK, 1), 0) >= TOK // 2
        for c in range(CB):
            cut = slice(c * CW, (c + 1) * CW)
            mix = w_ref[:, 0:1] * dot_tn(first, sc_ref[c]) + w_ref[:, 1:2] * dot_tn(second, sc_ref[c])
            gates = jnp.where(late, gate_ref[1:2, cut], gate_ref[0:1, cut])
            o_ref[:, cut] = (s_ref[:, cut] + gates * mix).astype(BF)

    return pl.pallas_call(
        kernel,
        in_specs=resident(5),
        out_specs=resident(1)[0],
        out_shape=jax.ShapeDtypeStruct((TOK, D), BF),
        scratch_shapes=[pltpu.VMEM((CB, SLOTS, CW), BF)],
        compiler_params=params(),
        name="combine",
    )(chunks, stream, gate, target, weight)


def plus(a, b):
    return (a.astype(F32) + b.astype(F32)).astype(BF)


def body(
    queries,
    keys,
    values,
    residual,
    out_weight,
    norm_gain,
    routes,
    route_weights,
    sample_flags,
    cond_gate,
    up_weight,
    down_weight,
    cotangent,
):
    z, core, dp = lax.axis_index("z"), lax.axis_index("core"), lax.axis_index("dp")
    place = jnp.stack([z, core, dp]).astype(jnp.int32)
    swap = [(0, 1), (1, 0)]
    above = [(i, (i + 1) % 4) for i in range(4)]
    below = [(i, (i + 3) % 4) for i in range(4)]
    exchange = functools.partial(lax.all_to_all, split_axis=0, concat_axis=0, tiled=True)

    ids = routes.reshape(2, TOK)
    earlier = jnp.arange(TOK)[:, None] > jnp.arange(TOK)[None, :]
    same = (ids[:, :, None] == ids[:, None, :]) & earlier[None]
    slot = jnp.sum(same.astype(jnp.int32), axis=2)
    row = ids * ROWS + slot * 2 + jnp.arange(2, dtype=jnp.int32)[:, None]
    target = row.reshape(TOK, 2).T
    weight_col = route_weights.reshape(TOK, 2)
    gate = jnp.where((sample_flags == 1)[:, None], cond_gate[1][None, :], cond_gate[0][None, :])

    rows = exchange(pack(queries, keys, values), SEQ)
    weight_other = lax.ppermute(out_weight, "core", swap)

    grad_chunks = send_grads(cotangent.reshape(TOK, D), gate, target, weight_col.T)
    rows, grad_chunks = lax.optimization_barrier((rows, grad_chunks))
    grad_arrived = exchange(grad_chunks, ALL)

    heads = attend(rows).reshape(16, 256, HEAD)
    heads, grad_arrived = lax.optimization_barrier((heads, grad_arrived))
    heads = exchange(heads, BACK).reshape(2, 4, 2, 4, 64, HEAD)
    *grads, back = grads_in(grad_arrived, down_weight[0])
    heads, back = lax.optimization_barrier((heads, back))
    far_0, far_1, far_2 = [lax.ppermute(g, "dp", swap) for g in grads]
    fa, ua, da, own_a = project(place, 0, heads, out_weight, weight_other)
    fa = lax.ppermute(fa, "z", above)
    heads, far_0 = lax.optimization_barrier((heads, far_0))
    fb, ub, db, own_b = project(place, 1, heads, out_weight, weight_other)
    fb = lax.ppermute(fb, "z", below)
    ub = lax.ppermute(ub, "z", above)
    da = lax.ppermute(da, "z", below)
    ua = lax.ppermute(plus(ua, fa), "z", above)
    db = lax.ppermute(plus(db, fb), "z", below)
    own_a, ua, far_1 = lax.optimization_barrier((own_a, ua, far_1))
    stream, chunks = norm_send(
        own_a, own_b, ua, ub, da, db, residual.reshape(TOK, D), norm_gain[None], target
    )
    arrived = exchange(chunks, ALL)

    own_rows, hidden, hid_other, hid_own, pre_other, pre_own = hidden_units(
        place, arrived, up_weight[0], back
    )
    hid_other, far_2 = lax.optimization_barrier((hid_other, far_2))
    hid_far = lax.ppermute(hid_other, "dp", swap)
    returned = exchange(expert_out(hidden, down_weight[0]), ALL)
    pre_other, hid_far = lax.optimization_barrier((pre_other, hid_far))
    up_other = up_half(own_rows, pre_other)
    up_far = lax.ppermute(up_other, "dp", swap)
    up_own = up_half(own_rows, pre_own)
    down_total = down_sum(hid_own, grads, hid_far, (far_0, far_1, far_2))
    block_out = combine(returned, stream, gate, target, weight_col)
    block_out, up_far = lax.optimization_barrier((block_out, up_far))
    up_total = plus(up_own, up_far)
    return (block_out.reshape(2, TOK // 2, D), up_total[None], down_total[None])


def solution(mesh):
    fine = Mesh(mesh.devices.reshape(2, 4, 2, 4, 2), ("dp", "x", "yl", "z", "core"))
    expert = ("z", "core")
    tokens = P("dp", ALL, None)
    placed = (
        P("dp", SEQ, expert),
        P("dp", SEQ, expert),
        P("dp", SEQ, expert),
        tokens,
        P(expert, None),
        P(),
        tokens,
        tokens,
        P("dp"),
        P(),
        P(ALL, None, None),
        P(ALL, None, None),
        tokens,
    )
    return jax.shard_map(
        body,
        mesh=fine,
        in_specs=placed,
        out_specs=(tokens, P(ALL, None, "dp"), P(ALL, "dp", None)),
        check_vma=False,
    )
```

```python
import functools

import jax
import jax.numpy as jnp
from jax import lax
from jax.experimental import pallas as pl
from jax.experimental.pallas import tpu as pltpu
from jax.sharding import Mesh
from jax.sharding import PartitionSpec as P

BF = jnp.bfloat16
F32 = jnp.float32
D = 4096
FF = 512
HEAD = 128
LENGTH = 4096
HALF = FF // 2
EXPERTS = 64
ROWS = 6
TOK = 128
SLOTS = EXPERTS * ROWS
CB = 4
CW = D // CB
GROUP = 8
GR = GROUP * ROWS
GRAD_WIDTHS = (CW, 2 * CW, CW)
GRAD_CUTS = ((0, slice(0, CW)), (1, slice(0, CW)), (1, slice(CW, 2 * CW)), (2, slice(0, CW)))
EXP_SCALE = HEAD**-0.5 * 1.4426950408889634
QB = 256
KB = 512
SEQ = ("x", "yl")
BACK = ("x", "yl", "core")
ALL = ("x", "yl", "z", "core")
VMEM_LIMIT = 24 * 1024 * 1024


def params(limit=VMEM_LIMIT):
    return pltpu.CompilerParams(vmem_limit_bytes=limit)


def cost(multiply_adds, transcendentals=0, size=1 << 20):
    return pl.CostEstimate(
        flops=2 * multiply_adds, bytes_accessed=size, transcendentals=transcendentals
    )


def whole(*shape):
    return pl.BlockSpec(shape, lambda *_: (0,) * len(shape))


def resident(count):
    return [pl.BlockSpec(memory_space=pltpu.VMEM)] * count


def scalars():
    return pl.BlockSpec(memory_space=pltpu.SMEM)


def array(*shape, dtype=BF):
    return jax.ShapeDtypeStruct(shape, dtype)


def dot_nt(a, b):
    return lax.dot_general(a, b, (((1,), (1,)), ((), ())), preferred_element_type=F32)


def dot_tn(a, b):
    return lax.dot_general(a, b, (((0,), (0,)), ((), ())), preferred_element_type=F32)


def dot_nn(a, b):
    return jnp.dot(a, b, preferred_element_type=F32)


def pack(queries, keys, values):
    def kernel(q_ref, k_ref, v_ref, o_ref):
        for part, ref in enumerate((q_ref, k_ref, v_ref)):
            for h in range(4):
                o_ref[h, part] = ref[0, :, h * HEAD : (h + 1) * HEAD]

    spec = pl.BlockSpec((1, 256, 4 * HEAD), lambda b, t: (b, t, 0))
    return pl.pallas_call(
        kernel,
        grid=(2, 2),
        in_specs=[spec] * 3,
        out_specs=pl.BlockSpec((4, 3, 256, HEAD), lambda b, t: (b, 0, t, 0)),
        out_shape=jax.ShapeDtypeStruct((8, 3, 512, HEAD), BF),
        compiler_params=params(56 * 1024 * 1024),
        name="pack_heads",
    )(queries, keys, values)


def lane_tiles(value):
    return [value[:, j : j + 128] for j in range(0, value.shape[1], 128)]


def attend(rows):
    pieces = [slice(i, i + KB) for i in range(0, LENGTH, KB)]

    def scores_of(q, k, s_ref):
        top = None
        for cut in pieces:
            s = dot_nt(q, k[cut])
            s_ref[:, cut] = s
            high = functools.reduce(jnp.maximum, lane_tiles(s))
            top = high if top is None else jnp.maximum(top, high)
        return jnp.max(top, axis=-1, keepdims=True)

    def step(q_next, k, s_next, s_now, top_now, v):
        top = None
        out = None
        for cut in pieces:
            s = dot_nt(q_next, k[cut])
            p = jnp.exp2((s_now[:, cut] - top_now) * EXP_SCALE).astype(BF)
            s_next[:, cut] = s
            high = functools.reduce(jnp.maximum, lane_tiles(s))
            top = high if top is None else jnp.maximum(top, high)
            wide = jnp.concatenate([v[cut], jnp.ones((KB, HEAD), BF)], axis=1)
            part = dot_nn(p, wide)
            out = part if out is None else out + part
        return jnp.max(top, axis=-1, keepdims=True), out[:, :HEAD] / out[:, HEAD:]

    def kernel(q_ref, qn_ref, k_ref, v_ref, o_ref, sa_ref, sb_ref, top_ref):
        k = k_ref[:, 0].reshape(LENGTH, HEAD)
        v = v_ref[:, 0].reshape(LENGTH, HEAD)

        @pl.when(pl.program_id(0) == 0)
        def _():
            top_ref[...] = jnp.broadcast_to(scores_of(q_ref[0, 0, :QB], k, sa_ref), (QB, 128))

        top_a = top_ref[:, :1]
        top_b, out_a = step(q_ref[0, 0, QB:], k, sb_ref, sa_ref, top_a, v)
        top_n, out_b = step(qn_ref[0, 0], k, sa_ref, sb_ref, top_b, v)
        top_ref[...] = jnp.broadcast_to(top_n, (QB, 128))
        for base, out in ((0, out_a), (4, out_b)):
            for t in range(QB // 64):
                j = base + t
                o_ref[0, j % 2, j // 2] = out[64 * t : 64 * t + 64].astype(BF)

    def following(i):
        j = jnp.minimum(2 * i + 2, LENGTH // QB - 1)
        return (j // 2, 0, j % 2, 0)

    return pl.pallas_call(
        kernel,
        grid=(8,),
        in_specs=[
            pl.BlockSpec((1, 1, 512, HEAD), lambda i: (i, 0, 0, 0)),
            pl.BlockSpec((1, 1, QB, HEAD), following),
            pl.BlockSpec((8, 1, 512, HEAD), lambda i: (0, 1, 0, 0)),
            pl.BlockSpec((8, 1, 512, HEAD), lambda i: (0, 2, 0, 0)),
        ],
        out_specs=pl.BlockSpec((1, 2, 4, 64, HEAD), lambda i: (i, 0, 0, 0, 0)),
        out_shape=jax.ShapeDtypeStruct((8, 2, 4, 64, HEAD), BF),
        scratch_shapes=[
            pltpu.VMEM((QB, LENGTH), F32),
            pltpu.VMEM((QB, LENGTH), F32),
            pltpu.VMEM((QB, 128), F32),
        ],
        compiler_params=params(),
        cost_estimate=pl.CostEstimate(
            flops=4 * LENGTH * LENGTH * 256, bytes_accessed=4 << 20, transcendentals=LENGTH * LENGTH
        ),
        name="attend",
    )(rows, rows, rows, rows)


def project(place, offsets, splits, heads, weight_own, weight_other):
    width = 512
    rows = len(offsets) * TOK
    shapes = [array(TOK, D // n) for n in splits for _ in range(n)]

    def kernel(place_ref, a_ref, wo_ref, ws_ref, *refs):
        lhs = refs[-1]
        core = place_ref[1]
        for side, c in enumerate((core, 1 - core)):
            for number, offset in enumerate(offsets):
                z = lax.rem(place_ref[0] + offset, 4)
                for b in range(2):
                    for h in range(4):
                        lhs[
                            number * TOK + b * 64 : number * TOK + (b + 1) * 64,
                            side * FF + h * HEAD : side * FF + (h + 1) * HEAD,
                        ] = a_ref[b, h, c, z]

        for half in range(2):

            @pl.loop(0, D // 2 // width)
            def _(n, half=half):
                near = pl.ds(pl.multiple_of(n * width, width), width)
                cut = pl.ds(pl.multiple_of(half * (D // 2) + n * width, width), width)
                total = dot_nn(lhs[:, :FF], wo_ref[:, cut]) + dot_nn(lhs[:, FF:], ws_ref[:, cut])
                first = 0
                for number, pieces in enumerate(splits):
                    part = total[number * TOK : (number + 1) * TOK].astype(BF)
                    if pieces == 2:
                        refs[first + half][:, near] = part
                    else:
                        refs[first][:, cut] = part
                    first += pieces

    return pl.pallas_call(
        kernel,
        in_specs=[scalars()] + resident(3),
        out_specs=resident(len(shapes)),
        scratch_shapes=[pltpu.VMEM((rows, 2 * FF), BF)],
        out_shape=shapes,
        compiler_params=params(),
        cost_estimate=cost(rows * 1024 * D),
        name="project",
    )(place, heads, weight_own, weight_other)


def source_of(d):
    return lax.rem(d, CB * ROWS) // ROWS * GR + d // (CB * ROWS) * ROWS + lax.rem(d, ROWS)


def mixer():
    n = CB * GR
    d = lax.broadcasted_iota(jnp.int32, (n, n), 0)
    s = lax.broadcasted_iota(jnp.int32, (n, n), 1)
    return (s == source_of(d)).astype(BF)


def unmixer():
    n = CB * GR
    s = lax.broadcasted_iota(jnp.int32, (n, n), 0)
    d = lax.broadcasted_iota(jnp.int32, (n, n), 1)
    return (s == source_of(d)).astype(BF)


def mix_out(sc_ref, o_ref):
    mat = mixer()
    for g in range(EXPERTS // GROUP):
        stack = jnp.concatenate([sc_ref[c, g * GR : (g + 1) * GR, :] for c in range(CB)], axis=0)
        o_ref[g * CB * GR : (g + 1) * CB * GR, :] = dot_nn(mat, stack).astype(BF)


def mix_in(i_ref, sc_ref):
    mat = unmixer()
    for g in range(EXPERTS // GROUP):
        stack = dot_nn(mat, i_ref[g * CB * GR : (g + 1) * CB * GR, :]).astype(BF)
        for c in range(CB):
            sc_ref[c, g * GR : (g + 1) * GR, :] = stack[c * GR : (c + 1) * GR]


def placing(tgt_ref, k):
    slot = lax.broadcasted_iota(jnp.int32, (SLOTS, TOK), 0)
    return slot == tgt_ref[k : k + 1, :]


def send_grads(cotangent, gate, target, weight):
    def kernel(cot_ref, gate_ref, tgt_ref, w_ref, o_ref, sc_ref):
        first, second = placing(tgt_ref, 0), placing(tgt_ref, 1)
        both = (first | second).astype(BF)
        w = jnp.sum(
            jnp.where(first, w_ref[0:1, :], 0.0) + jnp.where(second, w_ref[1:2, :], 0.0),
            axis=1,
            keepdims=True,
        )
        odd = lax.rem(lax.broadcasted_iota(jnp.int32, (SLOTS, 1), 0), 2) == 1
        for c in range(CB):
            cut = slice(c * CW, (c + 1) * CW)
            rows = dot_nn(both, cot_ref[:, cut])
            gates = jnp.where(odd, gate_ref[1:2, cut], gate_ref[0:1, cut])
            sc_ref[c] = (w * gates * rows).astype(BF)
        mix_out(sc_ref, o_ref)

    return pl.pallas_call(
        kernel,
        in_specs=resident(4),
        out_specs=resident(1)[0],
        out_shape=jax.ShapeDtypeStruct((CB * SLOTS, CW), BF),
        scratch_shapes=[pltpu.VMEM((CB, SLOTS, CW), BF)],
        compiler_params=params(),
        name="send_grads",
    )(cotangent, gate, target, weight)


def norm_send(own, up_a, up_b, down_a, down_b, residual, gain, target):
    def kernel(own_ref, ua, ub, da, db, res_ref, gain_ref, tgt_ref, s_ref, o_ref, sc_ref):
        square = jnp.zeros((TOK, 1), F32)
        for half, first, second in ((0, ua, da), (1, ub, db)):
            cut = slice(half * D // 2, (half + 1) * D // 2)
            s = own_ref[:, cut].astype(F32) + first[...].astype(F32) + second[...].astype(F32)
            s = res_ref[:, cut].astype(F32) + s
            s_ref[:, cut] = s
            square += jnp.sum(s * s, axis=1, keepdims=True)
        factor = lax.rsqrt(square * (1.0 / D) + 1e-06)
        both = (placing(tgt_ref, 0) | placing(tgt_ref, 1)).astype(BF)
        for c in range(CB):
            cut = slice(c * CW, (c + 1) * CW)
            normed = (s_ref[:, cut] * factor * gain_ref[:, cut]).astype(BF)
            sc_ref[c] = dot_nn(both, normed).astype(BF)
        mix_out(sc_ref, o_ref)

    return pl.pallas_call(
        kernel,
        in_specs=resident(8),
        out_specs=resident(2),
        out_shape=[
            jax.ShapeDtypeStruct((TOK, D), F32),
            jax.ShapeDtypeStruct((CB * SLOTS, CW), BF),
        ],
        scratch_shapes=[pltpu.VMEM((CB, SLOTS, CW), BF)],
        compiler_params=params(),
        name="norm_send",
    )(own, up_a, up_b, down_a, down_b, residual, gain, target)


def grads_in(chunks, down):
    def kernel(i_ref, d_ref, *refs):
        b_ref, sc_ref = refs[-2:]
        mix_in(i_ref, sc_ref)
        back = None
        for c in range(CB):
            number, cut = GRAD_CUTS[c]
            refs[number][:, cut] = sc_ref[c]
            part = dot_nt(sc_ref[c], d_ref[:, c * CW : (c + 1) * CW])
            back = part if back is None else back + part
        b_ref[...] = back

    return pl.pallas_call(
        kernel,
        in_specs=resident(2),
        out_specs=resident(4),
        out_shape=[jax.ShapeDtypeStruct((SLOTS, w), BF) for w in GRAD_WIDTHS]
        + [jax.ShapeDtypeStruct((SLOTS, FF), F32)],
        scratch_shapes=[pltpu.VMEM((CB, SLOTS, CW), BF)],
        compiler_params=params(),
        name="grads_in",
    )(chunks, down)


def gelu_pair(pre):
    cdf_part = 0.5 * (1.0 + lax.erf(pre * 0.7071067811865476))
    density = jnp.exp(-0.5 * pre * pre) * 0.3989422804014327
    return (pre * cdf_part, cdf_part + pre * density)


def hidden_units(place, chunks, up, back):
    def kernel(place_ref, i_ref, up_ref, b_ref, x_ref, hid_ref, ho_ref, hs_ref, po_ref, ps_ref):
        mix_in(i_ref, x_ref)
        pre = None
        for c in range(CB):
            part = dot_nn(x_ref[c], up_ref[c * CW : (c + 1) * CW, :])
            pre = part if pre is None else pre + part
        act, slope = gelu_pair(pre)
        hidden, grad = act.astype(BF), (b_ref[...] * slope).astype(BF)
        hid_ref[...] = hidden
        mine = place_ref[2] == 0
        for value, other, own in ((hidden, ho_ref, hs_ref), (grad, po_ref, ps_ref)):
            low, high = value[:, :HALF], value[:, HALF:]
            own[...] = jnp.where(mine, low, high)
            other[...] = jnp.where(mine, high, low)

    return pl.pallas_call(
        kernel,
        in_specs=[scalars()] + resident(3),
        out_specs=resident(6),
        out_shape=[array(CB, SLOTS, CW), array(SLOTS, FF)] + [array(SLOTS, HALF)] * 4,
        compiler_params=params(),
        name="hidden_units",
    )(place, chunks, up, back)


def expert_out(hidden, down):
    def kernel(h_ref, down_ref, o_ref, prod):
        for c in range(CB):
            prod[c] = dot_nn(h_ref[...], down_ref[:, c * CW : (c + 1) * CW]).astype(BF)
        mix_out(prod, o_ref)

    return pl.pallas_call(
        kernel,
        in_specs=resident(2),
        out_specs=resident(1)[0],
        out_shape=array(CB * SLOTS, CW),
        scratch_shapes=[pltpu.VMEM((CB, SLOTS, CW), BF)],
        compiler_params=params(),
        name="expert_out",
    )(hidden, down)


def up_half(rows, pre_grad):
    def kernel(x_ref, p_ref, o_ref):
        for c in range(CB):
            o_ref[c * CW : (c + 1) * CW, :] = dot_tn(x_ref[c], p_ref[...]).astype(BF)

    return pl.pallas_call(
        kernel,
        in_specs=resident(2),
        out_specs=resident(1)[0],
        out_shape=array(D, HALF),
        compiler_params=params(),
        cost_estimate=cost(SLOTS * D * HALF, size=6 << 20),
        name="up_half",
    )(rows, pre_grad)


def up_sum(rows, pre_grad, far):
    def kernel(x_ref, p_ref, f_ref, o_ref):
        for c in range(CB):
            cut = slice(c * CW, (c + 1) * CW)
            o_ref[cut, :] = (dot_tn(x_ref[c], p_ref[...]) + f_ref[cut, :].astype(F32)).astype(BF)

    return pl.pallas_call(
        kernel,
        in_specs=resident(3),
        out_specs=resident(1)[0],
        out_shape=array(D, HALF),
        compiler_params=params(),
        cost_estimate=cost(SLOTS * D * HALF, size=6 << 20),
        name="up_sum",
    )(rows, pre_grad, far)


def down_sum(hidden, grads, hidden_far, grads_far):
    def kernel(h_ref, hf_ref, *refs):
        o_ref = refs[-1]
        for c in range(CB):
            number, cut = GRAD_CUTS[c]
            near, far = refs[number], refs[3 + number]
            total = dot_tn(h_ref[...], near[:, cut]) + dot_tn(hf_ref[...], far[:, cut])
            o_ref[:, c * CW : (c + 1) * CW] = total.astype(BF)

    return pl.pallas_call(
        kernel,
        in_specs=resident(8),
        out_specs=resident(1)[0],
        out_shape=array(HALF, D),
        compiler_params=params(),
        cost_estimate=cost(2 * SLOTS * D * HALF, size=9 << 20),
        name="down_sum",
    )(hidden, hidden_far, *grads, *grads_far)


def combine(chunks, stream, gate, target, weight):
    def kernel(i_ref, s_ref, gate_ref, tgt_ref, w_ref, o_ref, sc_ref):
        mix_in(i_ref, sc_ref)
        first, second = placing(tgt_ref, 0).astype(BF), placing(tgt_ref, 1).astype(BF)
        late = lax.broadcasted_iota(jnp.int32, (TOK, 1), 0) >= TOK // 2
        for c in range(CB):
            cut = slice(c * CW, (c + 1) * CW)
            mix = w_ref[:, 0:1] * dot_tn(first, sc_ref[c]) + w_ref[:, 1:2] * dot_tn(second, sc_ref[c])
            gates = jnp.where(late, gate_ref[1:2, cut], gate_ref[0:1, cut])
            o_ref[:, cut] = (s_ref[:, cut] + gates * mix).astype(BF)

    return pl.pallas_call(
        kernel,
        in_specs=resident(5),
        out_specs=resident(1)[0],
        out_shape=jax.ShapeDtypeStruct((TOK, D), BF),
        scratch_shapes=[pltpu.VMEM((CB, SLOTS, CW), BF)],
        compiler_params=params(),
        name="combine",
    )(chunks, stream, gate, target, weight)


def plus(a, b):
    return (a.astype(F32) + b.astype(F32)).astype(BF)


def body(
    queries,
    keys,
    values,
    residual,
    out_weight,
    norm_gain,
    routes,
    route_weights,
    sample_flags,
    cond_gate,
    up_weight,
    down_weight,
    cotangent,
):
    z, core, dp = lax.axis_index("z"), lax.axis_index("core"), lax.axis_index("dp")
    place = jnp.stack([z, core, dp]).astype(jnp.int32)
    swap = [(0, 1), (1, 0)]
    above = [(i, (i + 1) % 4) for i in range(4)]
    below = [(i, (i + 3) % 4) for i in range(4)]
    exchange = functools.partial(lax.all_to_all, split_axis=0, concat_axis=0, tiled=True)

    ids = routes.reshape(2, TOK)
    earlier = jnp.arange(TOK)[:, None] > jnp.arange(TOK)[None, :]
    same = (ids[:, :, None] == ids[:, None, :]) & earlier[None]
    slot = jnp.sum(same.astype(jnp.int32), axis=2)
    row = ids * ROWS + slot * 2 + jnp.arange(2, dtype=jnp.int32)[:, None]
    target = row.reshape(TOK, 2).T
    weight_col = route_weights.reshape(TOK, 2)
    gate = jnp.where((sample_flags == 1)[:, None], cond_gate[1][None, :], cond_gate[0][None, :])

    rows = exchange(pack(queries, keys, values), SEQ)
    weight_other = lax.ppermute(out_weight, "core", swap)

    grad_chunks = send_grads(cotangent.reshape(TOK, D), gate, target, weight_col.T)
    rows, grad_chunks = lax.optimization_barrier((rows, grad_chunks))
    grad_arrived = exchange(grad_chunks, ALL)

    heads = attend(rows).reshape(16, 256, HEAD)
    heads, grad_arrived = lax.optimization_barrier((heads, grad_arrived))
    heads = exchange(heads, BACK).reshape(2, 4, 2, 4, 64, HEAD)
    *grads, back = grads_in(grad_arrived, down_weight[0])
    heads, back = lax.optimization_barrier((heads, back))
    far_0, far_1, far_2 = [lax.ppermute(g, "dp", swap) for g in grads]
    fa, fb = project(place, (2,), (2,), heads, out_weight, weight_other)
    fa = lax.ppermute(fa, "z", above)
    fb = lax.ppermute(fb, "z", below)
    heads, far_0 = lax.optimization_barrier((heads, far_0))
    ua, ub, da, db, own = project(place, (1, 3, 0), (2, 2, 1), heads, out_weight, weight_other)
    ub = lax.ppermute(ub, "z", above)
    da = lax.ppermute(da, "z", below)
    ua = lax.ppermute(plus(ua, fa), "z", above)
    db = lax.ppermute(plus(db, fb), "z", below)
    own, ua, far_1 = lax.optimization_barrier((own, ua, far_1))
    stream, chunks = norm_send(
        own, ua, ub, da, db, residual.reshape(TOK, D), norm_gain[None], target
    )
    arrived = exchange(chunks, ALL)

    own_rows, hidden, hid_other, hid_own, pre_other, pre_own = hidden_units(
        place, arrived, up_weight[0], back
    )
    hid_far = lax.ppermute(hid_other, "dp", swap)
    hidden, far_2 = lax.optimization_barrier((hidden, far_2))
    returned = exchange(expert_out(hidden, down_weight[0]), ALL)
    up_other = up_half(own_rows, pre_other)
    up_far = lax.ppermute(up_other, "dp", swap)
    block_out = combine(returned, stream, gate, target, weight_col)
    up_own = up_half(own_rows, pre_own)
    block_out, hid_far = lax.optimization_barrier((block_out, hid_far))
    down_total = down_sum(hid_own, grads, hid_far, (far_0, far_1, far_2))
    up_total = plus(up_own, up_far)
    return (block_out.reshape(2, TOK // 2, D), up_total[None], down_total[None])


def solution(mesh):
    fine = Mesh(mesh.devices.reshape(2, 4, 2, 4, 2), ("dp", "x", "yl", "z", "core"))
    expert = ("z", "core")
    tokens = P("dp", ALL, None)
    placed = (
        P("dp", SEQ, expert),
        P("dp", SEQ, expert),
        P("dp", SEQ, expert),
        tokens,
        P(expert, None),
        P(),
        tokens,
        tokens,
        P("dp"),
        P(),
        P(ALL, None, None),
        P(ALL, None, None),
        tokens,
    )
    return jax.shard_map(
        body,
        mesh=fine,
        in_specs=placed,
        out_specs=(tokens, P(ALL, None, "dp"), P(ALL, "dp", None)),
        check_vma=False,
    )
```

```python
import functools

import jax
import jax.numpy as jnp
from jax import lax
from jax.experimental import pallas as pl
from jax.experimental.pallas import tpu as pltpu
from jax.sharding import Mesh
from jax.sharding import PartitionSpec as P

BF = jnp.bfloat16
F32 = jnp.float32
D = 4096
FF = 512
HEAD = 128
LENGTH = 4096
HALF = FF // 2
EXPERTS = 64
ROWS = 6
TOK = 128
SLOTS = EXPERTS * ROWS
CB = 4
CW = D // CB
GROUP = 8
GR = GROUP * ROWS
GRAD_WIDTHS = (CW, 2 * CW, CW)
GRAD_CUTS = ((0, slice(0, CW)), (1, slice(0, CW)), (1, slice(CW, 2 * CW)), (2, slice(0, CW)))
EXP_SCALE = HEAD**-0.5 * 1.4426950408889634
QB = 256
KB = 512
SEQ = ("x", "yl")
BACK = ("x", "yl", "core")
ALL = ("x", "yl", "z", "core")
VMEM_LIMIT = 24 * 1024 * 1024


def params(limit=VMEM_LIMIT):
    return pltpu.CompilerParams(vmem_limit_bytes=limit)


def cost(multiply_adds, transcendentals=0, size=1 << 20):
    return pl.CostEstimate(
        flops=2 * multiply_adds, bytes_accessed=size, transcendentals=transcendentals
    )


def whole(*shape):
    return pl.BlockSpec(shape, lambda *_: (0,) * len(shape))


def resident(count):
    return [pl.BlockSpec(memory_space=pltpu.VMEM)] * count


def in_hbm():
    return pl.BlockSpec(memory_space=pltpu.HBM)


def scalars():
    return pl.BlockSpec(memory_space=pltpu.SMEM)


def array(*shape, dtype=BF):
    return jax.ShapeDtypeStruct(shape, dtype)


def dot_nt(a, b):
    return lax.dot_general(a, b, (((1,), (1,)), ((), ())), preferred_element_type=F32)


def dot_tn(a, b):
    return lax.dot_general(a, b, (((0,), (0,)), ((), ())), preferred_element_type=F32)


def dot_nn(a, b):
    return jnp.dot(a, b, preferred_element_type=F32)


def pack(queries, keys, values):
    def kernel(q_ref, k_ref, v_ref, o_ref):
        for part, ref in enumerate((q_ref, k_ref, v_ref)):
            for h in range(4):
                o_ref[h, part] = ref[0, :, h * HEAD : (h + 1) * HEAD]

    spec = pl.BlockSpec((1, 256, 4 * HEAD), lambda b, t: (b, t, 0))
    return pl.pallas_call(
        kernel,
        grid=(2, 2),
        in_specs=[spec] * 3,
        out_specs=pl.BlockSpec((4, 3, 256, HEAD), lambda b, t: (b, 0, t, 0)),
        out_shape=jax.ShapeDtypeStruct((8, 3, 512, HEAD), BF),
        compiler_params=params(56 * 1024 * 1024),
        name="pack_heads",
    )(queries, keys, values)


def lane_tiles(value):
    return [value[:, j : j + 128] for j in range(0, value.shape[1], 128)]


def attend(rows):
    pieces = [slice(i, i + KB) for i in range(0, LENGTH, KB)]

    def scores_of(q, k, s_ref):
        top = None
        for cut in pieces:
            s = dot_nt(q, k[cut])
            s_ref[:, cut] = s
            high = functools.reduce(jnp.maximum, lane_tiles(s))
            top = high if top is None else jnp.maximum(top, high)
        return jnp.max(top, axis=-1, keepdims=True)

    def step(q_next, k, s_next, s_now, top_now, v):
        top = None
        out = None
        for cut in pieces:
            s = dot_nt(q_next, k[cut])
            p = jnp.exp2((s_now[:, cut] - top_now) * EXP_SCALE).astype(BF)
            s_next[:, cut] = s
            high = functools.reduce(jnp.maximum, lane_tiles(s))
            top = high if top is None else jnp.maximum(top, high)
            wide = jnp.concatenate([v[cut], jnp.ones((KB, HEAD), BF)], axis=1)
            part = dot_nn(p, wide)
            out = part if out is None else out + part
        return jnp.max(top, axis=-1, keepdims=True), out[:, :HEAD] / out[:, HEAD:]

    def kernel(q_ref, qn_ref, k_ref, v_ref, o_ref, sa_ref, sb_ref, top_ref):
        k = k_ref[:, 0].reshape(LENGTH, HEAD)
        v = v_ref[:, 0].reshape(LENGTH, HEAD)

        @pl.when(pl.program_id(0) == 0)
        def _():
            top_ref[...] = jnp.broadcast_to(scores_of(q_ref[0, 0, :QB], k, sa_ref), (QB, 128))

        top_a = top_ref[:, :1]
        top_b, out_a = step(q_ref[0, 0, QB:], k, sb_ref, sa_ref, top_a, v)
        top_n, out_b = step(qn_ref[0, 0], k, sa_ref, sb_ref, top_b, v)
        top_ref[...] = jnp.broadcast_to(top_n, (QB, 128))
        for base, out in ((0, out_a), (4, out_b)):
            for t in range(QB // 64):
                j = base + t
                o_ref[0, j % 2, j // 2] = out[64 * t : 64 * t + 64].astype(BF)

    def following(i):
        j = jnp.minimum(2 * i + 2, LENGTH // QB - 1)
        return (j // 2, 0, j % 2, 0)

    return pl.pallas_call(
        kernel,
        grid=(8,),
        in_specs=[
            pl.BlockSpec((1, 1, 512, HEAD), lambda i: (i, 0, 0, 0)),
            pl.BlockSpec((1, 1, QB, HEAD), following),
            pl.BlockSpec((8, 1, 512, HEAD), lambda i: (0, 1, 0, 0)),
            pl.BlockSpec((8, 1, 512, HEAD), lambda i: (0, 2, 0, 0)),
        ],
        out_specs=pl.BlockSpec((1, 2, 4, 64, HEAD), lambda i: (i, 0, 0, 0, 0)),
        out_shape=jax.ShapeDtypeStruct((8, 2, 4, 64, HEAD), BF),
        scratch_shapes=[
            pltpu.VMEM((QB, LENGTH), F32),
            pltpu.VMEM((QB, LENGTH), F32),
            pltpu.VMEM((QB, 128), F32),
        ],
        compiler_params=params(),
        cost_estimate=pl.CostEstimate(
            flops=4 * LENGTH * LENGTH * 256, bytes_accessed=4 << 20, transcendentals=LENGTH * LENGTH
        ),
        name="attend",
    )(rows, rows, rows, rows)


def project(place, offsets, splits, heads, weight_own, weight_other):
    width = 512
    rows = len(offsets) * TOK
    shapes = [array(TOK, D // n) for n in splits for _ in range(n)]

    def kernel(place_ref, a_ref, wo_ref, ws_ref, *refs):
        lhs = refs[-1]
        core = place_ref[1]
        for side, c in enumerate((core, 1 - core)):
            for number, offset in enumerate(offsets):
                z = lax.rem(place_ref[0] + offset, 4)
                for b in range(2):
                    for h in range(4):
                        lhs[
                            number * TOK + b * 64 : number * TOK + (b + 1) * 64,
                            side * FF + h * HEAD : side * FF + (h + 1) * HEAD,
                        ] = a_ref[b, h, c, z]

        for half in range(2):

            @pl.loop(0, D // 2 // width)
            def _(n, half=half):
                near = pl.ds(pl.multiple_of(n * width, width), width)
                cut = pl.ds(pl.multiple_of(half * (D // 2) + n * width, width), width)
                total = dot_nn(lhs[:, :FF], wo_ref[:, cut]) + dot_nn(lhs[:, FF:], ws_ref[:, cut])
                first = 0
                for number, pieces in enumerate(splits):
                    part = total[number * TOK : (number + 1) * TOK].astype(BF)
                    if pieces == 2:
                        refs[first + half][:, near] = part
                    else:
                        refs[first][:, cut] = part
                    first += pieces

    return pl.pallas_call(
        kernel,
        in_specs=[scalars()] + resident(3),
        out_specs=resident(len(shapes)),
        scratch_shapes=[pltpu.VMEM((rows, 2 * FF), BF)],
        out_shape=shapes,
        compiler_params=params(),
        cost_estimate=cost(rows * 1024 * D),
        name="project",
    )(place, heads, weight_own, weight_other)


def source_of(d):
    return lax.rem(d, CB * ROWS) // ROWS * GR + d // (CB * ROWS) * ROWS + lax.rem(d, ROWS)


def mixer():
    n = CB * GR
    d = lax.broadcasted_iota(jnp.int32, (n, n), 0)
    s = lax.broadcasted_iota(jnp.int32, (n, n), 1)
    return (s == source_of(d)).astype(BF)


def unmixer():
    n = CB * GR
    s = lax.broadcasted_iota(jnp.int32, (n, n), 0)
    d = lax.broadcasted_iota(jnp.int32, (n, n), 1)
    return (s == source_of(d)).astype(BF)


def mix_out(sc_ref, o_ref):
    mat = mixer()
    for g in range(EXPERTS // GROUP):
        stack = jnp.concatenate([sc_ref[c, g * GR : (g + 1) * GR, :] for c in range(CB)], axis=0)
        o_ref[g * CB * GR : (g + 1) * CB * GR, :] = dot_nn(mat, stack).astype(BF)


def mix_to(sc_ref, buf_ref, o_ref, sem, first):
    mat = mixer()
    copies = []
    for g in range(EXPERTS // GROUP):
        cut = slice(g * CB * GR, (g + 1) * CB * GR)
        stack = jnp.concatenate([sc_ref[c, g * GR : (g + 1) * GR, :] for c in range(CB)], axis=0)
        buf_ref[cut, :] = dot_nn(mat, stack).astype(BF)
        copies.append(pltpu.make_async_copy(buf_ref.at[cut], o_ref.at[cut], sem.at[first + g]))
        copies[-1].start()
    return copies


def mix_in(i_ref, sc_ref):
    mat = unmixer()
    for g in range(EXPERTS // GROUP):
        stack = dot_nn(mat, i_ref[g * CB * GR : (g + 1) * CB * GR, :]).astype(BF)
        for c in range(CB):
            sc_ref[c, g * GR : (g + 1) * GR, :] = stack[c * GR : (c + 1) * GR]


def placing(tgt_ref, k):
    slot = lax.broadcasted_iota(jnp.int32, (SLOTS, TOK), 0)
    return slot == tgt_ref[k : k + 1, :]


def send_grads(cotangent, gate, target, weight):
    def kernel(cot_ref, gate_ref, tgt_ref, w_ref, o_ref, sc_ref):
        first, second = placing(tgt_ref, 0), placing(tgt_ref, 1)
        both = (first | second).astype(BF)
        w = jnp.sum(
            jnp.where(first, w_ref[0:1, :], 0.0) + jnp.where(second, w_ref[1:2, :], 0.0),
            axis=1,
            keepdims=True,
        )
        odd = lax.rem(lax.broadcasted_iota(jnp.int32, (SLOTS, 1), 0), 2) == 1
        for c in range(CB):
            cut = slice(c * CW, (c + 1) * CW)
            rows = dot_nn(both, cot_ref[:, cut])
            gates = jnp.where(odd, gate_ref[1:2, cut], gate_ref[0:1, cut])
            sc_ref[c] = (w * gates * rows).astype(BF)
        mix_out(sc_ref, o_ref)

    return pl.pallas_call(
        kernel,
        in_specs=resident(4),
        out_specs=resident(1)[0],
        out_shape=jax.ShapeDtypeStruct((CB * SLOTS, CW), BF),
        scratch_shapes=[pltpu.VMEM((CB, SLOTS, CW), BF)],
        compiler_params=params(),
        name="send_grads",
    )(cotangent, gate, target, weight)


def norm_send(own, up_a, up_b, down_a, down_b, residual, gain, target):
    def kernel(own_ref, ua, ub, da, db, res_ref, gain_ref, tgt_ref, so_ref, o_ref, sc_ref, s_ref, buf_ref, sem):
        square = jnp.zeros((TOK, 1), F32)
        for half, first, second in ((0, ua, da), (1, ub, db)):
            cut = slice(half * D // 2, (half + 1) * D // 2)
            s = own_ref[:, cut].astype(F32) + first[...].astype(F32) + second[...].astype(F32)
            s = res_ref[:, cut].astype(F32) + s
            s_ref[:, cut] = s
            square += jnp.sum(s * s, axis=1, keepdims=True)
        kept = pltpu.make_async_copy(s_ref, so_ref, sem.at[0])
        kept.start()
        factor = lax.rsqrt(square * (1.0 / D) + 1e-06)
        both = (placing(tgt_ref, 0) | placing(tgt_ref, 1)).astype(BF)
        for c in range(CB):
            cut = slice(c * CW, (c + 1) * CW)
            normed = (s_ref[:, cut] * factor * gain_ref[:, cut]).astype(BF)
            sc_ref[c] = dot_nn(both, normed).astype(BF)
        for copy in [kept] + mix_to(sc_ref, buf_ref, o_ref, sem, 1):
            copy.wait()

    return pl.pallas_call(
        kernel,
        in_specs=resident(8),
        out_specs=[in_hbm(), in_hbm()],
        out_shape=[
            jax.ShapeDtypeStruct((TOK, D), F32),
            jax.ShapeDtypeStruct((CB * SLOTS, CW), BF),
        ],
        scratch_shapes=[
            pltpu.VMEM((CB, SLOTS, CW), BF),
            pltpu.VMEM((TOK, D), F32),
            pltpu.VMEM((CB * SLOTS, CW), BF),
            pltpu.SemaphoreType.DMA((1 + EXPERTS // GROUP,)),
        ],
        compiler_params=params(),
        name="norm_send",
    )(own, up_a, up_b, down_a, down_b, residual, gain, target)


def grads_in(chunks, down):
    def kernel(i_ref, d_ref, *refs):
        b_ref, sc_ref = refs[-2:]
        mix_in(i_ref, sc_ref)
        back = None
        for c in range(CB):
            number, cut = GRAD_CUTS[c]
            refs[number][:, cut] = sc_ref[c]
            part = dot_nt(sc_ref[c], d_ref[:, c * CW : (c + 1) * CW])
            back = part if back is None else back + part
        b_ref[...] = back

    return pl.pallas_call(
        kernel,
        in_specs=resident(2),
        out_specs=resident(4),
        out_shape=[jax.ShapeDtypeStruct((SLOTS, w), BF) for w in GRAD_WIDTHS]
        + [jax.ShapeDtypeStruct((SLOTS, FF), F32)],
        scratch_shapes=[pltpu.VMEM((CB, SLOTS, CW), BF)],
        compiler_params=params(),
        name="grads_in",
    )(chunks, down)


def gelu_pair(pre):
    cdf_part = 0.5 * (1.0 + lax.erf(pre * 0.7071067811865476))
    density = jnp.exp(-0.5 * pre * pre) * 0.3989422804014327
    return (pre * cdf_part, cdf_part + pre * density)


def hidden_units(place, chunks, up, back):
    def kernel(
        place_ref, i_ref, up_hbm, b_ref, x_ref, hid_ref, ho_ref, hs_ref, po_ref, ps_ref, up_ref, sem
    ):
        cuts = [slice(c * CW, (c + 1) * CW) for c in range(CB)]
        copies = [
            pltpu.make_async_copy(up_hbm.at[cut], up_ref.at[cut], sem.at[c])
            for c, cut in enumerate(cuts)
        ]
        for copy in copies:
            copy.start()
        mix_in(i_ref, x_ref)
        pre = None
        for c in range(CB):
            copies[c].wait()
            part = dot_nn(x_ref[c], up_ref[cuts[c], :])
            pre = part if pre is None else pre + part
        act, slope = gelu_pair(pre)
        hidden, grad = act.astype(BF), (b_ref[...] * slope).astype(BF)
        hid_ref[...] = hidden
        mine = place_ref[2] == 0
        for value, other, own in ((hidden, ho_ref, hs_ref), (grad, po_ref, ps_ref)):
            low, high = value[:, :HALF], value[:, HALF:]
            own[...] = jnp.where(mine, low, high)
            other[...] = jnp.where(mine, high, low)

    return pl.pallas_call(
        kernel,
        in_specs=[scalars()] + resident(1) + [in_hbm()] + resident(1),
        out_specs=resident(6),
        scratch_shapes=[pltpu.VMEM((D, FF), BF), pltpu.SemaphoreType.DMA((CB,))],
        out_shape=[array(CB, SLOTS, CW), array(SLOTS, FF)] + [array(SLOTS, HALF)] * 4,
        compiler_params=params(),
        name="hidden_units",
    )(place, chunks, up, back)


def expert_out(hidden, down):
    def kernel(h_ref, down_ref, o_ref, prod, buf_ref, sem):
        for c in range(CB):
            prod[c] = dot_nn(h_ref[...], down_ref[:, c * CW : (c + 1) * CW]).astype(BF)
        for copy in mix_to(prod, buf_ref, o_ref, sem, 0):
            copy.wait()

    return pl.pallas_call(
        kernel,
        in_specs=resident(2),
        out_specs=in_hbm(),
        out_shape=array(CB * SLOTS, CW),
        scratch_shapes=[
            pltpu.VMEM((CB, SLOTS, CW), BF),
            pltpu.VMEM((CB * SLOTS, CW), BF),
            pltpu.SemaphoreType.DMA((EXPERTS // GROUP,)),
        ],
        compiler_params=params(),
        name="expert_out",
    )(hidden, down)


def up_half(rows, pre_grad):
    def kernel(x_ref, p_ref, o_ref):
        for c in range(CB):
            o_ref[c * CW : (c + 1) * CW, :] = dot_tn(x_ref[c], p_ref[...]).astype(BF)

    return pl.pallas_call(
        kernel,
        in_specs=resident(2),
        out_specs=resident(1)[0],
        out_shape=array(D, HALF),
        compiler_params=params(),
        cost_estimate=cost(SLOTS * D * HALF, size=6 << 20),
        name="up_half",
    )(rows, pre_grad)


def up_sum(rows, pre_grad, far):
    def kernel(x_ref, p_ref, f_ref, o_ref):
        for c in range(CB):
            cut = slice(c * CW, (c + 1) * CW)
            o_ref[cut, :] = (dot_tn(x_ref[c], p_ref[...]) + f_ref[cut, :].astype(F32)).astype(BF)

    return pl.pallas_call(
        kernel,
        in_specs=resident(3),
        out_specs=resident(1)[0],
        out_shape=array(D, HALF),
        compiler_params=params(),
        cost_estimate=cost(SLOTS * D * HALF, size=6 << 20),
        name="up_sum",
    )(rows, pre_grad, far)


def down_sum(hidden, grads, hidden_far, grads_far):
    def kernel(h_ref, hf_ref, *refs):
        o_ref = refs[-1]
        for c in range(CB):
            number, cut = GRAD_CUTS[c]
            near, far = refs[number], refs[3 + number]
            total = dot_tn(h_ref[...], near[:, cut]) + dot_tn(hf_ref[...], far[:, cut])
            o_ref[:, c * CW : (c + 1) * CW] = total.astype(BF)

    return pl.pallas_call(
        kernel,
        in_specs=resident(8),
        out_specs=resident(1)[0],
        out_shape=array(HALF, D),
        compiler_params=params(),
        cost_estimate=cost(2 * SLOTS * D * HALF, size=9 << 20),
        name="down_sum",
    )(hidden, hidden_far, *grads, *grads_far)


def combine(chunks, stream, gate, target, weight):
    def kernel(i_ref, s_ref, gate_ref, tgt_ref, w_ref, o_ref, sc_ref):
        mix_in(i_ref, sc_ref)
        first, second = placing(tgt_ref, 0).astype(BF), placing(tgt_ref, 1).astype(BF)
        late = lax.broadcasted_iota(jnp.int32, (TOK, 1), 0) >= TOK // 2
        for c in range(CB):
            cut = slice(c * CW, (c + 1) * CW)
            mix = w_ref[:, 0:1] * dot_tn(first, sc_ref[c]) + w_ref[:, 1:2] * dot_tn(second, sc_ref[c])
            gates = jnp.where(late, gate_ref[1:2, cut], gate_ref[0:1, cut])
            o_ref[:, cut] = (s_ref[:, cut] + gates * mix).astype(BF)

    return pl.pallas_call(
        kernel,
        in_specs=resident(5),
        out_specs=resident(1)[0],
        out_shape=jax.ShapeDtypeStruct((TOK, D), BF),
        scratch_shapes=[pltpu.VMEM((CB, SLOTS, CW), BF)],
        compiler_params=params(),
        name="combine",
    )(chunks, stream, gate, target, weight)


def plus(a, b):
    return (a.astype(F32) + b.astype(F32)).astype(BF)


def body(
    queries,
    keys,
    values,
    residual,
    out_weight,
    norm_gain,
    routes,
    route_weights,
    sample_flags,
    cond_gate,
    up_weight,
    down_weight,
    cotangent,
):
    z, core, dp = lax.axis_index("z"), lax.axis_index("core"), lax.axis_index("dp")
    place = jnp.stack([z, core, dp]).astype(jnp.int32)
    swap = [(0, 1), (1, 0)]
    above = [(i, (i + 1) % 4) for i in range(4)]
    below = [(i, (i + 3) % 4) for i in range(4)]
    exchange = functools.partial(lax.all_to_all, split_axis=0, concat_axis=0, tiled=True)

    ids = routes.reshape(2, TOK)
    earlier = jnp.arange(TOK)[:, None] > jnp.arange(TOK)[None, :]
    same = (ids[:, :, None] == ids[:, None, :]) & earlier[None]
    slot = jnp.sum(same.astype(jnp.int32), axis=2)
    row = ids * ROWS + slot * 2 + jnp.arange(2, dtype=jnp.int32)[:, None]
    target = row.reshape(TOK, 2).T
    weight_col = route_weights.reshape(TOK, 2)
    gate = jnp.where((sample_flags == 1)[:, None], cond_gate[1][None, :], cond_gate[0][None, :])

    rows = exchange(pack(queries, keys, values), SEQ)
    weight_other = lax.ppermute(out_weight, "core", swap)

    grad_chunks = send_grads(cotangent.reshape(TOK, D), gate, target, weight_col.T)
    rows, grad_chunks = lax.optimization_barrier((rows, grad_chunks))
    grad_arrived = exchange(grad_chunks, ALL)

    heads = attend(rows).reshape(16, 256, HEAD)
    heads, grad_arrived = lax.optimization_barrier((heads, grad_arrived))
    heads = exchange(heads, BACK).reshape(2, 4, 2, 4, 64, HEAD)
    *grads, back = grads_in(grad_arrived, down_weight[0])
    heads, back = lax.optimization_barrier((heads, back))
    far_0, far_1, far_2 = [lax.ppermute(g, "dp", swap) for g in grads]
    fa, fb = project(place, (2,), (2,), heads, out_weight, weight_other)
    fa = lax.ppermute(fa, "z", above)
    fb = lax.ppermute(fb, "z", below)
    heads, far_0 = lax.optimization_barrier((heads, far_0))
    ua, ub, da, db, own = project(place, (1, 3, 0), (2, 2, 1), heads, out_weight, weight_other)
    ub = lax.ppermute(ub, "z", above)
    da = lax.ppermute(da, "z", below)
    ua = lax.ppermute(plus(ua, fa), "z", above)
    db = lax.ppermute(plus(db, fb), "z", below)
    own, ua, far_1 = lax.optimization_barrier((own, ua, far_1))
    stream, chunks = norm_send(
        own, ua, ub, da, db, residual.reshape(TOK, D), norm_gain[None], target
    )
    arrived = exchange(chunks, ALL)

    own_rows, hidden, hid_other, hid_own, pre_other, pre_own = hidden_units(
        place, arrived, up_weight[0], back
    )
    hid_far = lax.ppermute(hid_other, "dp", swap)
    hidden, far_2, hid_far = lax.optimization_barrier((hidden, far_2, hid_far))
    returned = exchange(expert_out(hidden, down_weight[0]), ALL)
    up_other = up_half(own_rows, pre_other)
    up_far = lax.ppermute(up_other, "dp", swap)
    block_out = combine(returned, stream, gate, target, weight_col)
    up_own = up_half(own_rows, pre_own)
    down_total = down_sum(hid_own, grads, hid_far, (far_0, far_1, far_2))
    up_total = plus(up_own, up_far)
    return (block_out.reshape(2, TOK // 2, D), up_total[None], down_total[None])


def solution(mesh):
    fine = Mesh(mesh.devices.reshape(2, 4, 2, 4, 2), ("dp", "x", "yl", "z", "core"))
    expert = ("z", "core")
    tokens = P("dp", ALL, None)
    placed = (
        P("dp", SEQ, expert),
        P("dp", SEQ, expert),
        P("dp", SEQ, expert),
        tokens,
        P(expert, None),
        P(),
        tokens,
        tokens,
        P("dp"),
        P(),
        P(ALL, None, None),
        P(ALL, None, None),
        tokens,
    )
    return jax.shard_map(
        body,
        mesh=fine,
        in_specs=placed,
        out_specs=(tokens, P(ALL, None, "dp"), P(ALL, "dp", None)),
        check_vma=False,
    )
```

```python
import functools

import jax
import jax.numpy as jnp
from jax import lax
from jax.experimental import pallas as pl
from jax.experimental.pallas import tpu as pltpu
from jax.sharding import Mesh
from jax.sharding import PartitionSpec as P

BF = jnp.bfloat16
F32 = jnp.float32
D = 4096
FF = 512
HEAD = 128
LENGTH = 4096
HALF = FF // 2
EXPERTS = 64
ROWS = 6
TOK = 128
SLOTS = EXPERTS * ROWS
CB = 4
CW = D // CB
GROUP = 8
GR = GROUP * ROWS
GRAD_WIDTHS = (CW, 2 * CW, CW)
GRAD_CUTS = ((0, slice(0, CW)), (1, slice(0, CW)), (1, slice(CW, 2 * CW)), (2, slice(0, CW)))
EXP_SCALE = HEAD**-0.5 * 1.4426950408889634
QB = 256
KB = 512
SEQ = ("x", "yl")
BACK = ("x", "yl", "core")
ALL = ("x", "yl", "z", "core")
VMEM_LIMIT = 24 * 1024 * 1024


def params(limit=VMEM_LIMIT):
    return pltpu.CompilerParams(vmem_limit_bytes=limit)


def cost(multiply_adds, transcendentals=0, size=1 << 20):
    return pl.CostEstimate(
        flops=2 * multiply_adds, bytes_accessed=size, transcendentals=transcendentals
    )


def whole(*shape):
    return pl.BlockSpec(shape, lambda *_: (0,) * len(shape))


def resident(count):
    return [pl.BlockSpec(memory_space=pltpu.VMEM)] * count


def scalars():
    return pl.BlockSpec(memory_space=pltpu.SMEM)


def array(*shape, dtype=BF):
    return jax.ShapeDtypeStruct(shape, dtype)


def dot_nt(a, b):
    return lax.dot_general(a, b, (((1,), (1,)), ((), ())), preferred_element_type=F32)


def dot_tn(a, b):
    return lax.dot_general(a, b, (((0,), (0,)), ((), ())), preferred_element_type=F32)


def dot_nn(a, b):
    return jnp.dot(a, b, preferred_element_type=F32)


def pack(queries, keys, values):
    def kernel(q_ref, k_ref, v_ref, o_ref):
        for part, ref in enumerate((q_ref, k_ref, v_ref)):
            for h in range(4):
                o_ref[h, part] = ref[0, :, h * HEAD : (h + 1) * HEAD]

    spec = pl.BlockSpec((1, 256, 4 * HEAD), lambda b, t: (b, t, 0))
    return pl.pallas_call(
        kernel,
        grid=(2, 2),
        in_specs=[spec] * 3,
        out_specs=pl.BlockSpec((4, 3, 256, HEAD), lambda b, t: (b, 0, t, 0)),
        out_shape=jax.ShapeDtypeStruct((8, 3, 512, HEAD), BF),
        compiler_params=params(56 * 1024 * 1024),
        name="pack_heads",
    )(queries, keys, values)


def lane_tiles(value):
    return [value[:, j : j + 128] for j in range(0, value.shape[1], 128)]


def attend(rows):
    pieces = [slice(i, i + KB) for i in range(0, LENGTH, KB)]

    def scores_of(q, k, s_ref):
        top = None
        for cut in pieces:
            s = dot_nt(q, k[cut])
            s_ref[:, cut] = s
            high = functools.reduce(jnp.maximum, lane_tiles(s))
            top = high if top is None else jnp.maximum(top, high)
        return jnp.max(top, axis=-1, keepdims=True)

    def step(q_next, k, s_next, s_now, top_now, v):
        top = None
        out = None
        for cut in pieces:
            s = dot_nt(q_next, k[cut])
            p = jnp.exp2((s_now[:, cut] - top_now) * EXP_SCALE).astype(BF)
            s_next[:, cut] = s
            high = functools.reduce(jnp.maximum, lane_tiles(s))
            top = high if top is None else jnp.maximum(top, high)
            wide = jnp.concatenate([v[cut], jnp.ones((KB, HEAD), BF)], axis=1)
            part = dot_nn(p, wide)
            out = part if out is None else out + part
        return jnp.max(top, axis=-1, keepdims=True), out[:, :HEAD] / out[:, HEAD:]

    def kernel(q_ref, qn_ref, k_ref, v_ref, o_ref, sa_ref, sb_ref, top_ref):
        k = k_ref[:, 0].reshape(LENGTH, HEAD)
        v = v_ref[:, 0].reshape(LENGTH, HEAD)

        @pl.when(pl.program_id(0) == 0)
        def _():
            top_ref[...] = jnp.broadcast_to(scores_of(q_ref[0, 0, :QB], k, sa_ref), (QB, 128))

        top_a = top_ref[:, :1]
        top_b, out_a = step(q_ref[0, 0, QB:], k, sb_ref, sa_ref, top_a, v)
        top_n, out_b = step(qn_ref[0, 0], k, sa_ref, sb_ref, top_b, v)
        top_ref[...] = jnp.broadcast_to(top_n, (QB, 128))
        for base, out in ((0, out_a), (4, out_b)):
            for t in range(QB // 64):
                j = base + t
                o_ref[0, j % 2, j // 2] = out[64 * t : 64 * t + 64].astype(BF)

    def following(i):
        j = jnp.minimum(2 * i + 2, LENGTH // QB - 1)
        return (j // 2, 0, j % 2, 0)

    return pl.pallas_call(
        kernel,
        grid=(8,),
        in_specs=[
            pl.BlockSpec((1, 1, 512, HEAD), lambda i: (i, 0, 0, 0)),
            pl.BlockSpec((1, 1, QB, HEAD), following),
            pl.BlockSpec((8, 1, 512, HEAD), lambda i: (0, 1, 0, 0)),
            pl.BlockSpec((8, 1, 512, HEAD), lambda i: (0, 2, 0, 0)),
        ],
        out_specs=pl.BlockSpec((1, 2, 4, 64, HEAD), lambda i: (i, 0, 0, 0, 0)),
        out_shape=jax.ShapeDtypeStruct((8, 2, 4, 64, HEAD), BF),
        scratch_shapes=[
            pltpu.VMEM((QB, LENGTH), F32),
            pltpu.VMEM((QB, LENGTH), F32),
            pltpu.VMEM((QB, 128), F32),
        ],
        compiler_params=params(),
        cost_estimate=pl.CostEstimate(
            flops=4 * LENGTH * LENGTH * 256, bytes_accessed=4 << 20, transcendentals=LENGTH * LENGTH
        ),
        name="attend",
    )(rows, rows, rows, rows)


def project(place, offsets, splits, heads, weight_own, weight_other):
    width = 512
    rows = len(offsets) * TOK
    shapes = [array(TOK, D // n) for n in splits for _ in range(n)]

    def kernel(place_ref, a_ref, wo_ref, ws_ref, *refs):
        lhs = refs[-1]
        core = place_ref[1]
        for side, c in enumerate((core, 1 - core)):
            for number, offset in enumerate(offsets):
                z = lax.rem(place_ref[0] + offset, 4)
                for b in range(2):
                    for h in range(4):
                        lhs[
                            number * TOK + b * 64 : number * TOK + (b + 1) * 64,
                            side * FF + h * HEAD : side * FF + (h + 1) * HEAD,
                        ] = a_ref[b, h, c, z]

        for half in range(2):

            @pl.loop(0, D // 2 // width)
            def _(n, half=half):
                near = pl.ds(pl.multiple_of(n * width, width), width)
                cut = pl.ds(pl.multiple_of(half * (D // 2) + n * width, width), width)
                total = dot_nn(lhs[:, :FF], wo_ref[:, cut]) + dot_nn(lhs[:, FF:], ws_ref[:, cut])
                first = 0
                for number, pieces in enumerate(splits):
                    part = total[number * TOK : (number + 1) * TOK].astype(BF)
                    if pieces == 2:
                        refs[first + half][:, near] = part
                    else:
                        refs[first][:, cut] = part
                    first += pieces

    return pl.pallas_call(
        kernel,
        in_specs=[scalars()] + resident(3),
        out_specs=resident(len(shapes)),
        scratch_shapes=[pltpu.VMEM((rows, 2 * FF), BF)],
        out_shape=shapes,
        compiler_params=params(),
        cost_estimate=cost(rows * 1024 * D),
        name="project",
    )(place, heads, weight_own, weight_other)


def source_of(d):
    return lax.rem(d, CB * ROWS) // ROWS * GR + d // (CB * ROWS) * ROWS + lax.rem(d, ROWS)


def mixer():
    n = CB * GR
    d = lax.broadcasted_iota(jnp.int32, (n, n), 0)
    s = lax.broadcasted_iota(jnp.int32, (n, n), 1)
    return (s == source_of(d)).astype(BF)


def unmixer():
    n = CB * GR
    s = lax.broadcasted_iota(jnp.int32, (n, n), 0)
    d = lax.broadcasted_iota(jnp.int32, (n, n), 1)
    return (s == source_of(d)).astype(BF)


def mix_out(sc_ref, o_ref):
    mat = mixer()
    for g in range(EXPERTS // GROUP):
        stack = jnp.concatenate([sc_ref[c, g * GR : (g + 1) * GR, :] for c in range(CB)], axis=0)
        o_ref[g * CB * GR : (g + 1) * CB * GR, :] = dot_nn(mat, stack).astype(BF)


def mix_in(i_ref, sc_ref):
    mat = unmixer()
    for g in range(EXPERTS // GROUP):
        stack = dot_nn(mat, i_ref[g * CB * GR : (g + 1) * CB * GR, :]).astype(BF)
        for c in range(CB):
            sc_ref[c, g * GR : (g + 1) * GR, :] = stack[c * GR : (c + 1) * GR]


def placing(tgt_ref, k):
    slot = lax.broadcasted_iota(jnp.int32, (SLOTS, TOK), 0)
    return slot == tgt_ref[k : k + 1, :]


def send_grads(cotangent, gate, target, weight):
    def kernel(cot_ref, gate_ref, tgt_ref, w_ref, o_ref, sc_ref):
        first, second = placing(tgt_ref, 0), placing(tgt_ref, 1)
        both = (first | second).astype(BF)
        w = jnp.sum(
            jnp.where(first, w_ref[0:1, :], 0.0) + jnp.where(second, w_ref[1:2, :], 0.0),
            axis=1,
            keepdims=True,
        )
        odd = lax.rem(lax.broadcasted_iota(jnp.int32, (SLOTS, 1), 0), 2) == 1
        for c in range(CB):
            cut = slice(c * CW, (c + 1) * CW)
            rows = dot_nn(both, cot_ref[:, cut])
            gates = jnp.where(odd, gate_ref[1:2, cut], gate_ref[0:1, cut])
            sc_ref[c] = (w * gates * rows).astype(BF)
        mix_out(sc_ref, o_ref)

    return pl.pallas_call(
        kernel,
        in_specs=resident(4),
        out_specs=resident(1)[0],
        out_shape=jax.ShapeDtypeStruct((CB * SLOTS, CW), BF),
        scratch_shapes=[pltpu.VMEM((CB, SLOTS, CW), BF)],
        compiler_params=params(),
        name="send_grads",
    )(cotangent, gate, target, weight)


def norm_send(own, up_a, up_b, down_a, down_b, residual, gain, target):
    def kernel(own_ref, ua, ub, da, db, res_ref, gain_ref, tgt_ref, s_ref, o_ref, sc_ref):
        square = jnp.zeros((TOK, 1), F32)
        for half, first, second in ((0, ua, da), (1, ub, db)):
            cut = slice(half * D // 2, (half + 1) * D // 2)
            s = own_ref[:, cut].astype(F32) + first[...].astype(F32) + second[...].astype(F32)
            s = res_ref[:, cut].astype(F32) + s
            s_ref[:, cut] = s
            square += jnp.sum(s * s, axis=1, keepdims=True)
        factor = lax.rsqrt(square * (1.0 / D) + 1e-06)
        both = (placing(tgt_ref, 0) | placing(tgt_ref, 1)).astype(BF)
        for c in range(CB):
            cut = slice(c * CW, (c + 1) * CW)
            normed = (s_ref[:, cut] * factor * gain_ref[:, cut]).astype(BF)
            sc_ref[c] = dot_nn(both, normed).astype(BF)
        mix_out(sc_ref, o_ref)

    return pl.pallas_call(
        kernel,
        in_specs=resident(8),
        out_specs=resident(2),
        out_shape=[
            jax.ShapeDtypeStruct((TOK, D), F32),
            jax.ShapeDtypeStruct((CB * SLOTS, CW), BF),
        ],
        scratch_shapes=[pltpu.VMEM((CB, SLOTS, CW), BF)],
        compiler_params=params(),
        name="norm_send",
    )(own, up_a, up_b, down_a, down_b, residual, gain, target)


def grads_in(chunks, down):
    def kernel(i_ref, d_ref, *refs):
        b_ref, sc_ref = refs[-2:]
        mix_in(i_ref, sc_ref)
        back = None
        for c in range(CB):
            number, cut = GRAD_CUTS[c]
            refs[number][:, cut] = sc_ref[c]
            part = dot_nt(sc_ref[c], d_ref[:, c * CW : (c + 1) * CW])
            back = part if back is None else back + part
        b_ref[...] = back

    return pl.pallas_call(
        kernel,
        in_specs=resident(2),
        out_specs=resident(4),
        out_shape=[jax.ShapeDtypeStruct((SLOTS, w), BF) for w in GRAD_WIDTHS]
        + [jax.ShapeDtypeStruct((SLOTS, FF), F32)],
        scratch_shapes=[pltpu.VMEM((CB, SLOTS, CW), BF)],
        compiler_params=params(),
        name="grads_in",
    )(chunks, down)


def gelu_pair(pre):
    cdf_part = 0.5 * (1.0 + lax.erf(pre * 0.7071067811865476))
    density = jnp.exp(-0.5 * pre * pre) * 0.3989422804014327
    return (pre * cdf_part, cdf_part + pre * density)


def hidden_units(place, chunks, up, back):
    def kernel(place_ref, i_ref, up_ref, b_ref, x_ref, hid_ref, ho_ref, hs_ref, po_ref, ps_ref):
        mix_in(i_ref, x_ref)
        pre = None
        for c in range(CB):
            part = dot_nn(x_ref[c], up_ref[c * CW : (c + 1) * CW, :])
            pre = part if pre is None else pre + part
        act, slope = gelu_pair(pre)
        hidden, grad = act.astype(BF), (b_ref[...] * slope).astype(BF)
        hid_ref[...] = hidden
        mine = place_ref[2] == 0
        for value, other, own in ((hidden, ho_ref, hs_ref), (grad, po_ref, ps_ref)):
            low, high = value[:, :HALF], value[:, HALF:]
            own[...] = jnp.where(mine, low, high)
            other[...] = jnp.where(mine, high, low)

    return pl.pallas_call(
        kernel,
        in_specs=[scalars()] + resident(3),
        out_specs=resident(6),
        out_shape=[array(CB, SLOTS, CW), array(SLOTS, FF)] + [array(SLOTS, HALF)] * 4,
        compiler_params=params(),
        name="hidden_units",
    )(place, chunks, up, back)


def expert_out(hidden, down):
    def kernel(h_ref, down_ref, o_ref, prod):
        for c in range(CB):
            prod[c] = dot_nn(h_ref[...], down_ref[:, c * CW : (c + 1) * CW]).astype(BF)
        mix_out(prod, o_ref)

    return pl.pallas_call(
        kernel,
        in_specs=resident(2),
        out_specs=resident(1)[0],
        out_shape=array(CB * SLOTS, CW),
        scratch_shapes=[pltpu.VMEM((CB, SLOTS, CW), BF)],
        compiler_params=params(),
        name="expert_out",
    )(hidden, down)


def up_half(rows, pre_grad):
    def kernel(x_ref, p_ref, o_ref):
        for c in range(CB):
            o_ref[c * CW : (c + 1) * CW, :] = dot_tn(x_ref[c], p_ref[...]).astype(BF)

    return pl.pallas_call(
        kernel,
        in_specs=resident(2),
        out_specs=resident(1)[0],
        out_shape=array(D, HALF),
        compiler_params=params(),
        cost_estimate=cost(SLOTS * D * HALF, size=6 << 20),
        name="up_half",
    )(rows, pre_grad)


def up_sum(rows, pre_grad, far):
    def kernel(x_ref, p_ref, f_ref, o_ref):
        for c in range(CB):
            cut = slice(c * CW, (c + 1) * CW)
            o_ref[cut, :] = (dot_tn(x_ref[c], p_ref[...]) + f_ref[cut, :].astype(F32)).astype(BF)

    return pl.pallas_call(
        kernel,
        in_specs=resident(3),
        out_specs=resident(1)[0],
        out_shape=array(D, HALF),
        compiler_params=params(),
        cost_estimate=cost(SLOTS * D * HALF, size=6 << 20),
        name="up_sum",
    )(rows, pre_grad, far)


def down_sum(hidden, grads, hidden_far, grads_far):
    def kernel(h_ref, hf_ref, *refs):
        o_ref = refs[-1]
        for c in range(CB):
            number, cut = GRAD_CUTS[c]
            near, far = refs[number], refs[3 + number]
            total = dot_tn(h_ref[...], near[:, cut]) + dot_tn(hf_ref[...], far[:, cut])
            o_ref[:, c * CW : (c + 1) * CW] = total.astype(BF)

    return pl.pallas_call(
        kernel,
        in_specs=resident(8),
        out_specs=resident(1)[0],
        out_shape=array(HALF, D),
        compiler_params=params(),
        cost_estimate=cost(2 * SLOTS * D * HALF, size=9 << 20),
        name="down_sum",
    )(hidden, hidden_far, *grads, *grads_far)


def combine(chunks, stream, gate, target, weight):
    def kernel(i_ref, s_ref, gate_ref, tgt_ref, w_ref, o_ref, sc_ref):
        mix_in(i_ref, sc_ref)
        first, second = placing(tgt_ref, 0).astype(BF), placing(tgt_ref, 1).astype(BF)
        late = lax.broadcasted_iota(jnp.int32, (TOK, 1), 0) >= TOK // 2
        for c in range(CB):
            cut = slice(c * CW, (c + 1) * CW)
            mix = w_ref[:, 0:1] * dot_tn(first, sc_ref[c]) + w_ref[:, 1:2] * dot_tn(second, sc_ref[c])
            gates = jnp.where(late, gate_ref[1:2, cut], gate_ref[0:1, cut])
            o_ref[:, cut] = (s_ref[:, cut] + gates * mix).astype(BF)

    return pl.pallas_call(
        kernel,
        in_specs=resident(5),
        out_specs=resident(1)[0],
        out_shape=jax.ShapeDtypeStruct((TOK, D), BF),
        scratch_shapes=[pltpu.VMEM((CB, SLOTS, CW), BF)],
        compiler_params=params(),
        name="combine",
    )(chunks, stream, gate, target, weight)


def plus(a, b):
    return (a.astype(F32) + b.astype(F32)).astype(BF)


def body(
    queries,
    keys,
    values,
    residual,
    out_weight,
    norm_gain,
    routes,
    route_weights,
    sample_flags,
    cond_gate,
    up_weight,
    down_weight,
    cotangent,
):
    z, core, dp = lax.axis_index("z"), lax.axis_index("core"), lax.axis_index("dp")
    place = jnp.stack([z, core, dp]).astype(jnp.int32)
    swap = [(0, 1), (1, 0)]
    above = [(i, (i + 1) % 4) for i in range(4)]
    below = [(i, (i + 3) % 4) for i in range(4)]
    exchange = functools.partial(lax.all_to_all, split_axis=0, concat_axis=0, tiled=True)

    ids = routes.reshape(2, TOK)
    earlier = jnp.arange(TOK)[:, None] > jnp.arange(TOK)[None, :]
    same = (ids[:, :, None] == ids[:, None, :]) & earlier[None]
    slot = jnp.sum(same.astype(jnp.int32), axis=2)
    row = ids * ROWS + slot * 2 + jnp.arange(2, dtype=jnp.int32)[:, None]
    target = row.reshape(TOK, 2).T
    weight_col = route_weights.reshape(TOK, 2)
    gate = jnp.where((sample_flags == 1)[:, None], cond_gate[1][None, :], cond_gate[0][None, :])

    rows = exchange(pack(queries, keys, values), SEQ)
    weight_other = lax.ppermute(out_weight, "core", swap)

    grad_chunks = send_grads(cotangent.reshape(TOK, D), gate, target, weight_col.T)
    rows, grad_chunks = lax.optimization_barrier((rows, grad_chunks))
    grad_arrived = exchange(grad_chunks, ALL)

    heads = attend(rows).reshape(16, 256, HEAD)
    heads, grad_arrived = lax.optimization_barrier((heads, grad_arrived))
    heads = exchange(heads, BACK).reshape(2, 4, 2, 4, 64, HEAD)
    *grads, back = grads_in(grad_arrived, down_weight[0])
    heads, back = lax.optimization_barrier((heads, back))
    far_0, far_1, far_2 = [lax.ppermute(g, "dp", swap) for g in grads]
    fa, fb = project(place, (2,), (2,), heads, out_weight, weight_other)
    fa = lax.ppermute(fa, "z", above)
    fb = lax.ppermute(fb, "z", below)
    heads, far_0 = lax.optimization_barrier((heads, far_0))
    ua, ub, da, db, own = project(place, (1, 3, 0), (2, 2, 1), heads, out_weight, weight_other)
    ub = lax.ppermute(ub, "z", above)
    da = lax.ppermute(da, "z", below)
    ua = lax.ppermute(plus(ua, fa), "z", above)
    db = lax.ppermute(plus(db, fb), "z", below)
    own, ua, far_1 = lax.optimization_barrier((own, ua, far_1))
    stream, chunks = norm_send(
        own, ua, ub, da, db, residual.reshape(TOK, D), norm_gain[None], target
    )
    arrived = exchange(chunks, ALL)

    own_rows, hidden, hid_other, hid_own, pre_other, pre_own = hidden_units(
        place, arrived, up_weight[0], back
    )
    hid_far = lax.ppermute(hid_other, "dp", swap)
    products = expert_out(hidden, down_weight[0])
    products, far_2, hid_far = lax.optimization_barrier((products, far_2, hid_far))
    returned = exchange(products, ALL)
    up_other = up_half(own_rows, pre_other)
    up_far = lax.ppermute(up_other, "dp", swap)
    block_out = combine(returned, stream, gate, target, weight_col)
    up_own = up_half(own_rows, pre_own)
    down_total = down_sum(hid_own, grads, hid_far, (far_0, far_1, far_2))
    up_total = plus(up_own, up_far)
    return (block_out.reshape(2, TOK // 2, D), up_total[None], down_total[None])


def solution(mesh):
    fine = Mesh(mesh.devices.reshape(2, 4, 2, 4, 2), ("dp", "x", "yl", "z", "core"))
    expert = ("z", "core")
    tokens = P("dp", ALL, None)
    placed = (
        P("dp", SEQ, expert),
        P("dp", SEQ, expert),
        P("dp", SEQ, expert),
        tokens,
        P(expert, None),
        P(),
        tokens,
        tokens,
        P("dp"),
        P(),
        P(ALL, None, None),
        P(ALL, None, None),
        tokens,
    )
    return jax.shard_map(
        body,
        mesh=fine,
        in_specs=placed,
        out_specs=(tokens, P(ALL, None, "dp"), P(ALL, "dp", None)),
        check_vma=False,
    )
```

```python
import functools

import jax
import jax.numpy as jnp
from jax import lax
from jax.experimental import pallas as pl
from jax.experimental.pallas import tpu as pltpu
from jax.sharding import Mesh
from jax.sharding import PartitionSpec as P

BF = jnp.bfloat16
F32 = jnp.float32
D = 4096
FF = 512
HEAD = 128
LENGTH = 4096
HALF = FF // 2
EXPERTS = 64
ROWS = 6
TOK = 128
SLOTS = EXPERTS * ROWS
CB = 4
CW = D // CB
GROUP = 8
GR = GROUP * ROWS
GRAD_WIDTHS = (CW, 2 * CW, CW)
GRAD_CUTS = ((0, slice(0, CW)), (1, slice(0, CW)), (1, slice(CW, 2 * CW)), (2, slice(0, CW)))
EXP_SCALE = HEAD**-0.5 * 1.4426950408889634
QB = 256
KB = 512
SEQ = ("x", "yl")
BACK = ("x", "yl", "core")
ALL = ("x", "yl", "z", "core")
VMEM_LIMIT = 24 * 1024 * 1024


def params(limit=VMEM_LIMIT):
    return pltpu.CompilerParams(vmem_limit_bytes=limit)


def cost(multiply_adds, transcendentals=0, size=1 << 20):
    return pl.CostEstimate(
        flops=2 * multiply_adds, bytes_accessed=size, transcendentals=transcendentals
    )


def whole(*shape):
    return pl.BlockSpec(shape, lambda *_: (0,) * len(shape))


def resident(count):
    return [pl.BlockSpec(memory_space=pltpu.VMEM)] * count


def scalars():
    return pl.BlockSpec(memory_space=pltpu.SMEM)


def array(*shape, dtype=BF):
    return jax.ShapeDtypeStruct(shape, dtype)


def dot_nt(a, b):
    return lax.dot_general(a, b, (((1,), (1,)), ((), ())), preferred_element_type=F32)


def dot_tn(a, b):
    return lax.dot_general(a, b, (((0,), (0,)), ((), ())), preferred_element_type=F32)


def dot_nn(a, b):
    return jnp.dot(a, b, preferred_element_type=F32)


def pack(queries, keys, values):
    def kernel(q_ref, k_ref, v_ref, o_ref):
        for part, ref in enumerate((q_ref, k_ref, v_ref)):
            for h in range(4):
                o_ref[h, part] = ref[0, :, h * HEAD : (h + 1) * HEAD]

    spec = pl.BlockSpec((1, 256, 4 * HEAD), lambda b, t: (b, t, 0))
    return pl.pallas_call(
        kernel,
        grid=(2, 2),
        in_specs=[spec] * 3,
        out_specs=pl.BlockSpec((4, 3, 256, HEAD), lambda b, t: (b, 0, t, 0)),
        out_shape=jax.ShapeDtypeStruct((8, 3, 512, HEAD), BF),
        compiler_params=params(56 * 1024 * 1024),
        name="pack_heads",
    )(queries, keys, values)


def lane_tiles(value):
    return [value[:, j : j + 128] for j in range(0, value.shape[1], 128)]


def attend(rows):
    pieces = [slice(i, i + KB) for i in range(0, LENGTH, KB)]

    def scores_of(q, k, s_ref):
        top = None
        for cut in pieces:
            s = dot_nt(q, k[cut])
            s_ref[:, cut] = s
            high = functools.reduce(jnp.maximum, lane_tiles(s))
            top = high if top is None else jnp.maximum(top, high)
        return jnp.max(top, axis=-1, keepdims=True)

    def step(q_next, k, s_next, s_now, top_now, v):
        top = None
        out = None
        for cut in pieces:
            s = dot_nt(q_next, k[cut])
            p = jnp.exp2((s_now[:, cut] - top_now) * EXP_SCALE).astype(BF)
            s_next[:, cut] = s
            high = functools.reduce(jnp.maximum, lane_tiles(s))
            top = high if top is None else jnp.maximum(top, high)
            wide = jnp.concatenate([v[cut], jnp.ones((KB, HEAD), BF)], axis=1)
            part = dot_nn(p, wide)
            out = part if out is None else out + part
        return jnp.max(top, axis=-1, keepdims=True), out[:, :HEAD] / out[:, HEAD:]

    def kernel(q_ref, qn_ref, k_ref, v_ref, o_ref, sa_ref, sb_ref, top_ref):
        k = k_ref[:, 0].reshape(LENGTH, HEAD)
        v = v_ref[:, 0].reshape(LENGTH, HEAD)

        @pl.when(pl.program_id(0) == 0)
        def _():
            top_ref[...] = jnp.broadcast_to(scores_of(q_ref[0, 0, :QB], k, sa_ref), (QB, 128))

        top_a = top_ref[:, :1]
        top_b, out_a = step(q_ref[0, 0, QB:], k, sb_ref, sa_ref, top_a, v)
        top_n, out_b = step(qn_ref[0, 0], k, sa_ref, sb_ref, top_b, v)
        top_ref[...] = jnp.broadcast_to(top_n, (QB, 128))
        for base, out in ((0, out_a), (4, out_b)):
            for t in range(QB // 64):
                j = base + t
                o_ref[0, j % 2, j // 2] = out[64 * t : 64 * t + 64].astype(BF)

    def following(i):
        j = jnp.minimum(2 * i + 2, LENGTH // QB - 1)
        return (j // 2, 0, j % 2, 0)

    return pl.pallas_call(
        kernel,
        grid=(8,),
        in_specs=[
            pl.BlockSpec((1, 1, 512, HEAD), lambda i: (i, 0, 0, 0)),
            pl.BlockSpec((1, 1, QB, HEAD), following),
            pl.BlockSpec((8, 1, 512, HEAD), lambda i: (0, 1, 0, 0)),
            pl.BlockSpec((8, 1, 512, HEAD), lambda i: (0, 2, 0, 0)),
        ],
        out_specs=pl.BlockSpec((1, 2, 4, 64, HEAD), lambda i: (i, 0, 0, 0, 0)),
        out_shape=jax.ShapeDtypeStruct((8, 2, 4, 64, HEAD), BF),
        scratch_shapes=[
            pltpu.VMEM((QB, LENGTH), F32),
            pltpu.VMEM((QB, LENGTH), F32),
            pltpu.VMEM((QB, 128), F32),
        ],
        compiler_params=params(),
        cost_estimate=pl.CostEstimate(
            flops=4 * LENGTH * LENGTH * 256, bytes_accessed=4 << 20, transcendentals=LENGTH * LENGTH
        ),
        name="attend",
    )(rows, rows, rows, rows)


def project(place, offsets, splits, heads, weight_own, weight_other):
    width = 512
    rows = len(offsets) * TOK
    shapes = [array(TOK, D // n) for n in splits for _ in range(n)]

    def kernel(place_ref, a_ref, wo_ref, ws_ref, *refs):
        lhs = refs[-1]
        core = place_ref[1]
        for side, c in enumerate((core, 1 - core)):
            for number, offset in enumerate(offsets):
                z = lax.rem(place_ref[0] + offset, 4)
                for b in range(2):
                    for h in range(4):
                        lhs[
                            number * TOK + b * 64 : number * TOK + (b + 1) * 64,
                            side * FF + h * HEAD : side * FF + (h + 1) * HEAD,
                        ] = a_ref[b, h, c, z]

        for half in range(2):

            @pl.loop(0, D // 2 // width)
            def _(n, half=half):
                near = pl.ds(pl.multiple_of(n * width, width), width)
                cut = pl.ds(pl.multiple_of(half * (D // 2) + n * width, width), width)
                total = dot_nn(lhs[:, :FF], wo_ref[:, cut]) + dot_nn(lhs[:, FF:], ws_ref[:, cut])
                first = 0
                for number, pieces in enumerate(splits):
                    part = total[number * TOK : (number + 1) * TOK].astype(BF)
                    if pieces == 2:
                        refs[first + half][:, near] = part
                    else:
                        refs[first][:, cut] = part
                    first += pieces

    return pl.pallas_call(
        kernel,
        in_specs=[scalars()] + resident(3),
        out_specs=resident(len(shapes)),
        scratch_shapes=[pltpu.VMEM((rows, 2 * FF), BF)],
        out_shape=shapes,
        compiler_params=params(),
        cost_estimate=cost(rows * 1024 * D),
        name="project",
    )(place, heads, weight_own, weight_other)


def source_of(d):
    return lax.rem(d, CB * ROWS) // ROWS * GR + d // (CB * ROWS) * ROWS + lax.rem(d, ROWS)


def mixer():
    n = CB * GR
    d = lax.broadcasted_iota(jnp.int32, (n, n), 0)
    s = lax.broadcasted_iota(jnp.int32, (n, n), 1)
    return (s == source_of(d)).astype(BF)


def unmixer():
    n = CB * GR
    s = lax.broadcasted_iota(jnp.int32, (n, n), 0)
    d = lax.broadcasted_iota(jnp.int32, (n, n), 1)
    return (s == source_of(d)).astype(BF)


def mix_out(sc_ref, o_ref):
    mat = mixer()
    for g in range(EXPERTS // GROUP):
        stack = jnp.concatenate([sc_ref[c, g * GR : (g + 1) * GR, :] for c in range(CB)], axis=0)
        o_ref[g * CB * GR : (g + 1) * CB * GR, :] = dot_nn(mat, stack).astype(BF)


def mix_in(i_ref, sc_ref):
    mat = unmixer()
    for g in range(EXPERTS // GROUP):
        stack = dot_nn(mat, i_ref[g * CB * GR : (g + 1) * CB * GR, :]).astype(BF)
        for c in range(CB):
            sc_ref[c, g * GR : (g + 1) * GR, :] = stack[c * GR : (c + 1) * GR]


def placing(tgt_ref, k):
    slot = lax.broadcasted_iota(jnp.int32, (SLOTS, TOK), 0)
    return slot == tgt_ref[k : k + 1, :]


def send_grads(cotangent, gate, target, weight):
    def kernel(cot_ref, gate_ref, tgt_ref, w_ref, o_ref, sc_ref):
        first, second = placing(tgt_ref, 0), placing(tgt_ref, 1)
        both = (first | second).astype(BF)
        w = jnp.sum(
            jnp.where(first, w_ref[0:1, :], 0.0) + jnp.where(second, w_ref[1:2, :], 0.0),
            axis=1,
            keepdims=True,
        )
        odd = lax.rem(lax.broadcasted_iota(jnp.int32, (SLOTS, 1), 0), 2) == 1
        for c in range(CB):
            cut = slice(c * CW, (c + 1) * CW)
            rows = dot_nn(both, cot_ref[:, cut])
            gates = jnp.where(odd, gate_ref[1:2, cut], gate_ref[0:1, cut])
            sc_ref[c] = (w * gates * rows).astype(BF)
        mix_out(sc_ref, o_ref)

    return pl.pallas_call(
        kernel,
        in_specs=resident(4),
        out_specs=resident(1)[0],
        out_shape=jax.ShapeDtypeStruct((CB * SLOTS, CW), BF),
        scratch_shapes=[pltpu.VMEM((CB, SLOTS, CW), BF)],
        compiler_params=params(),
        name="send_grads",
    )(cotangent, gate, target, weight)


def norm_send(own, up_a, up_b, down_a, down_b, residual, gain, target):
    def kernel(own_ref, ua, ub, da, db, res_ref, gain_ref, tgt_ref, s_ref, o_ref, sc_ref):
        square = jnp.zeros((TOK, 1), F32)
        for half, first, second in ((0, ua, da), (1, ub, db)):
            cut = slice(half * D // 2, (half + 1) * D // 2)
            s = own_ref[:, cut].astype(F32) + first[...].astype(F32) + second[...].astype(F32)
            s = res_ref[:, cut].astype(F32) + s
            s_ref[:, cut] = s
            square += jnp.sum(s * s, axis=1, keepdims=True)
        factor = lax.rsqrt(square * (1.0 / D) + 1e-06)
        both = (placing(tgt_ref, 0) | placing(tgt_ref, 1)).astype(BF)
        for c in range(CB):
            cut = slice(c * CW, (c + 1) * CW)
            normed = (s_ref[:, cut] * factor * gain_ref[:, cut]).astype(BF)
            sc_ref[c] = dot_nn(both, normed).astype(BF)
        mix_out(sc_ref, o_ref)

    return pl.pallas_call(
        kernel,
        in_specs=resident(8),
        out_specs=resident(2),
        out_shape=[
            jax.ShapeDtypeStruct((TOK, D), F32),
            jax.ShapeDtypeStruct((CB * SLOTS, CW), BF),
        ],
        scratch_shapes=[pltpu.VMEM((CB, SLOTS, CW), BF)],
        compiler_params=params(),
        name="norm_send",
    )(own, up_a, up_b, down_a, down_b, residual, gain, target)


def grads_in(chunks, down):
    def kernel(i_ref, d_ref, *refs):
        b_ref, sc_ref = refs[-2:]
        mix_in(i_ref, sc_ref)
        back = None
        for c in range(CB):
            number, cut = GRAD_CUTS[c]
            refs[number][:, cut] = sc_ref[c]
            part = dot_nt(sc_ref[c], d_ref[:, c * CW : (c + 1) * CW])
            back = part if back is None else back + part
        b_ref[...] = back

    return pl.pallas_call(
        kernel,
        in_specs=resident(2),
        out_specs=resident(4),
        out_shape=[jax.ShapeDtypeStruct((SLOTS, w), BF) for w in GRAD_WIDTHS]
        + [jax.ShapeDtypeStruct((SLOTS, FF), F32)],
        scratch_shapes=[pltpu.VMEM((CB, SLOTS, CW), BF)],
        compiler_params=params(),
        name="grads_in",
    )(chunks, down)


def gelu_pair(pre):
    cdf_part = 0.5 * (1.0 + lax.erf(pre * 0.7071067811865476))
    density = jnp.exp(-0.5 * pre * pre) * 0.3989422804014327
    return (pre * cdf_part, cdf_part + pre * density)


def hidden_units(place, chunks, up, back):
    def kernel(place_ref, i_ref, up_ref, b_ref, x_ref, hid_ref, ho_ref, hs_ref, po_ref, ps_ref):
        mix_in(i_ref, x_ref)
        pre = None
        for c in range(CB):
            part = dot_nn(x_ref[c], up_ref[c * CW : (c + 1) * CW, :])
            pre = part if pre is None else pre + part
        act, slope = gelu_pair(pre)
        hidden, grad = act.astype(BF), (b_ref[...] * slope).astype(BF)
        hid_ref[...] = hidden
        mine = place_ref[2] == 0
        for value, other, own in ((hidden, ho_ref, hs_ref), (grad, po_ref, ps_ref)):
            low, high = value[:, :HALF], value[:, HALF:]
            own[...] = jnp.where(mine, low, high)
            other[...] = jnp.where(mine, high, low)

    return pl.pallas_call(
        kernel,
        in_specs=[scalars()] + resident(3),
        out_specs=resident(6),
        out_shape=[array(CB, SLOTS, CW), array(SLOTS, FF)] + [array(SLOTS, HALF)] * 4,
        compiler_params=params(),
        name="hidden_units",
    )(place, chunks, up, back)


def expert_out(hidden, down):
    def kernel(h_ref, down_ref, o_ref, prod):
        for c in range(CB):
            prod[c] = dot_nn(h_ref[...], down_ref[:, c * CW : (c + 1) * CW]).astype(BF)
        mix_out(prod, o_ref)

    return pl.pallas_call(
        kernel,
        in_specs=resident(2),
        out_specs=resident(1)[0],
        out_shape=array(CB * SLOTS, CW),
        scratch_shapes=[pltpu.VMEM((CB, SLOTS, CW), BF)],
        compiler_params=params(),
        name="expert_out",
    )(hidden, down)


def up_half(rows, pre_grad):
    def kernel(x_ref, p_ref, o_ref):
        for c in range(CB):
            o_ref[c * CW : (c + 1) * CW, :] = dot_tn(x_ref[c], p_ref[...]).astype(BF)

    return pl.pallas_call(
        kernel,
        in_specs=resident(2),
        out_specs=resident(1)[0],
        out_shape=array(D, HALF),
        compiler_params=params(),
        cost_estimate=cost(SLOTS * D * HALF, size=6 << 20),
        name="up_half",
    )(rows, pre_grad)


def up_sum(rows, pre_grad, far):
    def kernel(x_ref, p_ref, f_ref, o_ref):
        for c in range(CB):
            cut = slice(c * CW, (c + 1) * CW)
            o_ref[cut, :] = (dot_tn(x_ref[c], p_ref[...]) + f_ref[cut, :].astype(F32)).astype(BF)

    return pl.pallas_call(
        kernel,
        in_specs=resident(3),
        out_specs=resident(1)[0],
        out_shape=array(D, HALF),
        compiler_params=params(),
        cost_estimate=cost(SLOTS * D * HALF, size=6 << 20),
        name="up_sum",
    )(rows, pre_grad, far)


def down_sum(hidden, grads, hidden_far, grads_far):
    def kernel(h_ref, hf_ref, *refs):
        o_ref = refs[-1]
        for c in range(CB):
            number, cut = GRAD_CUTS[c]
            near, far = refs[number], refs[3 + number]
            total = dot_tn(h_ref[...], near[:, cut]) + dot_tn(hf_ref[...], far[:, cut])
            o_ref[:, c * CW : (c + 1) * CW] = total.astype(BF)

    return pl.pallas_call(
        kernel,
        in_specs=resident(8),
        out_specs=resident(1)[0],
        out_shape=array(HALF, D),
        compiler_params=params(),
        cost_estimate=cost(2 * SLOTS * D * HALF, size=9 << 20),
        name="down_sum",
    )(hidden, hidden_far, *grads, *grads_far)


def combine(chunks, stream, gate, target, weight):
    def kernel(i_ref, s_ref, gate_ref, tgt_ref, w_ref, o_ref, sc_ref):
        mix_in(i_ref, sc_ref)
        first, second = placing(tgt_ref, 0).astype(BF), placing(tgt_ref, 1).astype(BF)
        late = lax.broadcasted_iota(jnp.int32, (TOK, 1), 0) >= TOK // 2
        for c in range(CB):
            cut = slice(c * CW, (c + 1) * CW)
            mix = w_ref[:, 0:1] * dot_tn(first, sc_ref[c]) + w_ref[:, 1:2] * dot_tn(second, sc_ref[c])
            gates = jnp.where(late, gate_ref[1:2, cut], gate_ref[0:1, cut])
            o_ref[:, cut] = (s_ref[:, cut] + gates * mix).astype(BF)

    return pl.pallas_call(
        kernel,
        in_specs=resident(5),
        out_specs=resident(1)[0],
        out_shape=jax.ShapeDtypeStruct((TOK, D), BF),
        scratch_shapes=[pltpu.VMEM((CB, SLOTS, CW), BF)],
        compiler_params=params(),
        name="combine",
    )(chunks, stream, gate, target, weight)


def plus(a, b):
    return (a.astype(F32) + b.astype(F32)).astype(BF)


def body(
    queries,
    keys,
    values,
    residual,
    out_weight,
    norm_gain,
    routes,
    route_weights,
    sample_flags,
    cond_gate,
    up_weight,
    down_weight,
    cotangent,
):
    z, core, dp = lax.axis_index("z"), lax.axis_index("core"), lax.axis_index("dp")
    place = jnp.stack([z, core, dp]).astype(jnp.int32)
    swap = [(0, 1), (1, 0)]
    above = [(i, (i + 1) % 4) for i in range(4)]
    below = [(i, (i + 3) % 4) for i in range(4)]
    exchange = functools.partial(lax.all_to_all, split_axis=0, concat_axis=0, tiled=True)

    ids = routes.reshape(2, TOK)
    earlier = jnp.arange(TOK)[:, None] > jnp.arange(TOK)[None, :]
    same = (ids[:, :, None] == ids[:, None, :]) & earlier[None]
    slot = jnp.sum(same.astype(jnp.int32), axis=2)
    row = ids * ROWS + slot * 2 + jnp.arange(2, dtype=jnp.int32)[:, None]
    target = row.reshape(TOK, 2).T
    weight_col = route_weights.reshape(TOK, 2)
    gate = jnp.where((sample_flags == 1)[:, None], cond_gate[1][None, :], cond_gate[0][None, :])

    rows = exchange(pack(queries, keys, values), SEQ)
    weight_other = lax.ppermute(out_weight, "core", swap)

    grad_chunks = send_grads(cotangent.reshape(TOK, D), gate, target, weight_col.T)
    rows, grad_chunks = lax.optimization_barrier((rows, grad_chunks))
    grad_arrived = exchange(grad_chunks, ALL)

    heads = attend(rows).reshape(16, 256, HEAD)
    heads, grad_arrived = lax.optimization_barrier((heads, grad_arrived))
    heads = exchange(heads, BACK).reshape(2, 4, 2, 4, 64, HEAD)
    *grads, back = grads_in(grad_arrived, down_weight[0])
    heads, back = lax.optimization_barrier((heads, back))
    far_0, far_1, far_2 = [lax.ppermute(g, "dp", swap) for g in grads]
    fa, fb = project(place, (2,), (2,), heads, out_weight, weight_other)
    fa = lax.ppermute(fa, "z", above)
    fb = lax.ppermute(fb, "z", below)
    ua, ub, da, db, own = project(place, (1, 3, 0), (2, 2, 1), heads, out_weight, weight_other)
    ub = lax.ppermute(ub, "z", above)
    da = lax.ppermute(da, "z", below)
    fa, far_0 = lax.optimization_barrier((fa, far_0))
    ua = lax.ppermute(plus(ua, fa), "z", above)
    db = lax.ppermute(plus(db, fb), "z", below)
    own, ua, far_1 = lax.optimization_barrier((own, ua, far_1))
    stream, chunks = norm_send(
        own, ua, ub, da, db, residual.reshape(TOK, D), norm_gain[None], target
    )
    arrived = exchange(chunks, ALL)

    own_rows, hidden, hid_other, hid_own, pre_other, pre_own = hidden_units(
        place, arrived, up_weight[0], back
    )
    hid_far = lax.ppermute(hid_other, "dp", swap)
    products = expert_out(hidden, down_weight[0])
    products, far_2, hid_far = lax.optimization_barrier((products, far_2, hid_far))
    returned = exchange(products, ALL)
    up_other = up_half(own_rows, pre_other)
    up_far = lax.ppermute(up_other, "dp", swap)
    block_out = combine(returned, stream, gate, target, weight_col)
    up_own = up_half(own_rows, pre_own)
    down_total = down_sum(hid_own, grads, hid_far, (far_0, far_1, far_2))
    up_total = plus(up_own, up_far)
    return (block_out.reshape(2, TOK // 2, D), up_total[None], down_total[None])


def solution(mesh):
    fine = Mesh(mesh.devices.reshape(2, 4, 2, 4, 2), ("dp", "x", "yl", "z", "core"))
    expert = ("z", "core")
    tokens = P("dp", ALL, None)
    placed = (
        P("dp", SEQ, expert),
        P("dp", SEQ, expert),
        P("dp", SEQ, expert),
        tokens,
        P(expert, None),
        P(),
        tokens,
        tokens,
        P("dp"),
        P(),
        P(ALL, None, None),
        P(ALL, None, None),
        tokens,
    )
    return jax.shard_map(
        body,
        mesh=fine,
        in_specs=placed,
        out_specs=(tokens, P(ALL, None, "dp"), P(ALL, "dp", None)),
        check_vma=False,
    )
```
